128 devices in a mesh: blk: 16 (over z_hi, y, core), head: 8 (over z_lo, x).
Axes of the slice: x: 4, y: 4, z: 4 (z_hi: 2, z_lo: 2; z = z_hi * 2 + z_lo), core: 2. Of those that a mesh axis runs over, the one named last changes fastest.
Arguments:
- tokens: bfloat16 [16384, 1024], P(('blk', 'head')), may hold values from -6 to 6
- doc_starts: int32 [4], replicated, may hold values from 0 to 16383, as said below
- first_gain: bfloat16 [1024], replicated, may hold values from 0.5 to 1.5
- query_weight: bfloat16 [1024, 2048], P('blk', 'head'), may hold values from -0.1875 to 0.1875
- key_matrix: bfloat16 [1024, 1024], P('blk', 'head'), may hold values from -0.1875 to 0.1875
- value_matrix: bfloat16 [1024, 1024], P('blk', 'head'), may hold values from -0.1875 to 0.1875
- querynorm: bfloat16 [128], replicated, may hold values from 1 to 2
- keynorm: bfloat16 [128], replicated, may hold values from 1 to 2
- output_weight: bfloat16 [2048, 1024], P('head', 'blk'), may hold values from -0.75 to 0.75
- second_gain: bfloat16 [1024], replicated, may hold values from 0.5 to 1.5
- gate_weight: bfloat16 [1024, 3072], P('blk', 'head'), may hold values from -0.1875 to 0.1875
- up_weight: bfloat16 [1024, 3072], P('blk', 'head'), may hold values from -0.1875 to 0.1875
- down_weight: bfloat16 [3072, 1024], P('head', 'blk'), may hold values from -0.109375 to 0.109375
- grad_out: bfloat16 [16384, 1024], P(('blk', 'head')), may hold values from -24 to 24
Outputs:
- layer_out: bfloat16 [16384, 1024], P(('blk', 'head'))
- tokens_grad: bfloat16 [16384, 1024], P(('blk', 'head'))
- first_grad: float32 [1024], P(('blk', 'head'))
- query_grad: float32 [1024, 2048], P('blk', 'head')
- key_grad: float32 [1024, 1024], P('blk', 'head')
- value_grad: float32 [1024, 1024], P('blk', 'head')
- querynorm_grad: float32 [128], P(('blk', 'head'))
- keynorm_grad: float32 [128], P(('blk', 'head'))
- output_grad: float32 [2048, 1024], P('head', 'blk')
- second_grad: float32 [1024], P(('blk', 'head'))
- gate_grad: float32 [1024, 3072], P('blk', 'head')
- up_grad: float32 [1024, 3072], P('blk', 'head')
- down_grad: float32 [3072, 1024], P('head', 'blk')
The draws below stay inside these ranges and needn't reach their ends.
Inputs may be any that keep to these rules, and one draw needn't show every extreme that they name: `doc_starts`: strictly increasing; the first entry is 0; the second is below 1024 and the third above 15360.
All inputs are finite; a program needn't handle non-finite values.
Results may differ from the reference program's by a relative error of at most 0.035.
Values may be sent and summed in bfloat16 or wider, within the bound.
A program may use at most 128 MiB of HBM per device.

```python
import jax
import jax.numpy as jnp
from jax import lax

MODEL_WIDTH = 1024
FF = 3072
QUERY_HEADS = 16
KEY_VALUE_HEADS = 8
HEAD_SIZE = 128
STREAM_TOKENS = 16384
BLOCK_ROWS = 1024


def draw_doc_starts(key, part):
    key = jax.random.fold_in(key, 7)
    keys = jax.random.split(key, 3)
    second = jax.random.randint(keys[0], (), 1, BLOCK_ROWS, dtype=jnp.int32)
    third = jax.random.randint(keys[1], (), STREAM_TOKENS - BLOCK_ROWS + 1, STREAM_TOKENS - 1, dtype=jnp.int32)
    fourth = jax.random.randint(keys[2], (), third + 1, STREAM_TOKENS, dtype=jnp.int32)
    return jnp.stack([jnp.zeros((), jnp.int32), second, third, fourth]).astype(jnp.int32)


def spiked(entries, key, source, target, blocks, factor):
    def block_of(dim):
        return (jnp.arange(entries.shape[dim]) // (entries.shape[dim] // blocks)).reshape((-1,) + (1,) * (entries.ndim - 1 - dim))

    one_side = jax.random.permutation(key, blocks)[block_of(target)]
    second = (block_of(target) + blocks // 2) % blocks
    return jnp.where((block_of(source) == one_side) | (block_of(source) == second), factor * entries, entries)


def levels(rng, shape, shards, smallest, largest):
    level = 1.0
    for axis_at, blocks in shards:
        heights = jax.random.uniform(jax.random.fold_in(jax.random.fold_in(rng, 6), axis_at), (blocks,), jnp.float32, smallest / len(shards), largest / len(shards))
        level = level * jnp.repeat(jnp.exp(heights), shape[axis_at] // blocks).reshape((-1,) + (1,) * (len(shape) - 1 - axis_at))
    return level


def scatter_about(key, shape, width, reach, pieces=(), held_as=jnp.bfloat16):
    values = jax.random.normal(key, shape, jnp.float32) * width
    if len(pieces) > 0:
        values = levels(key, shape, pieces, -0.22, 0.18) * values
    return jnp.clip(values, min=-reach, max=reach).astype(held_as)


def bell_draw_with(own_key, extent, width, limit, cuts, heavy, held_as=jnp.bfloat16):
    entries = width * jax.random.normal(own_key, extent, jnp.float32)
    if cuts:
        entries = entries * levels(own_key, extent, cuts, -0.22, 0.18)
    return jnp.clip(spiked(entries, jax.random.fold_in(own_key, 3), *heavy), -limit, limit).astype(held_as)


def setup_inputs(seed: int = 0) -> dict:
    key_list = jax.random.split(jax.random.key(seed), 15)
    tokens = scatter_about(key_list[0], (STREAM_TOKENS, MODEL_WIDTH), 1.0, 6.0, ((0, 128),))
    doc_starts = draw_doc_starts(jax.random.fold_in(key_list[14], 71), 0)
    first_gain = jnp.clip(1.0 + 0.1 * jax.random.normal(key_list[2], (MODEL_WIDTH,), jnp.float32), 0.5, 1.5).astype(jnp.bfloat16)
    query_weight = scatter_about(key_list[3], (MODEL_WIDTH, QUERY_HEADS * HEAD_SIZE), MODEL_WIDTH ** -0.5, 0.1875, ((0, 16), (1, 8)))
    key_matrix = scatter_about(key_list[4], (MODEL_WIDTH, KEY_VALUE_HEADS * HEAD_SIZE), MODEL_WIDTH ** -0.5, 0.1875, ((0, 16), (1, 8)))
    value_matrix = scatter_about(key_list[5], (MODEL_WIDTH, KEY_VALUE_HEADS * HEAD_SIZE), MODEL_WIDTH ** -0.5, 0.1875, ((0, 16), (1, 8)))
    querynorm = jnp.clip(jax.random.uniform(key_list[6], (HEAD_SIZE,), jnp.float32, 1.0, 2.0), 1.0, 2.0).astype(jnp.bfloat16)
    keynorm = jnp.clip(jax.random.uniform(key_list[7], (HEAD_SIZE,), jnp.float32, 1.0, 2.0), 1.0, 2.0).astype(jnp.bfloat16)
    output_weight = scatter_about(key_list[8], (QUERY_HEADS * HEAD_SIZE, MODEL_WIDTH), (QUERY_HEADS * HEAD_SIZE // 32) ** -0.5, 0.75, ((0, 8), (1, 16)))
    second_gain = jnp.clip(1.0 + 0.1 * jax.random.normal(key_list[9], (MODEL_WIDTH,), jnp.float32), 0.5, 1.5).astype(jnp.bfloat16)
    gate_weight = scatter_about(key_list[10], (MODEL_WIDTH, FF), MODEL_WIDTH ** -0.5, 0.1875, ((0, 16), (1, 8)))
    up_weight = scatter_about(key_list[11], (MODEL_WIDTH, FF), MODEL_WIDTH ** -0.5, 0.1875, ((0, 16), (1, 8)))
    down_weight = scatter_about(key_list[12], (FF, MODEL_WIDTH), FF ** -0.5, 0.109375, ((0, 8), (1, 16)))
    grad_out = bell_draw_with(key_list[13], (STREAM_TOKENS, MODEL_WIDTH), 1.0, 24.0, ((0, 128),), (0, 1, 128, 5.5))
    return dict(tokens=tokens, doc_starts=doc_starts, first_gain=first_gain, query_weight=query_weight, key_matrix=key_matrix, value_matrix=value_matrix, querynorm=querynorm, keynorm=keynorm, output_weight=output_weight, second_gain=second_gain, gate_weight=gate_weight, up_weight=up_weight, down_weight=down_weight, grad_out=grad_out)


EPS = 1e-06
THETA = 1000000.0
NEGATIVE = -1e+30

@jax.custom_vjp
def low(v):
    return lax.optimization_barrier(v.astype(jnp.bfloat16)).astype(jnp.float32)

@jax.custom_vjp
def low_back(v):
    return v

def low_keep(v):
    return (low(v), None)

def low_pass(kept, grad):
    return (grad,)

def back_keep(v):
    return (v, None)

def back_low(kept, grad):
    return (low(grad),)
low.defvjp(low_keep, low_pass)
low_back.defvjp(back_keep, back_low)

def rms_scale(values, gain):
    return values * lax.rsqrt(lax.optimization_barrier(jnp.mean(values * values, axis=-1, keepdims=True)) + EPS) * gain

def rotary(values, position):
    half = values.shape[-1] // 2
    freqs = THETA ** (-(jnp.arange(half, dtype=jnp.float32) * 2.0 / values.shape[-1]))
    angle = position.astype(jnp.float32)[:, None] * freqs[None, :]
    cosine = jnp.cos(angle)[:, None, :]
    sine = jnp.sin(angle)[:, None, :]
    first = values[..., :half]
    second = values[..., half:]
    return jnp.concatenate([first * cosine - second * sine, second * cosine + first * sine], axis=-1)

def doc_info(index, starts):
    below = starts[None, :] <= index[:, None]
    number = lax.optimization_barrier(jnp.sum(below.astype(jnp.int32), axis=1)) - 1
    begin = lax.optimization_barrier(jnp.max(jnp.where(below, starts[None, :], 0), axis=1))
    return (number, index - begin)

def matrix_product(left, right):
    return jnp.dot(left, right, precision=lax.Precision.HIGHEST, preferred_element_type=jnp.float32)

def attend(query_rows, keys, values, index, docs):
    head_group = QUERY_HEADS // KEY_VALUE_HEADS
    row_count = min(256, STREAM_TOKENS)
    token_count = STREAM_TOKENS // row_count
    scale = HEAD_SIZE ** (-0.5)
    query_block_list = query_rows.reshape(token_count, row_count, KEY_VALUE_HEADS, head_group, HEAD_SIZE)
    iblocks = index.reshape(token_count, row_count)
    dblocks = docs.reshape(token_count, row_count)

    def one_block(item):
        qblock, qindex, qdoc = item
        raw = low_back(jnp.einsum('qkgd,pkd->kgqp', qblock, keys, precision=lax.Precision.HIGHEST))
        allowed = (index[None, :] <= qindex[:, None]) & (docs[None, :] == qdoc[:, None])
        logits = jnp.where(allowed, raw * scale, NEGATIVE)
        probs = jax.nn.softmax(logits, axis=-1)
        return jnp.einsum('kgqp,pkd->qkgd', low(probs), values, precision=lax.Precision.HIGHEST)
    result = lax.map(jax.checkpoint(one_block), (query_block_list, iblocks, dblocks))
    return result.reshape(STREAM_TOKENS, QUERY_HEADS * HEAD_SIZE)

def reference(tokens, doc_starts, first_gain, query_weight, key_matrix, value_matrix, querynorm, keynorm, output_weight, second_gain, gate_weight, up_weight, down_weight, grad_out):
    index = jnp.arange(STREAM_TOKENS, dtype=jnp.int32)
    docs, position = doc_info(index, doc_starts)

    def layer(inputs, gain_one, wquery, key_param, value_param, qgain, kgain, woutput, gain_two, wgate, wupper, wdown):
        first_hidden = low(rms_scale(inputs, gain_one))
        qproj = low_back(matrix_product(first_hidden, wquery)).reshape(STREAM_TOKENS, QUERY_HEADS, HEAD_SIZE)
        key_projected = low_back(matrix_product(first_hidden, key_param)).reshape(STREAM_TOKENS, KEY_VALUE_HEADS, HEAD_SIZE)
        value_projected = matrix_product(first_hidden, value_param).reshape(STREAM_TOKENS, KEY_VALUE_HEADS, HEAD_SIZE)
        query_rows = low(rotary(rms_scale(qproj, qgain), position))
        keys = low(rotary(rms_scale(key_projected, kgain), position))
        values = low(low_back(value_projected))
        context = low(low_back(attend(query_rows, keys, values, index, docs)))
        middle = inputs + low_back(matrix_product(context, woutput))
        hidden_two = low(rms_scale(middle, gain_two))
        gate = low_back(matrix_product(hidden_two, wgate))
        upper = low_back(matrix_product(hidden_two, wupper))
        activated = low(jax.nn.silu(gate) * upper)
        return middle + low_back(matrix_product(activated, wdown))
    floats = [item.astype(jnp.float32) for item in (tokens, first_gain, query_weight, key_matrix, value_matrix, querynorm, keynorm, output_weight, second_gain, gate_weight, up_weight, down_weight)]
    result, pull = jax.vjp(layer, floats[0], floats[1], floats[2], floats[3], floats[4], floats[5], floats[6], floats[7], floats[8], floats[9], floats[10], floats[11])
    grads = pull(grad_out.astype(jnp.float32))
    return (result.astype(jnp.bfloat16), grads[0].astype(jnp.bfloat16), grads[1], grads[2], grads[3], grads[4], grads[5], grads[6], grads[7], grads[8], grads[9], grads[10], grads[11])
```

```python
import functools

import jax
import jax.numpy as jnp
from jax import lax
from jax.experimental import pallas as pl
from jax.experimental.pallas import tpu as pltpu
from jax.sharding import PartitionSpec as P

EPS = 1e-06
THETA = 1000000.0
MESH = pl.DeviceIdType.MESH
F32 = jnp.float32
BF16 = jnp.bfloat16
LOG2E = 1.4426950408889634
LN2 = 0.6931471805599453
HEAD_DIM = 128
SCALE = HEAD_DIM**-0.5
VMEM_LIMIT = 62 * 2**20

QC, KC, VC, OC, GC, UC, DC, END = 0, 256, 384, 512, 768, 1152, 1536, 1920


def nn(a, b):
    return jnp.dot(a, b, preferred_element_type=F32)


def nt(a, b):
    return lax.dot_general(a, b, (((1,), (1,)), ((), ())), preferred_element_type=F32)


def tn(a, b):
    return lax.dot_general(a, b, (((0,), (0,)), ((), ())), preferred_element_type=F32)


class HeadRing:
    def __init__(self):
        self.b = lax.axis_index("blk")
        h = lax.axis_index("head")
        self.p, self.r = lax.div(h, 4), lax.rem(h, 4)

    def at(self, dp, dr):
        return lax.rem(self.p + dp, 2) * 4 + lax.rem(self.r + dr + 4, 4)

    plane = at
    slot = at

    def dev(self, dp, dr):
        return (self.b, self.at(dp, dr))

    def near(self):
        return [self.dev(1, 0), self.dev(0, 1), self.dev(0, -1)]


class BlkRing:
    def __init__(self):
        b = lax.axis_index("blk")
        self.h = lax.axis_index("head")
        self.b = b
        self.p, self.r, self.c = lax.div(b, 8), lax.rem(lax.div(b, 2), 4), lax.rem(b, 2)

    def plane(self, dp, dr):
        return lax.rem(self.p + dp, 2) * 4 + lax.rem(self.r + dr + 4, 4)

    def slot(self, dp, dr):
        return self.plane(dp, dr) * 2 + self.c

    def dev(self, dp, dr):
        return (self.slot(dp, dr), self.h)

    def sibling(self):
        return (self.plane(0, 0) * 2 + 1 - self.c, self.h)

    def mirror(self):
        return (15 - self.b, self.h)

    def near(self):
        return [self.dev(1, 0), self.dev(0, 1), self.dev(0, -1), self.sibling()]


def barrier(devices):
    sem = pltpu.get_barrier_semaphore()
    for d in devices:
        pl.semaphore_signal(sem, inc=1, device_id=d, device_id_type=MESH)
    pl.semaphore_wait(sem, len(devices))


def put(src, dst, ss, rs, dev):
    copy = pltpu.make_async_remote_copy(
        src_ref=src, dst_ref=dst, send_sem=ss, recv_sem=rs, device_id=dev, device_id_type=MESH
    )
    copy.start()
    return copy


def gather(ring, full, n, ss, rs, sib=None):
    def rows(dp, dr, part=None):
        base = pl.multiple_of(ring.slot(dp, dr) * n, n)
        if part is None:
            return full.at[pl.ds(base, n)]
        return full.at[pl.ds(base + part * (n // 2), n // 2)]

    sent = []

    def send(ref, dev, k):
        copy = put(ref, ref, ss.at[k], rs.at[k], dev)
        sent.append(copy)
        return copy

    def across(dp, dr, k):
        if sib is not None:
            ref = rows(dp, dr)
            copy = put(ref, ref, sib[0].at[k], sib[1].at[k], ring.sibling())
            sent.append(copy)
            crossed.append(copy)

    crossed = []
    c0 = send(rows(0, 0), ring.dev(1, 0), 0)
    c1 = send(rows(0, 0), ring.dev(0, 1), 1)
    c2 = send(rows(0, 0), ring.dev(0, -1), 2)
    across(0, 0, 0)
    yield
    c0.wait_recv()
    c3 = send(rows(1, 0), ring.dev(0, 1), 3)
    c4 = send(rows(1, 0), ring.dev(0, -1), 4)
    across(1, 0, 1)
    c1.wait_recv()
    c5 = send(rows(0, -1, 0), ring.dev(0, 1), 5)
    across(0, -1, 2)
    c2.wait_recv()
    c6 = send(rows(0, 1, 1), ring.dev(0, -1), 6)
    across(0, 1, 3)
    yield
    c5.wait_recv()
    c6.wait_recv()
    c7 = send(rows(0, 2), ring.dev(1, 0), 7)
    across(0, 2, 4)
    yield
    c3.wait_recv()
    across(1, -1, 5)
    c4.wait_recv()
    across(1, 1, 6)
    c7.wait_recv()
    across(1, 2, 7)
    yield
    for copy in crossed:
        copy.wait_recv()
    for copy in sent:
        copy.wait_send()


def add_into(dst, src):
    dst[...] = (dst[...].astype(F32) + src[...].astype(F32)).astype(dst.dtype)


def scatter(ring, part, bufs, ss, rs):
    n = part.shape[1]
    sent = []

    def own(dp, dr, half=None):
        view = part.at[ring.plane(dp, dr)]
        if half is None:
            return view
        return view.at[pl.ds(half * (n // 2), n // 2)]

    def send(ref, dst, dev, k):
        copy = put(ref, dst, ss.at[k], rs.at[k], dev)
        sent.append(copy)
        return copy

    far, up, down, home, from_up, from_down, halves = (bufs.at[k] for k in range(7))
    first, second = halves.at[pl.ds(0, n // 2)], halves.at[pl.ds(n // 2, n // 2)]
    c0 = send(own(1, 2), far, ring.dev(1, 0), 0)
    c1 = send(own(1, 1), up, ring.dev(0, 1), 1)
    c2 = send(own(1, -1), down, ring.dev(0, -1), 2)
    yield
    c0.wait_recv()
    add_into(own(0, 2), far)
    c3 = send(own(0, 2, 0), first, ring.dev(0, 1), 3)
    c4 = send(own(0, 2, 1), second, ring.dev(0, -1), 4)
    c1.wait_recv()
    c2.wait_recv()
    mine = own(1, 0)
    mine[...] = (mine[...].astype(F32) + up[...].astype(F32) + down[...].astype(F32)).astype(mine.dtype)
    c5 = send(own(1, 0), home, ring.dev(1, 0), 5)
    yield
    c3.wait_recv()
    add_into(own(0, 1, 0), first)
    c6 = send(own(0, 1), from_up, ring.dev(0, 1), 6)
    c4.wait_recv()
    add_into(own(0, -1, 1), second)
    c7 = send(own(0, -1), from_down, ring.dev(0, -1), 7)
    yield
    c5.wait_recv()
    c6.wait_recv()
    c7.wait_recv()
    for copy in sent:
        copy.wait_send()


def total(ring, part, bufs):
    return (
        part[ring.plane(0, 0)].astype(F32)
        + bufs[3].astype(F32)
        + bufs[4].astype(F32)
        + bufs[5].astype(F32)
    )


def blk_scatter(ring, part, both, bufs, ss, rs, sib_ss, sib_rs):
    copy = put(part.at[:, 1 - ring.c], both, sib_ss, sib_rs, ring.sibling())
    yield
    copy.wait_recv()

    def body(k, carry):
        both[k] = (both[k].astype(F32) + part[k, ring.c].astype(F32)).astype(both.dtype)
        return carry

    lax.fori_loop(0, 8, body, 0)
    copy.wait_send()
    yield from scatter(ring, both, bufs, ss, rs)


def together(*parts):
    live = list(parts)
    while live:
        for item in list(live):
            try:
                next(item)
            except StopIteration:
                live.remove(item)


def sems(*counts):
    return [pltpu.SemaphoreType.DMA((c,)) for c in counts]


VM = pl.BlockSpec(memory_space=pltpu.VMEM)
SM = pl.BlockSpec(memory_space=pltpu.SMEM)


def kernel_call(body, outs, scratch, collective_id, args, smem=0, flops=0):
    params = dict(vmem_limit_bytes=VMEM_LIMIT)
    if collective_id is not None:
        params.update(collective_id=collective_id, has_side_effects=True)
    return pl.pallas_call(
        body,
        out_shape=[jax.ShapeDtypeStruct(s, d) for s, d in outs],
        in_specs=[SM] * smem + [VM] * (len(args) - smem),
        out_specs=[VM] * len(outs),
        scratch_shapes=scratch,
        compiler_params=pltpu.CompilerParams(**params),
    )(*args)


def chunk(i, size):
    return pl.ds(pl.multiple_of(i * size, size), size)


def loop(count, body):
    def step(i, carry):
        body(i)
        return carry

    lax.fori_loop(0, count, step, 0)


def rope(v, cosine, sine):
    return v * cosine + pltpu.roll(v, 64, 1) * sine


def rope_back(g, cosine, sine):
    return g * cosine + pltpu.roll(g * sine, 64, 1)


def inverse(v):
    return lax.rsqrt(jnp.mean(v * v, axis=-1, keepdims=True) + EPS)


def project_kernel(
    tok, gain, wcat, cosine, sine, qgain, kgain,
    block, weights, query, kv, qraw, kraw,
    hs, hr, ws, wr, cs, cr,
):
    head, blk = HeadRing(), BlkRing()
    x = tok[...].astype(F32)
    block[chunk(head.slot(0, 0), 128), :] = (x * inverse(x) * gain[...]).astype(BF16)
    weights[chunk(blk.slot(0, 0), 64), :] = wcat[...]
    barrier(head.near() + blk.near())
    together(gather(blk, weights, 64, ws, wr, (cs, cr)), gather(head, block, 128, hs, hr))

    def rows(i):
        at = chunk(i, 256)
        out = nn(block[at, :], weights[:, QC:OC])
        cs_, sn_ = cosine[at, :], sine[at, :]
        for k in range(2):
            v = out[:, 128 * k : 128 * k + 128]
            qraw[at, 128 * k : 128 * k + 128] = v
            v = rope(v * inverse(v) * qgain[...], cs_, sn_) * (SCALE * LOG2E)
            query[at, 128 * k : 128 * k + 128] = v.astype(BF16)
        v = out[:, KC:VC]
        kraw[at, :] = v
        kv[at, 0:128] = rope(v * inverse(v) * kgain[...], cs_, sn_).astype(BF16)
        kv[at, 128:256] = out[:, VC:OC].astype(BF16)

    loop(4, rows)


def share_kernel(kv, dy, query, kv_all, block_dy, query_far, hs, hr, ws, wr, cs, cr, ms, mr):
    head, blk = HeadRing(), BlkRing()
    kv_all[chunk(blk.slot(0, 0), 1024), :] = kv[...]
    block_dy[chunk(head.slot(0, 0), 128), :] = dy[...]
    barrier(head.near() + blk.near() + [blk.mirror()])
    swap = put(query.at[pl.ds(512, 512)], query_far, ms.at[0], mr.at[0], blk.mirror())
    together(gather(blk, kv_all, 1024, ws, wr, (cs, cr)), gather(head, block_dy, 128, hs, hr))
    swap.wait()


def spans(half):
    top = jnp.minimum(half, 30)
    low = jnp.minimum(half + 1, 2)
    high = jnp.maximum(top, 2)
    return top, low, high, low + jnp.maximum(half + 1 - high, 0)


def begin_of(starts, index):
    begin = jnp.zeros_like(index)
    for k in range(1, 4):
        begin = jnp.where(index >= starts[k], starts[k], begin)
    return begin


def attend_kernel(starts, qa, qb, kv, ctxa, ctxb, lsea, lseb, stack, accum):
    block = lax.axis_index("blk")
    ones = jnp.ones((512, 128), BF16)
    for q, ctx, lse, half in ((qa, ctxa, lsea, 2 * block), (qb, ctxb, lseb, 31 - 2 * block)):
        stack[0:512, :] = q[:, 0:128]
        stack[512:1024, :] = q[:, 128:256]
        accum[...] = jnp.zeros_like(accum)
        top, low, high, masked_count = spans(half)

        def tile(j, masked):
            keys = kv[chunk(j, 512), 0:128]
            values = jnp.concatenate([kv[chunk(j, 512), 128:256], ones], axis=1)
            for c in range(4):
                s = nt(stack[c * 256 : c * 256 + 256, :], keys)
                p = jnp.exp2(s)
                if masked:
                    qi = half * 512 + (c % 2) * 256 + lax.broadcasted_iota(jnp.int32, (256, 1), 0)
                    ki = j * 512 + lax.broadcasted_iota(jnp.int32, (1, 512), 1)
                    p = jnp.where((ki >= begin_of(starts, qi)) & (ki <= qi), p, 0.0)
                accum[c * 256 : c * 256 + 256, :] += nn(p.astype(BF16), values)

        def plain(j, carry):
            tile(j, False)
            return carry

        lax.fori_loop(2, top, plain, 0)
        for c in range(4):
            qi = half * 512 + (c % 2) * 256 + lax.broadcasted_iota(jnp.int32, (256, 1), 0)
            keep = qi < starts[2]
            accum[c * 256 : c * 256 + 256, :] = jnp.where(keep, accum[c * 256 : c * 256 + 256, :], 0.0)

        def careful(t, carry):
            tile(jnp.where(t < low, t, t - low + high), True)
            return carry

        lax.fori_loop(0, masked_count, careful, 0)
        for k in range(2):
            at = pl.ds(512 * k, 512)
            norm = accum[at, 128:256]
            ctx[:, 128 * k : 128 * k + 128] = (accum[at, 0:128] / norm).astype(BF16)
            lse[at, :] = jnp.log2(norm)


def split3(v):
    a = (-v).astype(BF16)
    rest = -v - a.astype(F32)
    b = rest.astype(BF16)
    c = (rest - b.astype(F32)).astype(BF16)
    lane = lax.broadcasted_iota(jnp.int32, v.shape, 1)
    zero = jnp.zeros_like(v)
    out = jnp.where(lane == 0, a.astype(F32), jnp.where(lane == 1, b.astype(F32), jnp.where(lane == 2, c.astype(F32), zero)))
    return out


def attend_back_kernel(
    starts, qa, qb, ctxa, ctxb, lsea, lseb, da, db, kv,
    dkv, dqa, dqb,
    qx, qfar, dox, dq, acc,
):
    block = lax.axis_index("blk")
    ones = jnp.ones((512, 128), BF16)

    def clear(j):
        acc[j] = jnp.zeros((512, 256), F32)

    loop(32, clear)
    for q, ctx, lse, do, dq_out, half in (
        (qa, ctxa, lsea, da, dqa, 2 * block),
        (qb, ctxb, lseb, db, dqb, 31 - 2 * block),
    ):
        for k in range(2):
            at = pl.ds(512 * k, 512)
            cols = slice(128 * k, 128 * k + 128)
            qx[at, 0:128] = q[:, cols]
            terms = split3(lse[at, :])
            qx[at, 128:256] = terms.astype(BF16)
            qi = half * 512 + lax.broadcasted_iota(jnp.int32, (512, 128), 0)
            lane = lax.broadcasted_iota(jnp.int32, (512, 128), 1)
            gone = jnp.where(lane == 0, -1e30, 0.0)
            qfar[at, 0:128] = q[:, cols]
            qfar[at, 128:256] = jnp.where(qi < starts[2], terms, gone).astype(BF16)
            grad = do[:, cols]
            delta = jnp.sum(grad.astype(F32) * ctx[:, cols].astype(F32), axis=1, keepdims=True)
            dox[at, 0:128] = grad
            dox[at, 128:256] = split3(jnp.broadcast_to(delta, (512, 128))).astype(BF16)
        dq[...] = jnp.zeros_like(dq)
        top, low, high, masked_count = spans(half)

        def tile(j, masked):
            keys = kv[chunk(j, 512), 0:128]
            values = kv[chunk(j, 512), 128:256]
            kx = jnp.concatenate([keys, ones], axis=1)
            vx = jnp.concatenate([values, ones], axis=1)
            source = qx if masked else qfar
            for c in range(4):
                at = pl.ds(c * 256, 256)
                p = jnp.exp2(nt(kx, source[at, :]))
                if masked:
                    ki = j * 512 + lax.broadcasted_iota(jnp.int32, (512, 1), 0)
                    qi = half * 512 + (c % 2) * 256 + lax.broadcasted_iota(jnp.int32, (1, 256), 1)
                    p = jnp.where((ki >= begin_of(starts, qi)) & (ki <= qi), p, 0.0)
                ds = (p * nt(vx, dox[at, :])).astype(BF16)
                acc[j, :, 0:128] += nn(ds, source[at, 0:128])
                acc[j, :, 128:256] += nn(p.astype(BF16), dox[at, 0:128])
                dq[at, :] += tn(ds, keys)

        def plain(j, carry):
            tile(j, False)
            return carry

        def careful(t, carry):
            tile(jnp.where(t < low, t, t - low + high), True)
            return carry

        lax.fori_loop(2, top, plain, 0)
        lax.fori_loop(0, masked_count, careful, 0)
        for k in range(2):
            dq_out[:, 128 * k : 128 * k + 128] = (dq[512 * k : 512 * k + 512, :] * SCALE).astype(BF16)

    def store(j):
        dkv[lax.div(j, 4), lax.rem(lax.div(j, 2), 2), chunk(lax.rem(j, 2), 512), :] = acc[j].astype(BF16)

    loop(32, store)


def middle_kernel(
    ctxa, ctxb, weights, tok, gain,
    ctx, middle, block,
    part, bufs, hs, hr, gs, gr, ms, mr,
):
    head, blk = HeadRing(), BlkRing()
    barrier(head.near() + [blk.mirror()])
    swap = put(ctxb, ctx.at[pl.ds(512, 512)], ms.at[0], mr.at[0], blk.mirror())
    ctx[0:512, :] = ctxa[...]

    def rows(i):
        for k in range(2):
            part[2 * i + k] = nt(ctx[chunk(2 * i + k, 128), :], weights[:, OC:GC]).astype(BF16)

    loop(2, rows)
    swap.wait()

    def rest(i):
        rows(i + 2)

    loop(2, rest)
    together(scatter(head, part, bufs, hs, hr))
    mid = tok[...].astype(F32) + total(head, part, bufs)
    middle[...] = mid
    block[chunk(head.slot(0, 0), 128), :] = (mid * inverse(mid) * gain[...]).astype(BF16)
    together(gather(head, block, 128, gs, gr))


def norm_back(v, gain, grad):
    r = inverse(v)
    n = v * r
    scaled = grad * gain
    return grad * n, r * (scaled - n * jnp.mean(scaled * n, axis=-1, keepdims=True))


def forward_kernel(
    block_two, block_dy, weights, middle, dy, gain, ctx,
    ff_part, wpart, middle_grad, gain_part, grad_near, grad_far, block_mid,
    part, bufs, acts, grad_all, hs, hr, gs, gr, ms, mr,
):
    head, blk = HeadRing(), BlkRing()

    def rows(i):
        at = chunk(i, 128)
        hidden = block_two[at, :]
        both = nn(hidden, weights[:, GC:DC])
        gate, upper = both[:, 0:384], both[:, 384:768]
        sigma = 1.0 / (1.0 + jnp.exp(-gate))
        silu = gate * sigma
        act = (silu * upper).astype(BF16)
        act_grad = nn(block_dy[at, :], weights[:, DC:END])
        gate_low = (act_grad * upper * sigma * (1.0 + gate * (1.0 - sigma))).astype(BF16)
        up_low = (act_grad * silu).astype(BF16)
        low = jnp.concatenate([gate_low, up_low], axis=1)
        acts[at, 0:768] = low
        acts[at, 768:1152] = act
        part[i] = nt(low, weights[:, GC:DC]).astype(BF16)

    loop(8, rows)
    barrier(head.near() + [blk.mirror()])
    reduce = scatter(head, part, bufs, hs, hr)
    next(reduce)

    def down(i):
        ff_part[i] = nt(acts[chunk(i, 128), 768:1152], weights[:, DC:END]).astype(BF16)

    loop(8, down)
    next(reduce)

    def grads(i):
        wpart[chunk(i, 128), 256:1024] = tn(block_two[:, chunk(i, 128)], acts[:, 0:768]).astype(BF16)

    loop(8, grads)
    together(reduce)
    gain_terms, part_grad = norm_back(middle[...], gain[...], total(head, part, bufs))
    mid_grad = dy[...].astype(F32) + part_grad
    middle_grad[...] = mid_grad
    block_mid[chunk(head.slot(0, 0), 128), :] = mid_grad.astype(BF16)
    collect = gather(head, block_mid, 128, gs, gr)
    next(collect)
    gain_part[...] = jnp.sum(gain_terms, axis=0, keepdims=True)

    def down_grads(i):
        wpart[chunk(i, 128), 1024:1408] = tn(block_dy[:, chunk(i, 128)], acts[:, 768:1152]).astype(BF16)

    loop(8, down_grads)
    together(collect)

    def context_grads(i):
        at = chunk(i, 256)
        grad_all[at, :] = nn(block_mid[at, :], weights[:, OC:GC]).astype(BF16)

    loop(4, context_grads)
    swap = put(grad_all.at[pl.ds(512, 512)], grad_far, ms.at[0], mr.at[0], blk.mirror())
    grad_near[...] = grad_all[0:512, :]

    def output_grads(i):
        wpart[chunk(i, 128), 0:256] = tn(block_mid[:, chunk(i, 128)], ctx[...]).astype(BF16)

    loop(8, output_grads)
    swap.wait()


def sums_kernel(
    dkv, ff_part, wpart, dq_far, middle,
    kv_grad, layer_out, wsum, dq_home,
    kv_both, kv_bufs, ff_work, ff_bufs, w_both, w_bufs,
    ks, kr, fs, fr, ws, wr, cs, cr, ms, mr,
):
    head, blk = HeadRing(), BlkRing()
    ff_work[...] = ff_part[...]
    barrier(head.near() + blk.near() + [blk.mirror()])
    swap = put(dq_far, dq_home, ms.at[0], mr.at[0], blk.mirror())
    together(
        blk_scatter(blk, dkv, kv_both, kv_bufs, ks, kr, cs.at[0], cr.at[0]),
        scatter(head, ff_work, ff_bufs, fs, fr),
        blk_scatter(blk, wpart, w_both, w_bufs, ws, wr, cs.at[1], cr.at[1]),
    )
    kv_grad[...] = total(blk, kv_both, kv_bufs)
    wsum[...] = total(blk, w_both, w_bufs)
    layer_out[...] = (middle[...] + total(head, ff_work, ff_bufs)).astype(BF16)
    swap.wait()


def finish_kernel(
    dq_near, dq_home, kv_grad, qraw, kraw, cosine, sine, qgain, kgain, block_one, weights, tok, gain, middle_grad, gain_two,
    tokens_grad, wsum, gains,
    low, part, bufs, wpart, w_both, w_bufs, gvec, gin, gstage, gin2,
    hs, hr, ws, wr, cs, cr, g1s, g1r, g2s, g2r,
):
    head, blk = HeadRing(), BlkRing()
    gvec[...] = jnp.zeros_like(gvec)

    def back(raw, grad, at, gains_):
        cs_, sn_ = cosine[at, :], sine[at, :]
        return norm_back(raw, gains_, rope_back(grad, cs_, sn_))

    for i in range(4):
        at = slice(256 * i, 256 * i + 256)
        source = dq_near if i < 2 else dq_home
        local = slice(256 * (i % 2), 256 * (i % 2) + 256)
        for k in range(2):
            cols = slice(128 * k, 128 * k + 128)
            terms, out = back(qraw[at, cols], source[local, cols].astype(F32), at, qgain[...])
            low[at, cols] = out.astype(BF16)
            gvec[:, 2048:2176] += jnp.sum(terms, axis=0, keepdims=True)
        terms, out = back(kraw[at, :], kv_grad[at, 0:128] * LN2, at, kgain[...])
        low[at, 256:384] = out.astype(BF16)
        gvec[:, 2176:2304] += jnp.sum(terms, axis=0, keepdims=True)
        low[at, 384:512] = kv_grad[at, 128:256].astype(BF16)

    def rows(i):
        part[i] = nt(low[chunk(i, 128), :], weights[:, QC:OC]).astype(BF16)

    loop(8, rows)
    head_peers = [(dp, dr) for dp in range(2) for dr in range(4) if (dp, dr) != (0, 0)]
    blk_peers = [(dp, dr, dc) for dp in range(2) for dr in range(4) for dc in range(2) if (dp, dr, dc) != (0, 0, 0)]

    def blk_dev(dp, dr, dc):
        return (blk.plane(dp, dr) * 2 + lax.rem(blk.c + dc, 2), blk.h)

    barrier([head.dev(*d) for d in head_peers] + [blk_dev(*d) for d in blk_peers])
    reduce = scatter(head, part, bufs, hs, hr)
    next(reduce)

    def grads(i):
        plane, core = lax.div(i, 2), lax.rem(i, 2)
        out = tn(block_one[:, chunk(i, 128)], low[...]).astype(BF16)
        wpart[i, 0] = out[0:64]
        wpart[i, 1] = out[64:128]

    loop(8, grads)
    wreduce = blk_scatter(blk, wpart, w_both, w_bufs, ws, wr, cs.at[0], cr.at[0])
    together(wreduce, reduce)
    x = tok[...].astype(F32)
    terms, part_grad = norm_back(x, gain[...], total(head, part, bufs))
    gvec[:, 0:1024] = jnp.sum(terms, axis=0, keepdims=True)
    gvec[:, 1024:2048] = gain_two[...]
    first = [put(gvec, gin.at[i], g1s.at[i], g1r.at[i], head.dev(*d)) for i, d in enumerate(head_peers)]
    tokens_grad[...] = (middle_grad[...] + part_grad).astype(BF16)
    wsum[...] = total(blk, w_both, w_bufs)
    for copy in first:
        copy.wait()
    summed = gvec[...]
    for i in range(7):
        summed = summed + gin[i]
    for k in range(8):
        gstage[k, :, 0:128] = summed[:, 128 * k : 128 * k + 128]
        gstage[k, :, 128:256] = summed[:, 1024 + 128 * k : 1152 + 128 * k]
        gstage[k, :, 256:512] = summed[:, 2048:2304]
    second = [
        put(gstage.at[blk.plane(d[0], d[1])], gin2.at[i], g2s.at[i], g2r.at[i], blk_dev(*d))
        for i, d in enumerate(blk_peers)
    ]
    for copy in second:
        copy.wait()
    out = gstage[blk.plane(0, 0)]
    for i in range(15):
        out = out + gin2[i]
    gains[...] = out


def per_device(
    tokens, doc_starts, first_gain, query_weight, key_matrix, value_matrix, querynorm, keynorm,
    output_weight, second_gain, gate_weight, up_weight, down_weight, grad_out,
):
    block_id = lax.axis_index("blk")
    head_id = lax.axis_index("head")
    index = block_id * 1024 + jnp.arange(1024, dtype=jnp.int32)
    begin = jnp.max(jnp.where(doc_starts[None, :] <= index[:, None], doc_starts[None, :], 0), axis=1)
    position = (index - begin).astype(F32)
    freqs = THETA ** (-(jnp.arange(64, dtype=F32) * 2.0 / HEAD_DIM))
    angle = position[:, None] * freqs[None, :]
    cosine, sine = jnp.cos(angle), jnp.sin(angle)
    cosine = jnp.concatenate([cosine, cosine], axis=1)
    sine = jnp.concatenate([-sine, sine], axis=1)
    wcat = jnp.concatenate(
        [query_weight, key_matrix, value_matrix, output_weight.T, gate_weight, up_weight, down_weight.T], axis=1
    )
    gain1 = first_gain.astype(F32)[None, :]
    gain2 = second_gain.astype(F32)[None, :]
    qgain = querynorm.astype(F32)[None, :]
    kgain = keynorm.astype(F32)[None, :]
    S = jax.ShapeDtypeStruct
    block_one, weights, query, kv, qraw, kraw = kernel_call(
        project_kernel,
        [((1024, 1024), BF16), ((1024, 1920), BF16), ((1024, 256), BF16), ((1024, 256), BF16), ((1024, 256), F32), ((1024, 128), F32)],
        sems(8, 8, 8, 8, 8, 8),
        1,
        (tokens, gain1, wcat, cosine, sine, qgain, kgain),
    )
    kv_all, block_dy, query_far = kernel_call(
        share_kernel,
        [((16384, 256), BF16), ((1024, 1024), BF16), ((512, 256), BF16)],
        sems(8, 8, 8, 8, 8, 8, 1, 1),
        2,
        (kv, grad_out, query),
    )
    query_near = query[0:512]
    ctx_near, ctx_far, lse_near, lse_far = kernel_call(
        attend_kernel,
        [((512, 256), BF16), ((512, 256), BF16), ((1024, 128), F32), ((1024, 128), F32)],
        [pltpu.VMEM((1024, 128), BF16), pltpu.VMEM((1024, 256), F32)],
        None,
        (doc_starts, query_near, query_far, kv_all),
        smem=1,
    )
    ctx, middle, block_two = kernel_call(
        middle_kernel,
        [((1024, 256), BF16), ((128, 1024), F32), ((1024, 1024), BF16)],
        [pltpu.VMEM((8, 128, 1024), BF16), pltpu.VMEM((7, 128, 1024), BF16)] + sems(8, 8, 8, 8, 1, 1),
        3,
        (ctx_near, ctx_far, weights, tokens, gain2),
    )
    ff_part, wpart, middle_grad, gain_two, grad_near, grad_far, block_mid = kernel_call(
        forward_kernel,
        [
            ((8, 128, 1024), BF16), ((1024, 1408), BF16), ((128, 1024), F32), ((1, 1024), F32),
            ((512, 256), BF16), ((512, 256), BF16), ((1024, 1024), BF16),
        ],
        [
            pltpu.VMEM((8, 128, 1024), BF16), pltpu.VMEM((7, 128, 1024), BF16),
            pltpu.VMEM((1024, 1152), BF16), pltpu.VMEM((1024, 256), BF16),
        ] + sems(8, 8, 8, 8, 1, 1),
        4,
        (block_two, block_dy, weights, middle, grad_out, gain2, ctx),
    )
    dkv, dq_near, dq_far = kernel_call(
        attend_back_kernel,
        [((8, 2, 1024, 256), BF16), ((512, 256), BF16), ((512, 256), BF16)],
        [
            pltpu.VMEM((1024, 256), BF16), pltpu.VMEM((1024, 256), BF16), pltpu.VMEM((1024, 256), BF16),
            pltpu.VMEM((1024, 128), F32), pltpu.VMEM((32, 512, 256), F32),
        ],
        None,
        (doc_starts, query_near, query_far, ctx_near, ctx_far, lse_near, lse_far, grad_near, grad_far, kv_all),
        smem=1,
    )
    kv_grad, layer_out, wsum, dq_home = kernel_call(
        sums_kernel,
        [((1024, 256), F32), ((128, 1024), BF16), ((64, 1408), F32), ((512, 256), BF16)],
        [
            pltpu.VMEM((8, 1024, 256), BF16), pltpu.VMEM((7, 1024, 256), BF16),
            pltpu.VMEM((8, 128, 1024), BF16), pltpu.VMEM((7, 128, 1024), BF16),
            pltpu.VMEM((8, 64, 1408), BF16), pltpu.VMEM((7, 64, 1408), BF16),
        ] + sems(8, 8, 8, 8, 8, 8, 2, 2, 1, 1),
        5,
        (dkv, ff_part, wpart.reshape(8, 2, 64, 1408), dq_far, middle),
    )
    tokens_grad, qkv_sum, gains = kernel_call(
        finish_kernel,
        [((128, 1024), BF16), ((64, 512), F32), ((1, 512), F32)],
        [
            pltpu.VMEM((1024, 512), BF16), pltpu.VMEM((8, 128, 1024), BF16), pltpu.VMEM((7, 128, 1024), BF16),
            pltpu.VMEM((8, 2, 64, 512), BF16), pltpu.VMEM((8, 64, 512), BF16), pltpu.VMEM((7, 64, 512), BF16),
            pltpu.VMEM((1, 2304), F32), pltpu.VMEM((7, 1, 2304), F32), pltpu.VMEM((8, 1, 512), F32), pltpu.VMEM((15, 1, 512), F32),
        ] + sems(8, 8, 8, 8, 1, 1, 7, 7, 15, 15),
        6,
        (
            dq_near, dq_home, kv_grad, qraw, kraw, cosine, sine, qgain, kgain, block_one, weights, tokens,
            gain1, middle_grad, gain_two,
        ),
    )
    gains = gains[0]
    offset = (block_id % 2) * 64 + head_id * 8
    lane = block_id * 8 + head_id
    return (
        layer_out,
        tokens_grad,
        lax.dynamic_slice_in_dim(gains, offset, 8),
        qkv_sum[:, 0:256],
        qkv_sum[:, 256:384],
        qkv_sum[:, 384:512],
        lax.dynamic_slice_in_dim(gains, 256 + lane, 1),
        lax.dynamic_slice_in_dim(gains, 384 + lane, 1),
        wsum[:, 0:256].T,
        lax.dynamic_slice_in_dim(gains, 128 + offset, 8),
        wsum[:, 256:640],
        wsum[:, 640:1024],
        wsum[:, 1024:1408].T,
    )


def solution(mesh):
    return jax.shard_map(
        per_device,
        mesh=mesh,
        in_specs=(
            P(("blk", "head"), None),
            P(),
            P(),
            P("blk", "head"),
            P("blk", "head"),
            P("blk", "head"),
            P(),
            P(),
            P("head", "blk"),
            P(),
            P("blk", "head"),
            P("blk", "head"),
            P("head", "blk"),
            P(("blk", "head"), None),
        ),
        out_specs=(
            P(("blk", "head"), None),
            P(("blk", "head"), None),
            P(("blk", "head")),
            P("blk", "head"),
            P("blk", "head"),
            P("blk", "head"),
            P(("blk", "head")),
            P(("blk", "head")),
            P("head", "blk"),
            P(("blk", "head")),
            P("blk", "head"),
            P("blk", "head"),
            P("head", "blk"),
        ),
        check_vma=False,
    )
```

```python
import functools

import jax
import jax.numpy as jnp
from jax import lax
from jax.experimental import pallas as pl
from jax.experimental.pallas import tpu as pltpu
from jax.sharding import PartitionSpec as P

EPS = 1e-06
THETA = 1000000.0
MESH = pl.DeviceIdType.MESH
F32 = jnp.float32
BF16 = jnp.bfloat16
LOG2E = 1.4426950408889634
LN2 = 0.6931471805599453
HEAD_DIM = 128
SCALE = HEAD_DIM**-0.5
VMEM_LIMIT = 64 * 2**20 - 2**16

QC, KC, VC, OC, GC, UC, DC, END = 0, 256, 384, 512, 768, 1152, 1536, 1920


def nn(a, b):
    return jnp.dot(a, b, preferred_element_type=F32)


def nt(a, b):
    return lax.dot_general(a, b, (((1,), (1,)), ((), ())), preferred_element_type=F32)


def tn(a, b):
    return lax.dot_general(a, b, (((0,), (0,)), ((), ())), preferred_element_type=F32)


def chunk(i, size):
    return pl.ds(pl.multiple_of(i * size, size), size)


def loop(count, body):
    def step(i, carry):
        body(i)
        return carry

    lax.fori_loop(0, count, step, 0)


class HeadRing:
    def __init__(self):
        self.b = lax.axis_index("blk")
        h = lax.axis_index("head")
        self.h = h
        self.p, self.r = lax.div(h, 4), lax.rem(h, 4)

    def plane(self, dp, dr):
        return lax.rem(self.p + dp, 2) * 4 + lax.rem(self.r + dr + 4, 4)

    slot = plane

    def dev(self, dp, dr):
        return (self.b, self.plane(dp, dr))

    def peers(self):
        return [self.dev(dp, dr) for dp in range(2) for dr in range(4) if (dp, dr) != (0, 0)]


class BlkRing:
    def __init__(self):
        b = lax.axis_index("blk")
        self.h = lax.axis_index("head")
        self.b = b
        self.p, self.r, self.c = lax.div(b, 8), lax.rem(lax.div(b, 2), 4), lax.rem(b, 2)

    def plane(self, dp, dr):
        return lax.rem(self.p + dp, 2) * 4 + lax.rem(self.r + dr + 4, 4)

    def slot(self, dp, dr, dc=0):
        return self.plane(dp, dr) * 2 + lax.rem(self.c + dc, 2)

    def dev(self, dp, dr, dc=0):
        return (self.slot(dp, dr, dc), self.h)

    def sibling(self):
        return self.dev(0, 0, 1)

    def mirror(self):
        return (15 - self.b, self.h)

    def peers(self):
        every = [(dp, dr, dc) for dp in range(2) for dr in range(4) for dc in range(2)]
        return [self.dev(*d) for d in every if d != (0, 0, 0)]


def barrier(devices):
    sem = pltpu.get_barrier_semaphore()
    for d in devices:
        pl.semaphore_signal(sem, inc=1, device_id=d, device_id_type=MESH)
    pl.semaphore_wait(sem, len(devices))


def remote(src, dst, ss, rs, dev):
    return pltpu.make_async_remote_copy(
        src_ref=src, dst_ref=dst, send_sem=ss, recv_sem=rs, device_id=dev, device_id_type=MESH
    )


class Gather:
    ORDER = ((0, 0), (1, 0), (0, -1), (0, 1), (0, 2), (1, -1), (1, 1), (1, 2))

    def __init__(self, ring, full, n, ss, rs, sib=None, off=0, stride=None, k0=0):
        self.ring, self.full, self.n, self.ss, self.rs, self.sib = ring, full, n, ss, rs, sib
        self.off, self.stride, self.k0 = off, stride or n, k0

    def rows(self, dp, dr, part=None):
        base = self.ring.slot(dp, dr) * self.stride + self.off
        size = self.n
        if part is not None:
            size = self.n // 2
            base = base + part * size
        return self.full.at[pl.ds(pl.multiple_of(base, size), size)]

    def copy(self, k):
        ring = self.ring
        ref, dev = (
            lambda: (self.rows(0, 0), ring.dev(1, 0)),
            lambda: (self.rows(0, 0), ring.dev(0, 1)),
            lambda: (self.rows(0, 0), ring.dev(0, -1)),
            lambda: (self.rows(1, 0), ring.dev(0, 1)),
            lambda: (self.rows(1, 0), ring.dev(0, -1)),
            lambda: (self.rows(0, -1, 0), ring.dev(0, 1)),
            lambda: (self.rows(0, 1, 1), ring.dev(0, -1)),
            lambda: (self.rows(0, 2), ring.dev(1, 0)),
        )[k]()
        return remote(ref, ref, self.ss.at[self.k0 + k], self.rs.at[self.k0 + k], dev)

    def send(self, *ks):
        for k in ks:
            self.copy(k).start()

    def wait(self, *ks):
        for k in ks:
            self.copy(k).wait_recv()

    def crossing(self, k):
        ref = self.rows(*self.ORDER[k])
        return remote(ref, ref, self.sib[0].at[k], self.sib[1].at[k], self.ring.sibling())

    def cross(self, *ks):
        if self.sib is not None:
            for k in ks:
                self.crossing(k).start()

    def begin(self):
        self.send(1, 2, 0)
        self.cross(0)

    def step1(self):
        self.wait(1)
        self.send(5)
        self.wait(2)
        self.send(6)
        self.cross(2, 3)
        self.wait(0)
        self.send(3, 4)
        self.cross(1)

    def step2(self):
        self.wait(5, 6)
        self.send(7)
        self.cross(4)

    def step3(self):
        self.wait(3, 4, 7)
        self.cross(5, 6, 7)

    def crossed(self, *ks):
        if self.sib is not None:
            for k in ks:
                self.crossing(k).wait_recv()

    def end(self):
        for k in range(8):
            self.copy(k).wait_send()
        if self.sib is not None:
            for k in range(8):
                self.crossing(k).wait_send()

    def steps(self):
        return [self.begin, self.step1, self.step2, self.step3, lambda: (self.crossed(*range(8)), self.end())]


class Scatter:
    def __init__(self, ring, part, bufs, ss, rs, off=0, n=None, k0=0):
        self.ring, self.part, self.bufs, self.ss, self.rs = ring, part, bufs, ss, rs
        self.off, self.n, self.k0 = off, n or part.shape[1], k0

    def span(self, half):
        if half is None:
            return pl.ds(self.off, self.n)
        return pl.ds(self.off + half * (self.n // 2), self.n // 2)

    def own(self, dp, dr, half=None):
        return self.part.at[self.ring.plane(dp, dr), self.span(half)]

    def buf(self, i, half=None):
        return self.bufs.at[i, self.span(half)]

    def copy(self, k):
        ring, own, buf = self.ring, self.own, self.buf
        src, dst, dev = (
            lambda: (own(1, 2), buf(0), ring.dev(1, 0)),
            lambda: (own(1, 1), buf(1), ring.dev(0, 1)),
            lambda: (own(1, -1), buf(2), ring.dev(0, -1)),
            lambda: (own(0, 2, 0), buf(6, 0), ring.dev(0, 1)),
            lambda: (own(0, 2, 1), buf(6, 1), ring.dev(0, -1)),
            lambda: (own(1, 0), buf(3), ring.dev(1, 0)),
            lambda: (own(0, 1), buf(4), ring.dev(0, 1)),
            lambda: (own(0, -1), buf(5), ring.dev(0, -1)),
        )[k]()
        return remote(src, dst, self.ss.at[self.k0 + k], self.rs.at[self.k0 + k], dev)

    def send(self, *ks):
        for k in ks:
            self.copy(k).start()

    def wait(self, *ks):
        for k in ks:
            self.copy(k).wait_recv()

    def add(self, dst, *srcs):
        value = dst[...].astype(F32)
        for src in srcs:
            value = value + src[...].astype(F32)
        dst[...] = value.astype(dst.dtype)

    def begin(self):
        self.send(1, 2, 0)

    def opposite(self):
        self.wait(0)
        self.add(self.own(0, 2), self.buf(0))
        self.send(3, 4)

    def home(self):
        self.wait(1, 2)
        self.add(self.own(1, 0), self.buf(1), self.buf(2))
        self.send(5)

    def up(self):
        self.wait(3)
        self.add(self.own(0, 1, 0), self.buf(6, 0))
        self.send(6)

    def down(self):
        self.wait(4)
        self.add(self.own(0, -1, 1), self.buf(6, 1))
        self.send(7)

    def end(self):
        self.wait(5, 6, 7)
        for k in range(8):
            self.copy(k).wait_send()

    def steps(self):
        return [self.begin, self.opposite, self.up, self.down, self.home, self.end]

    def total(self):
        out = self.own(0, 0)[...].astype(F32)
        for i in (3, 4, 5):
            out = out + self.buf(i)[...].astype(F32)
        return out


class BlkScatter(Scatter):
    def __init__(self, ring, terms, part, bufs, ss, rs, cs, cr):
        super().__init__(ring, part, bufs, ss, rs)
        self.terms, self.cs, self.cr = terms, cs, cr

    def crossing(self):
        return remote(self.terms.at[:, 1 - self.ring.c], self.part, self.cs, self.cr, self.ring.sibling())

    def cross(self):
        self.crossing().start()

    def merge(self):
        self.crossing().wait_recv()

        def body(k):
            self.part[k] = (self.part[k].astype(F32) + self.terms[k, self.ring.c].astype(F32)).astype(BF16)

        loop(8, body)
        self.crossing().wait_send()

    def steps(self):
        return [self.cross, lambda: (self.merge(), self.begin()), self.opposite, self.up, self.down, self.home, self.end]


def run_all(*actions):
    def run():
        for action in actions:
            action()

    return run


def when(condition, action):
    def run():
        action()

    pl.when(condition)(run)


def weave(*lists):
    for i in range(max(len(item) for item in lists)):
        for item in lists:
            if i < len(item):
                item[i]()


def rope(v, cosine, sine):
    return v * cosine + pltpu.roll(v, 64, 1) * sine


def rope_back(g, cosine, sine):
    return g * cosine + pltpu.roll(g * sine, 64, 1)


def inverse(v):
    return lax.rsqrt(jnp.mean(v * v, axis=-1, keepdims=True) + EPS)


def norm_back(v, gain, grad):
    r = inverse(v)
    n = v * r
    scaled = grad * gain
    return grad * n, r * (scaled - n * jnp.mean(scaled * n, axis=-1, keepdims=True))


def split3(v):
    a = (-v).astype(BF16).astype(F32)
    rest = -v - a
    b = rest.astype(BF16).astype(F32)
    lane = lax.broadcasted_iota(jnp.int32, v.shape, 1)
    return jnp.where(lane == 0, a, jnp.where(lane == 1, b, jnp.where(lane == 2, rest - b, 0.0)))


def begin_of(starts, index):
    begin = jnp.zeros_like(index)
    for k in range(1, 4):
        begin = jnp.where(index >= starts[k], starts[k], begin)
    return begin


def pick(index, values):
    out = jnp.int32(values[-1])
    for k in range(len(values) - 2, -1, -1):
        out = jnp.where(index == k, jnp.int32(values[k]), out)
    return out


def layer_kernel(
    starts, tok, dy, wcat, gain1, gain2, qgain, kgain, cosine, sine,
    layer_out, tokens_grad, query_out, key_out, value_out, output_out, gate_out, up_out, down_out,
    first_out, second_out, qn_out, kn_out, saved,
    weights, block_a, block_b, block_dy, kv, qs, qsend, qraw, kraw, accum, ctx, ctxb, qx, qfar, middle,
    part, bufs, ffpart, ffbufs, acts, grad_all, grad_far, dox, wpart, wboth, wbufs, vpart, vboth, vbufs,
    xs, kvboth, kvbufs, dqsend, dqhome, gvec, gin, gstage, gin2,
    hs, hr, ws, wr, wcs, wcr, ks, kr, kcs, kcr, ds_, dr_, ms, mr, rs1, rr1, gs1, gr1, rs2, rr2, gs2, gr2, rs3, rr3,
    fs, fr, vs, vr, vcs, vcr, qs_s, qr_r, qcs, qcr, xss, xrr, xcs, xcr, g1s, g1r, g2s, g2r, local,
):
    head, blk = HeadRing(), BlkRing()
    block = blk.b

    def halves(make):
        first, second = make(0), make(1)
        return [functools.partial(lambda f, s: (f(), s()), f, s) for f, s in zip(first.steps(), second.steps())]

    x = tok[...].astype(F32)
    block_a[chunk(head.slot(0, 0), 128), :] = (x * inverse(x) * gain1[...]).astype(BF16)
    weights[chunk(blk.slot(0, 0), 64), :] = wcat[...]
    block_dy[chunk(head.slot(0, 0), 128), :] = dy[...]
    barrier(head.peers() + blk.peers())
    wgather = Gather(blk, weights, 64, ws, wr, (wcs, wcr))
    weave(halves(lambda q: Gather(head, block_a, 64, hs, hr, off=64 * q, stride=128, k0=8 * q)), wgather.steps())

    keep = pltpu.make_async_copy(block_a, saved, local.at[0])
    keep.start()
    base = pl.multiple_of(block * 1024, 1024)

    def keys_rows(i):
        at = chunk(i, 256)
        out = nn(block_a[at, :], weights[:, KC:OC])
        v = out[:, 0:128]
        kraw[at, :] = v
        to = pl.ds(pl.multiple_of(base + i * 256, 256), 256)
        kv[to, 0:128] = rope(v * inverse(v) * kgain[...], cosine[at, :], sine[at, :]).astype(BF16)
        kv[to, 128:256] = out[:, 128:256].astype(BF16)

    loop(4, keys_rows)
    kvgather = Gather(blk, kv, 1024, ks, kr, (kcs, kcr))
    kvgather.begin()

    def query_rows(half, dst):
        for i in range(2):
            at = slice(512 * half + 256 * i, 512 * half + 256 * i + 256)
            out = nn(block_a[at, :], weights[:, QC:KC])
            for k in range(2):
                v = out[:, 128 * k : 128 * k + 128]
                qraw[at, 128 * k : 128 * k + 128] = v
                v = rope(v * inverse(v) * qgain[...], cosine[at, :], sine[at, :]) * (SCALE * LOG2E)
                dst[512 * k + 256 * i : 512 * k + 256 * i + 256, :] = v.astype(BF16)

    query_rows(1, qsend)
    qswap = remote(qsend, qs.at[1], ms.at[0], mr.at[0], blk.mirror())
    qswap.start()
    dygather = Gather(head, block_dy, 128, ds_, dr_)
    dygather.begin()
    query_rows(0, qs.at[0])

    def clear(i):
        accum[i] = jnp.zeros((1024, 256), F32)

    loop(4, clear)
    ones = jnp.ones((1024, 128), BF16)

    def limit_of(side):
        return jnp.where(side == 0, block, 15 - block)

    def half_of(side):
        return jnp.where(side == 0, 2 * block, 31 - 2 * block)

    def mask(side, jb, c, rows, transposed):
        first = half_of(side) * 512 + lax.rem(c * rows, 512)
        shape_q, shape_k = ((1, rows), (1024, 1)) if transposed else ((rows, 1), (1, 1024))
        qi = first + lax.broadcasted_iota(jnp.int32, shape_q, 1 if transposed else 0)
        ki = jb * 1024 + lax.broadcasted_iota(jnp.int32, shape_k, 0 if transposed else 1)
        return (ki >= begin_of(starts, qi)) & (ki <= qi)

    def attend(side, jb, masked):
        at = chunk(jb, 1024)
        keys = kv[at, 0:128]
        values = jnp.concatenate([kv[at, 128:256], ones], axis=1)
        row = 2 * side + masked
        for c in range(4):
            rows = slice(c * 256, c * 256 + 256)
            p = jnp.exp2(nt(qs[side, rows, :], keys))
            if masked:
                p = jnp.where(mask(side, jb, c, 256, False), p, 0.0)
            accum[row, rows, :] += nn(p.astype(BF16), values)

    planes = (1, 2)
    del planes
    forward_order = ((0, 0), (0, -1), (0, 1), (1, 0), (0, 2), (1, -1), (1, 1), (1, 2))
    at_step = {
        1: lambda: kvgather.crossed(0),
        2: lambda: qswap.wait_recv(),
        4: kvgather.step1,
        6: lambda: (kvgather.crossed(2), dygather.step1()),
        10: lambda: (kvgather.crossed(3), dygather.step2()),
        12: kvgather.step2,
        14: lambda: kvgather.crossed(1),
        18: lambda: kvgather.crossed(4),
        20: lambda: (kvgather.wait(3, 4), kvgather.cross(5, 6)),
        22: lambda: kvgather.crossed(5),
        26: lambda: kvgather.crossed(6),
        28: lambda: (kvgather.wait(7), kvgather.cross(7)),
        30: lambda: kvgather.crossed(7),
    }

    def attend_step(u):
        side = jnp.where(u < 4, lax.div(u, 2), lax.rem(u, 2))
        t = jnp.where(u < 4, lax.rem(u, 2), lax.div(u, 2))
        s, core = lax.div(t, 2), lax.rem(t, 2)
        jb = blk.slot(pick(s, [d[0] for d in forward_order]), pick(s, [d[1] for d in forward_order]), core)
        for k, action in at_step.items():
            when(u == k, action)
        limit = limit_of(side)
        careful = (jb == 0) | (jb == limit)
        when((jb <= limit) & jnp.logical_not(careful), lambda: attend(side, jb, False))
        when((jb <= limit) & careful, lambda: attend(side, jb, True))

    loop(32, attend_step)

    def context_of(side, dst):
        for k in range(2):
            rows = slice(512 * k, 512 * k + 512)
            qi = half_of(side) * 512 + lax.broadcasted_iota(jnp.int32, (512, 1), 0)
            here = qi < starts[2]
            both = accum[2 * side + 1, rows, :] + jnp.where(here, accum[2 * side, rows, :], 0.0)
            dst[:, 128 * k : 128 * k + 128] = (both[:, 0:128] / both[:, 128:256]).astype(BF16)
            accum[2 * side, rows, 0:128] = both[:, 128:256]

    def extend(side):
        for k in range(2):
            rows = slice(512 * k, 512 * k + 512)
            terms = split3(jnp.log2(accum[2 * side, rows, 0:128]))
            qi = half_of(side) * 512 + lax.broadcasted_iota(jnp.int32, (512, 128), 0)
            lane = lax.broadcasted_iota(jnp.int32, (512, 128), 1)
            gone = jnp.where(lane == 0, -1e30, 0.0)
            qx[side, rows, 0:128] = qs[side, rows, :]
            qx[side, rows, 128:256] = terms.astype(BF16)
            qfar[side, rows, 0:128] = qs[side, rows, :]
            qfar[side, rows, 128:256] = jnp.where(qi < starts[2], terms, gone).astype(BF16)

    context_of(1, ctxb)
    cswap = remote(ctxb, ctx.at[pl.ds(512, 512)], ms.at[1], mr.at[1], blk.mirror())
    cswap.start()
    context_of(0, ctx.at[pl.ds(0, 512)])
    dygather.step3()
    extend(1)
    extend(0)
    cswap.wait_recv()

    far, near = (1 - head.p) * 512, head.p * 512

    def output_rows(base, i):
        at = pl.ds(pl.multiple_of(base + i * 256, 256), 256)
        out = nt(ctx[at, :], weights[:, OC:GC]).astype(BF16)
        first = lax.div(base, 128) + 2 * i
        part[first] = out[0:128]
        part[first + 1] = out[128:256]

    loop(2, lambda i: output_rows(far, i))
    steps = halves(lambda q: Scatter(head, part, bufs, rs1, rr1, off=64 * q, n=64, k0=8 * q))
    steps[0]()
    loop(2, lambda i: output_rows(near, i))
    for step in steps[1:]:
        step()
    reduced = Scatter(head, part, bufs, rs1, rr1)
    mid = x + reduced.total()
    middle[...] = mid
    block_b[chunk(head.slot(0, 0), 128), :] = (mid * inverse(mid) * gain2[...]).astype(BF16)
    steps = halves(lambda q: Gather(head, block_b, 64, gs1, gr1, off=64 * q, stride=128, k0=8 * q))
    steps[0]()
    qswap.wait_send()
    cswap.wait_send()
    kvgather.end()
    dygather.end()
    keep.wait()
    steps[1]()
    steps[2]()

    def forward_rows(base, i):
        at = pl.ds(pl.multiple_of(base + i * 256, 256), 256)
        both = nn(block_b[at, :], weights[:, GC:DC])
        gate, upper = both[:, 0:384], both[:, 384:768]
        sigma = 1.0 / (1.0 + jnp.exp(-gate))
        silu = gate * sigma
        act_grad = nn(block_dy[at, :], weights[:, DC:END])
        gate_low = (act_grad * upper * sigma * (1.0 + gate * (1.0 - sigma))).astype(BF16)
        low = jnp.concatenate([gate_low, (act_grad * silu).astype(BF16)], axis=1)
        acts[at, 0:768] = low
        acts[at, 768:1152] = (silu * upper).astype(BF16)
        out = nt(low, weights[:, GC:DC]).astype(BF16)
        first = lax.div(base, 128) + 2 * i
        part[first] = out[0:128]
        part[first + 1] = out[128:256]

    loop(2, lambda i: forward_rows(near, i))
    for step in steps[3:]:
        step()
    loop(2, lambda i: forward_rows(far, i))
    steps = halves(lambda q: Scatter(head, part, bufs, rs2, rr2, off=64 * q, n=64, k0=8 * q))
    steps[0]()

    def down_rows(i):
        out = nt(acts[chunk(i, 256), 768:1152], weights[:, DC:END]).astype(BF16)
        ffpart[2 * i] = out[0:128]
        ffpart[2 * i + 1] = out[128:256]

    loop(4, down_rows)
    steps[1]()

    def put_terms(i, out, cols):
        for k in range(2):
            wpart[2 * i + k, 0, :, cols] = out[128 * k : 128 * k + 64]
            wpart[2 * i + k, 1, :, cols] = out[128 * k + 64 : 128 * k + 128]

    def gate_up_grads(i):
        put_terms(i, tn(block_b[:, chunk(i, 256)], acts[:, 0:768]).astype(BF16), slice(256, 1024))

    loop(2, gate_up_grads)
    steps[2]()
    steps[3]()
    steps[4]()
    loop(2, lambda i: gate_up_grads(i + 2))
    steps[5]()
    reduced = Scatter(head, part, bufs, rs2, rr2)
    gain_terms, part_grad = norm_back(middle[...], gain2[...], reduced.total())
    mid_grad = dy[...].astype(F32) + part_grad
    block_a[chunk(head.slot(0, 0), 128), :] = mid_grad.astype(BF16)
    steps = halves(lambda q: Gather(head, block_a, 64, gs2, gr2, off=64 * q, stride=128, k0=8 * q))
    steps[0]()
    gvec[:, 1024:2048] = jnp.sum(gain_terms, axis=0, keepdims=True)

    def down_grads(i):
        put_terms(i, tn(block_dy[:, chunk(i, 256)], acts[:, 768:1152]).astype(BF16), slice(1024, 1408))

    loop(2, down_grads)
    steps[1]()
    steps[2]()
    loop(2, lambda i: down_grads(i + 2))
    for step in steps[3:]:
        step()

    def context_grads(i):
        at = chunk(i, 256)
        grad_all[at, :] = nn(block_a[at, :], weights[:, OC:GC]).astype(BF16)

    loop(2, lambda i: context_grads(i + 2))
    gswap = remote(grad_all.at[pl.ds(512, 512)], grad_far, ms.at[2], mr.at[2], blk.mirror())
    gswap.start()
    loop(2, context_grads)

    def output_grads(i):
        put_terms(i, tn(block_a[:, chunk(i, 256)], ctx[...]).astype(BF16), slice(0, 256))

    loop(4, output_grads)
    reload = pltpu.make_async_copy(saved, block_b, local.at[1])
    reload.start()
    ffscatter = Scatter(head, ffpart, ffbufs, fs, fr)
    wscatter = BlkScatter(blk, wpart, wboth, wbufs, vs, vr, vcs.at[0], vcr.at[0])
    ffscatter.begin()
    wscatter.cross()

    def extend_grad(side, grads, context):
        for k in range(2):
            rows, cols = slice(512 * k, 512 * k + 512), slice(128 * k, 128 * k + 128)
            grad = grads[0:512, cols]
            delta = jnp.sum(grad.astype(F32) * context[0:512, cols].astype(F32), axis=1, keepdims=True)
            dox[side, rows, 0:128] = grad
            dox[side, rows, 128:256] = split3(jnp.broadcast_to(delta, (512, 128))).astype(BF16)

    extend_grad(0, grad_all, ctx)
    loop(2, lambda i: clear(i))
    gswap.wait_recv()
    extend_grad(1, grad_far, ctxb)

    back_order = ((1, 2), (1, 1), (1, -1), (0, 2), (1, 0), (0, 1), (0, -1), (0, 0))

    def attend_back(side, jb, masked):
        at = chunk(jb, 1024)
        keys = kv[at, 0:128]
        kx = jnp.concatenate([keys, ones], axis=1)
        vx = jnp.concatenate([kv[at, 128:256], ones], axis=1)
        source = qx if masked else qfar
        cols = pl.ds(pl.multiple_of(side * 128, 128), 128)
        for c in range(4):
            rows = slice(c * 256, c * 256 + 256)
            p = jnp.exp2(nt(kx, source[side, rows, :]))
            if masked:
                p = jnp.where(mask(side, jb, c, 256, True), p, 0.0)
            ds = (p * nt(vx, dox[side, rows, :])).astype(BF16)
            accum[0, :, 0:128] += nn(ds, source[side, rows, 0:128])
            accum[0, :, 128:256] += nn(p.astype(BF16), dox[side, rows, 0:128])
            accum[1, rows, cols] += tn(ds, keys)

    kvscatter = Scatter(blk, kvboth, kvbufs, xss, xrr)

    def crossing(s, which):
        dst = kvboth.at[which]
        return remote(xs.at[s % 2], dst, xcs.at[s], xcr.at[s], blk.sibling())

    actions = (
        lambda: kvscatter.send(0),
        lambda: kvscatter.send(1),
        lambda: kvscatter.send(2),
        kvscatter.opposite,
        kvscatter.home,
        kvscatter.up,
        kvscatter.down,
        lambda: None,
    )
    others = {
        0: lambda: (wscatter.merge(), wscatter.begin()),
        2: lambda: (wscatter.opposite(), ffscatter.opposite()),
        4: lambda: (wscatter.up(), wscatter.down(), wscatter.home(), ffscatter.up(), ffscatter.down(), ffscatter.home()),
        6: lambda: (wscatter.end(), ffscatter.end()),
    }

    def back_step(t):
        s, core = lax.div(t, 2), 1 - lax.rem(t, 2)
        plane = blk.plane(pick(s, [d[0] for d in back_order]), pick(s, [d[1] for d in back_order]))
        jb = plane * 2 + lax.rem(blk.c + core, 2)
        accum[0] = jnp.zeros((1024, 256), F32)

        def one(side):
            limit = limit_of(side)
            careful = (jb == 0) | (jb == limit)
            when((jb <= limit) & jnp.logical_not(careful), lambda: attend_back(side, jb, False))
            when((jb <= limit) & careful, lambda: attend_back(side, jb, True))

        loop(2, one)
        for k in range(8):
            which = blk.plane(*back_order[k])

            def out(k=k, which=which):
                if k >= 2:
                    crossing(k - 2, blk.plane(*back_order[k - 2])).wait_send()
                xs[k % 2] = accum[0].astype(BF16)
                crossing(k, which).start()
                if k in others:
                    others[k]()

            def merge(k=k, which=which):
                crossing(k, which).wait_recv()
                kvboth[which] = (kvboth[which].astype(F32) + accum[0]).astype(BF16)
                actions[k]()

            when(t == 2 * k, out)
            when(t == 2 * k + 1, merge)

    loop(16, back_step)
    for k in (6, 7):
        crossing(k, blk.plane(*back_order[k])).wait_send()

    for k in range(2):
        dqsend[:, 128 * k : 128 * k + 128] = (accum[1, 512 * k : 512 * k + 512, 128:256] * SCALE).astype(BF16)
    dswap = remote(dqsend, dqhome, ms.at[3], mr.at[3], blk.mirror())
    dswap.start()
    reload.wait()
    gswap.wait_send()
    gvec[:, 2048:2304] = jnp.zeros((1, 256), F32)

    def back(raw, grad, at, gains):
        return norm_back(raw, gains, rope_back(grad, cosine[at, :], sine[at, :]))

    def query_back(i, grads):
        at = slice(256 * i, 256 * i + 256)
        for k in range(2):
            cols = slice(128 * k, 128 * k + 128)
            terms, out = back(qraw[at, cols], grads(i, k), at, qgain[...])
            acts[at, cols] = out.astype(BF16)
            gvec[:, 2048:2176] += jnp.sum(terms, axis=0, keepdims=True)

    for i in range(2):
        query_back(i, lambda i, k: accum[1, 512 * k + 256 * i : 512 * k + 256 * i + 256, 0:128] * SCALE)
    layer_out[...] = (middle[...] + ffscatter.total()).astype(BF16)
    wsum = wscatter.total()
    output_out[...] = jnp.transpose(wsum[:, 0:256])
    gate_out[...] = wsum[:, 256:640]
    up_out[...] = wsum[:, 640:1024]
    down_out[...] = jnp.transpose(wsum[:, 1024:1408])
    dswap.wait_recv()
    for i in range(2, 4):
        query_back(i, lambda i, k: dqhome[256 * (i - 2) : 256 * (i - 2) + 256, 128 * k : 128 * k + 128].astype(F32))
    kvscatter.end()
    kvsum = kvscatter
    accum[2] = kvsum.total()

    def key_back(i):
        at = slice(256 * i, 256 * i + 256)
        terms, out = back(kraw[at, :], accum[2, at, 0:128] * LN2, at, kgain[...])
        acts[at, 256:384] = out.astype(BF16)
        gvec[:, 2176:2304] += jnp.sum(terms, axis=0, keepdims=True)
        acts[at, 384:512] = accum[2, at, 128:256].astype(BF16)

    for i in range(4):
        key_back(i)
    dswap.wait_send()

    def input_rows(base, i):
        at = pl.ds(pl.multiple_of(base + i * 256, 256), 256)
        out = nt(acts[at, 0:512], weights[:, QC:OC]).astype(BF16)
        first = lax.div(base, 128) + 2 * i
        part[first] = out[0:128]
        part[first + 1] = out[128:256]

    loop(2, lambda i: input_rows(far, i))
    steps = halves(lambda q: Scatter(head, part, bufs, rs3, rr3, off=64 * q, n=64, k0=8 * q))
    steps[0]()

    def project_grads(i):
        out = tn(block_b[:, chunk(i, 256)], acts[:, 0:512]).astype(BF16)
        for k in range(2):
            vpart[2 * i + k, 0] = out[128 * k : 128 * k + 64]
            vpart[2 * i + k, 1] = out[128 * k + 64 : 128 * k + 128]

    loop(2, lambda i: input_rows(near, i))
    loop(4, project_grads)
    vscatter = BlkScatter(blk, vpart, vboth, vbufs, qs_s, qr_r, qcs.at[0], qcr.at[0])
    weave(vscatter.steps(), steps[1:])
    reduced = Scatter(head, part, bufs, rs3, rr3)
    terms, input_part = norm_back(x, gain1[...], reduced.total())
    gvec[:, 0:1024] = jnp.sum(terms, axis=0, keepdims=True)

    first = [remote(gvec, gin.at[i], g1s.at[i], g1r.at[i], d) for i, d in enumerate(head.peers())]
    for copy in first:
        copy.start()
    again = middle[...]
    del again
    tokens_grad[...] = (mid_grad + input_part).astype(BF16)
    vsum = vscatter.total()
    query_out[...] = vsum[:, 0:256]
    key_out[...] = vsum[:, 256:384]
    value_out[...] = vsum[:, 384:512]
    for copy in first:
        copy.wait()
    summed = gvec[...]
    for i in range(7):
        summed = summed + gin[i]
    for k in range(8):
        gstage[k, :, 0:128] = summed[:, 128 * k : 128 * k + 128]
        gstage[k, :, 128:256] = summed[:, 1024 + 128 * k : 1152 + 128 * k]
        gstage[k, :, 256:512] = summed[:, 2048:2304]
    every = [(dp, dr, dc) for dp in range(2) for dr in range(4) for dc in range(2)][1:]
    second = [
        remote(gstage.at[blk.plane(d[0], d[1])], gin2.at[i], g2s.at[i], g2r.at[i], blk.dev(*d))
        for i, d in enumerate(every)
    ]
    for copy in second:
        copy.start()
    for copy in second:
        copy.wait()
    out = gstage[blk.plane(0, 0)]
    for i in range(15):
        out = out + gin2[i]
    offset = blk.c * 64 + head.h * 8
    lane = block * 8 + head.h
    first_out[...] = pltpu.roll(out[:, 0:128], lax.rem(128 - offset, 128), 1)[:, 0:8]
    second_out[...] = pltpu.roll(out[:, 128:256], lax.rem(128 - offset, 128), 1)[:, 0:8]
    qn_out[...] = pltpu.roll(out[:, 256:384], lax.rem(128 - lane, 128), 1)[:, 0:1]
    kn_out[...] = pltpu.roll(out[:, 384:512], lax.rem(128 - lane, 128), 1)[:, 0:1]


def sems(*counts):
    return [pltpu.SemaphoreType.DMA((c,)) for c in counts]


def per_device(
    tokens, doc_starts, first_gain, query_weight, key_matrix, value_matrix, querynorm, keynorm,
    output_weight, second_gain, gate_weight, up_weight, down_weight, grad_out,
):
    index = lax.axis_index("blk") * 1024 + jnp.arange(1024, dtype=jnp.int32)
    begin = jnp.max(jnp.where(doc_starts[None, :] <= index[:, None], doc_starts[None, :], 0), axis=1)
    position = (index - begin).astype(F32)
    freqs = THETA ** (-(jnp.arange(64, dtype=F32) * 2.0 / HEAD_DIM))
    angle = position[:, None] * freqs[None, :]
    cosine, sine = jnp.cos(angle), jnp.sin(angle)
    cosine = jnp.concatenate([cosine, cosine], axis=1)
    sine = jnp.concatenate([-sine, sine], axis=1)
    wcat = jnp.concatenate(
        [query_weight, key_matrix, value_matrix, output_weight.T, gate_weight, up_weight, down_weight.T], axis=1
    )
    vm = pl.BlockSpec(memory_space=pltpu.VMEM)
    outs = [
        ((128, 1024), BF16), ((128, 1024), BF16), ((64, 256), F32), ((64, 128), F32), ((64, 128), F32),
        ((256, 64), F32), ((64, 384), F32), ((64, 384), F32), ((384, 64), F32),
        ((1, 8), F32), ((1, 8), F32), ((1, 1), F32), ((1, 1), F32), ((1024, 1024), BF16),
    ]
    scratch = [
        ((1024, 1920), BF16), ((1024, 1024), BF16), ((1024, 1024), BF16), ((1024, 1024), BF16), ((16384, 256), BF16),
        ((2, 1024, 128), BF16), ((1024, 128), BF16), ((1024, 256), F32), ((1024, 128), F32), ((4, 1024, 256), F32),
        ((1024, 256), BF16), ((512, 256), BF16), ((2, 1024, 256), BF16), ((2, 1024, 256), BF16), ((128, 1024), F32),
        ((8, 128, 1024), BF16), ((7, 128, 1024), BF16), ((8, 128, 1024), BF16), ((7, 128, 1024), BF16),
        ((1024, 1152), BF16), ((1024, 256), BF16), ((512, 256), BF16), ((2, 1024, 256), BF16),
        ((8, 2, 64, 1408), BF16), ((8, 64, 1408), BF16), ((7, 64, 1408), BF16),
        ((8, 2, 64, 512), BF16), ((8, 64, 512), BF16), ((7, 64, 512), BF16),
        ((2, 1024, 256), BF16), ((8, 1024, 256), BF16), ((7, 1024, 256), BF16), ((512, 256), BF16), ((512, 256), BF16),
        ((1, 2304), F32), ((7, 1, 2304), F32), ((8, 1, 512), F32), ((15, 1, 512), F32),
    ]
    counts = (16, 16, 8, 8, 8, 8, 8, 8, 8, 8, 8, 8, 4, 4) + (16,) * 10 + (8, 8, 8, 8, 1, 1, 8, 8, 1, 1, 8, 8, 8, 8, 7, 7, 15, 15, 2)
    out = pl.pallas_call(
        layer_kernel,
        out_shape=[jax.ShapeDtypeStruct(s, d) for s, d in outs],
        in_specs=[pl.BlockSpec(memory_space=pltpu.SMEM)] + [vm] * 9,
        out_specs=[vm] * 13 + [pl.BlockSpec(memory_space=pl.ANY)],
        scratch_shapes=[pltpu.VMEM(s, d) for s, d in scratch] + sems(*counts),
        compiler_params=pltpu.CompilerParams(vmem_limit_bytes=VMEM_LIMIT, collective_id=1, has_side_effects=True),
    )(
        doc_starts, tokens, grad_out, wcat, first_gain.astype(F32)[None, :], second_gain.astype(F32)[None, :],
        querynorm.astype(F32)[None, :], keynorm.astype(F32)[None, :], cosine, sine,
    )
    layer_out, tokens_grad, query, key, value, output, gate, up, down, first, second, qn, kn, _ = out
    return (
        layer_out, tokens_grad, first.reshape(8), query, key, value, qn.reshape(1), kn.reshape(1),
        output, second.reshape(8), gate, up, down,
    )


def solution(mesh):
    return jax.shard_map(
        per_device,
        mesh=mesh,
        in_specs=(
            P(("blk", "head"), None),
            P(),
            P(),
            P("blk", "head"),
            P("blk", "head"),
            P("blk", "head"),
            P(),
            P(),
            P("head", "blk"),
            P(),
            P("blk", "head"),
            P("blk", "head"),
            P("head", "blk"),
            P(("blk", "head"), None),
        ),
        out_specs=(
            P(("blk", "head"), None),
            P(("blk", "head"), None),
            P(("blk", "head")),
            P("blk", "head"),
            P("blk", "head"),
            P("blk", "head"),
            P(("blk", "head")),
            P(("blk", "head")),
            P("head", "blk"),
            P(("blk", "head")),
            P("blk", "head"),
            P("blk", "head"),
            P("head", "blk"),
        ),
        check_vma=False,
    )
```

```python
import functools

import jax
import jax.numpy as jnp
from jax import lax
from jax.experimental import pallas as pl
from jax.experimental.pallas import tpu as pltpu
import numpy as np
from jax.sharding import PartitionSpec as P

EPS = 1e-06
THETA = 1000000.0
MESH = pl.DeviceIdType.MESH
F32 = jnp.float32
BF16 = jnp.bfloat16
LOG2E = 1.4426950408889634
LN2 = 0.6931471805599453
HEAD_DIM = 128
SCALE = HEAD_DIM**-0.5
VMEM_LIMIT = 64 * 2**20 - 2**16

QC, KC, VC, OC, GC, UC, DC, END = 0, 256, 384, 512, 768, 1152, 1536, 1920


def nn(a, b):
    return jnp.dot(a, b, preferred_element_type=F32)


def nt(a, b):
    return lax.dot_general(a, b, (((1,), (1,)), ((), ())), preferred_element_type=F32)


def tn(a, b):
    return lax.dot_general(a, b, (((0,), (0,)), ((), ())), preferred_element_type=F32)


def chunk(i, size):
    return pl.ds(pl.multiple_of(i * size, size), size)


def loop(count, body):
    def step(i, carry):
        body(i)
        return carry

    lax.fori_loop(0, count, step, 0)


def run_all(*actions):
    def run():
        for action in actions:
            action()

    return run


def when(condition, action):
    def run():
        action()

    pl.when(condition)(run)


class HeadRing:
    def __init__(self):
        self.b = lax.axis_index("blk")
        h = lax.axis_index("head")
        self.h = h
        self.p, self.r = lax.div(h, 4), lax.rem(h, 4)

    def plane(self, dp, dr):
        return lax.rem(self.p + dp, 2) * 4 + lax.rem(self.r + dr + 4, 4)

    slot = plane

    def dev(self, dp, dr):
        return (self.b, self.plane(dp, dr))

    def peers(self):
        return [self.dev(dp, dr) for dp in range(2) for dr in range(4) if (dp, dr) != (0, 0)]


class BlkRing:
    def __init__(self):
        b = lax.axis_index("blk")
        self.h = lax.axis_index("head")
        self.b = b
        self.p, self.r, self.c = lax.div(b, 8), lax.rem(lax.div(b, 2), 4), lax.rem(b, 2)

    def plane(self, dp, dr):
        return lax.rem(self.p + dp, 2) * 4 + lax.rem(self.r + dr + 4, 4)

    def slot(self, dp, dr, dc=0):
        return self.plane(dp, dr) * 2 + lax.rem(self.c + dc, 2)

    def dev(self, dp, dr, dc=0):
        return (self.slot(dp, dr, dc), self.h)

    def sibling(self):
        return self.dev(0, 0, 1)

    def mirror(self):
        return (15 - self.b, self.h)

    def peers(self):
        every = [(dp, dr, dc) for dp in range(2) for dr in range(4) for dc in range(2)]
        return [self.dev(*d) for d in every if d != (0, 0, 0)]


def barrier(devices):
    sem = pltpu.get_barrier_semaphore()
    for d in devices:
        pl.semaphore_signal(sem, inc=1, device_id=d, device_id_type=MESH)
    pl.semaphore_wait(sem, len(devices))


def remote(src, dst, ss, rs, dev):
    return pltpu.make_async_remote_copy(
        src_ref=src, dst_ref=dst, send_sem=ss, recv_sem=rs, device_id=dev, device_id_type=MESH
    )


class Gather:
    ORDER = ((0, 0), (1, 0), (0, -1), (0, 1), (0, 2), (1, -1), (1, 1), (1, 2))

    def __init__(self, ring, full, n, ss, rs, sib=None, on_ring=False, off=0, stride=None, k0=0):
        self.ring, self.full, self.n, self.ss, self.rs, self.sib = ring, full, n, ss, rs, sib
        self.on_ring, self.off, self.stride, self.k0 = on_ring, off, stride or n, k0
        self.last = (11, 12) if on_ring else (9, 10)

    def rows(self, dp, dr, part=None):
        base = self.ring.slot(dp, dr) * self.stride + self.off
        size = self.n
        if part is not None:
            size = self.n // 2
            base = base + part * size
        return self.full.at[pl.ds(pl.multiple_of(base, size), size)]

    def copy(self, k):
        ring, rows = self.ring, self.rows
        ref, dev = (
            lambda: (rows(0, 0), ring.dev(1, 0)),
            lambda: (rows(0, 0, 0), ring.dev(0, 1)),
            lambda: (rows(0, 0, 1), ring.dev(0, -1)),
            lambda: (rows(0, 0, 1), ring.dev(0, 1)),
            lambda: (rows(0, 0, 0), ring.dev(0, -1)),
            lambda: (rows(0, -1, 0), ring.dev(0, 1)),
            lambda: (rows(0, 1, 1), ring.dev(0, -1)),
            lambda: (rows(1, 0), ring.dev(0, 1)),
            lambda: (rows(1, 0), ring.dev(0, -1)),
            lambda: (rows(0, 2, 0), ring.dev(1, 0)),
            lambda: (rows(0, 2, 1), ring.dev(1, 0)),
            lambda: (rows(1, -1, 0), ring.dev(0, 1)),
            lambda: (rows(1, 1, 1), ring.dev(0, -1)),
        )[k]()
        return remote(ref, ref, self.ss.at[self.k0 + k], self.rs.at[self.k0 + k], dev)

    def send(self, *ks):
        for k in ks:
            self.copy(k).start()

    def wait(self, *ks):
        for k in ks:
            self.copy(k).wait_recv()

    def crossing(self, dp, dr):
        k = self.ORDER.index((dp, dr))
        ref = self.rows(dp, dr)
        return remote(ref, ref, self.sib[0].at[k], self.sib[1].at[k], self.ring.sibling())

    def cross(self, *which):
        if self.sib is not None:
            for w in which:
                self.crossing(*w).start()

    def crossed(self, *which):
        if self.sib is not None:
            for w in which:
                self.crossing(*w).wait_recv()

    def begin(self):
        self.send(1, 2, 0, 3, 4)
        self.cross((0, 0))

    def travel(self):
        self.wait(1)
        self.send(5)
        self.wait(2)
        self.send(6)

    def pair_on(self):
        self.wait(0)
        self.send(7, 8)
        self.cross((1, 0))

    def step1(self):
        self.travel()
        self.pair_on()

    def opposite_on(self):
        self.wait(5)
        if not self.on_ring:
            self.send(9)
        self.wait(6)
        if not self.on_ring:
            self.send(10)
        self.cross((0, 2))

    def ring_done(self):
        self.wait(3, 4)
        self.cross((0, -1), (0, 1))

    def step2(self):
        self.opposite_on()
        self.ring_done()

    def step3(self):
        self.wait(7)
        if self.on_ring:
            self.send(11)
        self.wait(8)
        if self.on_ring:
            self.send(12)
        self.cross((1, -1), (1, 1))

    def step4(self):
        self.wait(*self.last)
        self.cross((1, 2))

    def end(self):
        for k in tuple(range(9)) + self.last:
            self.copy(k).wait_send()
        if self.sib is not None:
            for w in self.ORDER:
                self.crossing(*w).wait_send()

    def finish(self):
        self.crossed(*self.ORDER)
        self.end()

    def steps(self):
        return [self.begin, self.step1, self.step2, self.step3, self.step4, self.finish]


class Scatter:
    def __init__(self, ring, part, bufs, ss, rs, off=0, n=None, k0=0):
        self.ring, self.part, self.bufs, self.ss, self.rs = ring, part, bufs, ss, rs
        self.off, self.n, self.k0 = off, n or part.shape[1], k0

    def span(self, half):
        if half is None:
            return pl.ds(self.off, self.n)
        return pl.ds(self.off + half * (self.n // 2), self.n // 2)

    def own(self, dp, dr, half=None):
        return self.part.at[self.ring.plane(dp, dr), self.span(half)]

    def buf(self, i, half=None):
        return self.bufs.at[i, self.span(half)]

    def copy(self, k):
        ring, own, buf = self.ring, self.own, self.buf
        src, dst, dev = (
            lambda: (own(1, 2), buf(0), ring.dev(1, 0)),
            lambda: (own(1, 1), buf(1), ring.dev(0, 1)),
            lambda: (own(1, -1), buf(2), ring.dev(0, -1)),
            lambda: (own(0, 2, 0), buf(6, 0), ring.dev(0, 1)),
            lambda: (own(0, 2, 1), buf(6, 1), ring.dev(0, -1)),
            lambda: (own(1, 0), buf(3), ring.dev(1, 0)),
            lambda: (own(0, 1), buf(4), ring.dev(0, 1)),
            lambda: (own(0, -1), buf(5), ring.dev(0, -1)),
        )[k]()
        return remote(src, dst, self.ss.at[self.k0 + k], self.rs.at[self.k0 + k], dev)

    def send(self, *ks):
        for k in ks:
            self.copy(k).start()

    def wait(self, *ks):
        for k in ks:
            self.copy(k).wait_recv()

    def add(self, dst, *srcs):
        value = dst[...].astype(F32)
        for src in srcs:
            value = value + src[...].astype(F32)
        dst[...] = value.astype(dst.dtype)

    def begin(self):
        self.send(1, 2, 0)

    def opposite(self):
        self.wait(0)
        self.add(self.own(0, 2), self.buf(0))
        self.send(3, 4)

    def home(self):
        self.wait(1, 2)
        self.add(self.own(1, 0), self.buf(1), self.buf(2))
        self.send(5)

    def up(self):
        self.wait(3)
        self.add(self.own(0, 1, 0), self.buf(6, 0))
        self.send(6)

    def down(self):
        self.wait(4)
        self.add(self.own(0, -1, 1), self.buf(6, 1))
        self.send(7)

    def end(self):
        self.wait(5, 6, 7)
        for k in range(8):
            self.copy(k).wait_send()

    def late(self):
        self.up()
        self.down()
        self.home()

    def total(self):
        out = self.own(0, 0)[...].astype(F32)
        for i in (3, 4, 5):
            out = out + self.buf(i)[...].astype(F32)
        return out


class BlkScatter(Scatter):
    def __init__(self, ring, terms, part, bufs, ss, rs, cs, cr):
        super().__init__(ring, part, bufs, ss, rs)
        self.terms, self.cs, self.cr = terms, cs, cr

    def crossing(self):
        return remote(self.terms.at[:, 1 - self.ring.c], self.part, self.cs, self.cr, self.ring.sibling())

    def cross(self):
        self.crossing().start()

    def merge(self):
        self.crossing().wait_recv()

        def body(k):
            self.part[k] = (self.part[k].astype(F32) + self.terms[k, self.ring.c].astype(F32)).astype(BF16)

        loop(8, body)
        self.crossing().wait_send()


def weave(*lists):
    for i in range(max(len(item) for item in lists)):
        for item in lists:
            if i < len(item):
                item[i]()


def rope(v, cosine, sine):
    return v * cosine + pltpu.roll(v, 64, 1) * sine


def rope_back(g, cosine, sine):
    return g * cosine + pltpu.roll(g * sine, 64, 1)


def inverse(v):
    return lax.rsqrt(jnp.mean(v * v, axis=-1, keepdims=True) + EPS)


def norm_back(v, gain, grad):
    r = inverse(v)
    n = v * r
    scaled = grad * gain
    return grad * n, r * (scaled - n * jnp.mean(scaled * n, axis=-1, keepdims=True))


def split3(v):
    a = (-v).astype(BF16).astype(F32)
    rest = -v - a
    b = rest.astype(BF16).astype(F32)
    lane = lax.broadcasted_iota(jnp.int32, v.shape, 1)
    return jnp.where(lane == 0, a, jnp.where(lane == 1, b, jnp.where(lane == 2, rest - b, 0.0)))


def begin_of(starts, index):
    begin = jnp.zeros_like(index)
    for k in range(1, 4):
        begin = jnp.where(index >= starts[k], starts[k], begin)
    return begin


def pick(index, values):
    out = jnp.int32(values[-1])
    for k in range(len(values) - 2, -1, -1):
        out = jnp.where(index == k, jnp.int32(values[k]), out)
    return out


def layer_kernel(
    starts, tok, dy, wq, wk, wv, wo, wg, wu, wd, gain_one, gain_two, gain_q, gain_k, freqs,
    layer_out, tokens_grad, query_out, key_out, value_out, output_out, gate_out, up_out, down_out,
    first_out, second_out, qn_out, kn_out, saved,
    cosine, sine, weights, block_a, block_b, block_dy, kv, qs, qsend, qraw, kraw, accum, ctx, ctxb, qx, qfar, middle,
    part, bufs, ffpart, ffbufs, acts, grad_all, grad_far, dox, wpart, wboth, wbufs, vpart, vboth, vbufs,
    xs, kvboth, kvbufs, dqsend, dqhome, gvec, gin, gstage, gin2,
    hs, hr, ws, wr, wcs, wcr, ks, kr, kcs, kcr, ds_, dr_, ms, mr, rs1, rr1, gs1, gr1, rs2, rr2, gs2, gr2, rs3, rr3,
    fs, fr, vs, vr, vcs, vcr, qs_s, qr_r, qcs, qcr, xss, xrr, xcs, xcr, g1s, g1r, g2s, g2r, local,
):
    head, blk = HeadRing(), BlkRing()
    block = blk.b

    def line(ref):
        value = ref[...].astype(F32)
        return jnp.concatenate([value[i : i + 1] for i in range(8)], axis=1)

    gain1, gain2 = line(gain_one), line(gain_two)
    qgain, kgain = gain_q[...].astype(F32), gain_k[...].astype(F32)
    x = tok[...].astype(F32)
    block_a[chunk(head.slot(0, 0), 128), :] = (x * inverse(x) * gain1).astype(BF16)
    mine = chunk(blk.slot(0, 0), 64)
    for ref, first in ((wq, QC), (wk, KC), (wv, VC), (wo, OC), (wg, GC), (wu, UC), (wd, DC)):
        weights[mine, first : first + ref.shape[1]] = ref[...]
    block_dy[chunk(head.slot(0, 0), 128), :] = dy[...]
    barrier(head.peers() + blk.peers())
    wgather = Gather(blk, weights, 64, ws, wr, (wcs, wcr), on_ring=True)
    first = Gather(head, block_a, 128, hs, hr).steps()
    first[0]()
    wgather.begin()
    for i in range(4):
        at = slice(256 * i, 256 * i + 256)
        index = block * 1024 + 256 * i + lax.broadcasted_iota(jnp.int32, (256, 1), 0)
        angle = (index - begin_of(starts, index)).astype(F32) * freqs[...]
        lane = lax.broadcasted_iota(jnp.int32, (256, 128), 1)
        cosine[at, :] = jnp.cos(angle)
        turn = jnp.sin(angle)
        sine[at, :] = jnp.where(lane < 64, -turn, turn)
    weave(first[1:], wgather.steps()[1:])

    keep = pltpu.make_async_copy(block_a, saved, local.at[0])
    keep.start()
    base = pl.multiple_of(block * 1024, 1024)
    far, near = pl.multiple_of((1 - head.p) * 512, 512), pl.multiple_of(head.p * 512, 512)

    def query_rows(base, dst):
        for i in range(2):
            at = pl.ds(pl.multiple_of(base + 256 * i, 256), 256)
            out = nn(block_a[at, :], weights[:, QC:KC])
            for k in range(2):
                v = out[:, 128 * k : 128 * k + 128]
                qraw[at, 128 * k : 128 * k + 128] = v
                v = rope(v * inverse(v) * qgain, cosine[at, :], sine[at, :]) * (SCALE * LOG2E)
                dst[512 * k + 256 * i : 512 * k + 256 * i + 256, :] = v.astype(BF16)

    query_rows(near, qsend)
    qswap = remote(qsend, qs.at[1], ms.at[0], mr.at[0], blk.mirror())
    qswap.start()

    def keys_rows(i):
        at = chunk(i, 256)
        out = nn(block_a[at, :], weights[:, KC:OC])
        v = out[:, 0:128]
        kraw[at, :] = v
        to = pl.ds(pl.multiple_of(base + i * 256, 256), 256)
        kv[to, 0:128] = rope(v * inverse(v) * kgain, cosine[at, :], sine[at, :]).astype(BF16)
        kv[to, 128:256] = out[:, 128:256].astype(BF16)

    loop(4, keys_rows)
    kvgather = Gather(blk, kv, 1024, ks, kr, (kcs, kcr))
    kvgather.send(1, 2, 0)
    kvgather.cross((0, 0))
    query_rows(far, qs.at[0])
    dygather = Gather(head, block_dy, 128, ds_, dr_, on_ring=True)
    dygather.begin()

    def clear(i):
        accum[i] = jnp.zeros((1024, 256), F32)

    loop(4, clear)
    ones = jnp.ones((1024, 128), BF16)

    def limit_of(side):
        return jnp.where(side == 0, block, 15 - block)

    def half_of(side):
        return jnp.where(side == 0, 2 * block + 1 - head.p, 30 - 2 * block + head.p)

    def mask(side, jb, c, rows, transposed):
        first = half_of(side) * 512 + lax.rem(c * rows, 512)
        shape_q, shape_k = ((1, rows), (1024, 1)) if transposed else ((rows, 1), (1, 1024))
        qi = first + lax.broadcasted_iota(jnp.int32, shape_q, 1 if transposed else 0)
        ki = jb * 1024 + lax.broadcasted_iota(jnp.int32, shape_k, 0 if transposed else 1)
        return (ki >= begin_of(starts, qi)) & (ki <= qi)

    def attend(side, jb, masked):
        at = chunk(jb, 1024)
        keys = kv[at, 0:128]
        values = jnp.concatenate([kv[at, 128:256], ones], axis=1)
        row = 2 * side + masked
        for c in range(4):
            rows = slice(c * 256, c * 256 + 256)
            p = jnp.exp2(nt(qs[side, rows, :], keys))
            if masked:
                p = jnp.where(mask(side, jb, c, 256, False), p, 0.0)
            accum[row, rows, :] += nn(p.astype(BF16), values)

    order0 = ((0, 0), (0, 2), (1, 0), (0, -1), (0, 1), (1, 2), (1, -1), (1, 1))
    order1 = ((0, 0), (1, 0), (0, 2), (1, -1), (1, 1), (1, 2), (0, -1), (0, 1))
    g = kvgather
    every_step = {
        1: lambda: g.crossed((0, 0)),
        2: lambda: (g.travel(), qswap.wait_recv()),
        8: dygather.step1,
        14: dygather.step2,
        20: dygather.step3,
    }
    step_p0 = {
        4: lambda: (g.opposite_on(), g.send(3, 4), g.wait(0), g.cross((1, 0))),
        12: lambda: (g.ring_done(), g.send(7, 8)),
        20: g.step4,
        24: lambda: (g.wait(7, 8), g.cross((1, -1), (1, 1))),
    }
    step_p1 = {
        4: lambda: (g.pair_on(), g.opposite_on()),
        12: lambda: (g.wait(7, 8), g.cross((1, -1), (1, 1)), g.send(3, 4)),
        16: g.step4,
        24: g.ring_done,
    }
    for i in range(1, 8):
        for steps, order in ((step_p0, order0), (step_p1, order1)):
            steps[4 * i + 2] = functools.partial(g.crossed, order[i])

    def along(s, first, second):
        return tuple(
            jnp.where(blk.p == 0, pick(s, [d[i] for d in first]), pick(s, [d[i] for d in second])) for i in range(2)
        )

    def attend_step(u):
        side = jnp.where(u < 4, lax.div(u, 2), lax.rem(u, 2))
        t = jnp.where(u < 4, lax.rem(u, 2), lax.div(u, 2))
        s, core = lax.div(t, 2), lax.rem(t, 2)
        jb = blk.slot(*along(s, order0, order1), core)
        for k, action in step_p0.items():
            when((u == k) & (blk.p == 0), action)
        for k, action in step_p1.items():
            when((u == k) & (blk.p == 1), action)
        for k, action in every_step.items():
            when(u == k, action)
        limit = limit_of(side)
        careful = (jb == 0) | (jb == limit)
        when((jb <= limit) & jnp.logical_not(careful), lambda: attend(side, jb, False))
        when((jb <= limit) & careful, lambda: attend(side, jb, True))

    loop(32, attend_step)

    def context_of(side, dst):
        for k in range(2):
            rows = slice(512 * k, 512 * k + 512)
            qi = half_of(side) * 512 + lax.broadcasted_iota(jnp.int32, (512, 1), 0)
            here = qi < starts[2]
            both = accum[2 * side + 1, rows, :] + jnp.where(here, accum[2 * side, rows, :], 0.0)
            dst[:, 128 * k : 128 * k + 128] = (both[:, 0:128] / both[:, 128:256]).astype(BF16)
            accum[2 * side, rows, 0:128] = both[:, 128:256]

    def extend(side):
        for k in range(2):
            rows = slice(512 * k, 512 * k + 512)
            terms = split3(jnp.log2(accum[2 * side, rows, 0:128]))
            qi = half_of(side) * 512 + lax.broadcasted_iota(jnp.int32, (512, 128), 0)
            lane = lax.broadcasted_iota(jnp.int32, (512, 128), 1)
            gone = jnp.where(lane == 0, -1e30, 0.0)
            qx[side, rows, 0:128] = qs[side, rows, :]
            qx[side, rows, 128:256] = terms.astype(BF16)
            qfar[side, rows, 0:128] = qs[side, rows, :]
            qfar[side, rows, 128:256] = jnp.where(qi < starts[2], terms, gone).astype(BF16)

    context_of(1, ctxb)
    near_ctx, far_ctx = ctx.at[pl.ds(near, 512)], ctx.at[pl.ds(far, 512)]
    cswap = remote(ctxb, near_ctx, ms.at[1], mr.at[1], blk.mirror())
    cswap.start()
    context_of(0, far_ctx)

    def output_rows(base, i):
        at = pl.ds(pl.multiple_of(base + i * 256, 256), 256)
        out = nt(ctx[at, :], weights[:, OC:GC]).astype(BF16)
        first = lax.div(base, 128) + 2 * i
        part[first] = out[0:128]
        part[first + 1] = out[128:256]

    def halves(make):
        return make(0), make(1)

    def scatters(ss, rs):
        return halves(lambda q: Scatter(head, part, bufs, ss, rs, off=64 * q, n=64, k0=8 * q))

    def gathers(full, ss, rs):
        return halves(lambda q: Gather(head, full, 64, ss, rs, off=64 * q, stride=128, k0=13 * q))

    loop(2, lambda i: output_rows(far, i))
    one, two = scatters(rs1, rr1)
    one.begin()
    two.begin()
    dygather.step4()
    cswap.wait_recv()
    loop(2, lambda i: output_rows(near, i))
    extend(1)
    one.opposite()
    two.opposite()
    extend(0)
    first, second = gathers(block_b, gs1, gr1)
    own = pl.multiple_of(head.slot(0, 0) * 128, 128)
    for q, (item, collect) in enumerate(((one, first), (two, second))):
        item.late()
    for q, (item, collect) in enumerate(((one, first), (two, second))):
        item.end()
        rows = slice(64 * q, 64 * q + 64)
        mid = tok[rows, :].astype(F32) + item.total()
        middle[rows, :] = mid
        block_b[pl.ds(own + 64 * q, 64), :] = (mid * inverse(mid) * gain2).astype(BF16)
        collect.begin()
    qswap.wait_send()
    cswap.wait_send()
    kvgather.end()
    dygather.end()
    keep.wait()
    first.step1()
    second.step1()
    first.step2()
    second.step2()

    def forward_rows(base, i):
        at = pl.ds(pl.multiple_of(base + i * 256, 256), 256)
        both = nn(block_b[at, :], weights[:, GC:DC])
        gate, upper = both[:, 0:384], both[:, 384:768]
        sigma = 1.0 / (1.0 + jnp.exp(-gate))
        silu = gate * sigma
        act_grad = nn(block_dy[at, :], weights[:, DC:END])
        gate_low = (act_grad * upper * sigma * (1.0 + gate * (1.0 - sigma))).astype(BF16)
        low = jnp.concatenate([gate_low, (act_grad * silu).astype(BF16)], axis=1)
        acts[at, 0:768] = low
        acts[at, 768:1152] = (silu * upper).astype(BF16)
        out = nt(low, weights[:, GC:DC]).astype(BF16)
        first = lax.div(base, 128) + 2 * i
        part[first] = out[0:128]
        part[first + 1] = out[128:256]

    loop(2, lambda i: forward_rows(near, i))
    for collect in (first, second):
        collect.step3()
    for collect in (first, second):
        collect.step4()
        collect.finish()
    loop(2, lambda i: forward_rows(far, i))
    one, two = scatters(rs2, rr2)
    one.begin()
    two.begin()

    def down_rows(i):
        out = nt(acts[chunk(i, 256), 768:1152], weights[:, DC:END]).astype(BF16)
        ffpart[2 * i] = out[0:128]
        ffpart[2 * i + 1] = out[128:256]

    loop(4, down_rows)
    one.opposite()
    two.opposite()

    def put_terms(i, out, cols):
        for k in range(2):
            wpart[2 * i + k, 0, :, cols] = out[128 * k : 128 * k + 64]
            wpart[2 * i + k, 1, :, cols] = out[128 * k + 64 : 128 * k + 128]

    def gate_up_grads(i):
        put_terms(i, tn(block_b[:, chunk(i, 256)], acts[:, 0:768]).astype(BF16), slice(0, 768))

    loop(2, gate_up_grads)
    one.late()
    two.late()
    loop(2, lambda i: gate_up_grads(i + 2))
    first, second = gathers(block_a, gs2, gr2)
    gvec[:, 1024:2048] = jnp.zeros((1, 1024), F32)
    for q, (item, collect) in enumerate(((one, first), (two, second))):
        item.end()
        rows = slice(64 * q, 64 * q + 64)
        terms, part_grad = norm_back(middle[rows, :], gain2, item.total())
        mid_grad = dy[rows, :].astype(F32) + part_grad
        block_a[pl.ds(own + 64 * q, 64), :] = mid_grad.astype(BF16)
        collect.begin()
        gvec[:, 1024:2048] += jnp.sum(terms, axis=0, keepdims=True)
        for i in range(4):
            accum[3, 128 * i + 64 * q : 128 * i + 64 * q + 64, :] = mid_grad[:, 256 * i : 256 * i + 256]

    def down_grads(i):
        put_terms(i, tn(block_dy[:, chunk(i, 256)], acts[:, 768:1152]).astype(BF16), slice(768, 1152))

    loop(2, down_grads)
    first.step1()
    second.step1()
    first.step2()
    second.step2()
    loop(2, lambda i: down_grads(i + 2))
    for collect in (first, second):
        collect.step3()
    for collect in (first, second):
        collect.step4()
        collect.finish()

    def context_grads(base, i):
        at = pl.ds(pl.multiple_of(base + 256 * i, 256), 256)
        grad_all[at, :] = nn(block_a[at, :], weights[:, OC:GC]).astype(BF16)

    loop(2, lambda i: context_grads(near, i))
    gswap = remote(grad_all.at[pl.ds(near, 512)], grad_far, ms.at[2], mr.at[2], blk.mirror())
    gswap.start()
    loop(2, lambda i: context_grads(far, i))
    reload = pltpu.make_async_copy(saved, block_b, local.at[1])
    reload.start()
    ffscatter = Scatter(head, ffpart, ffbufs, fs, fr)
    wscatter = BlkScatter(blk, wpart, wboth, wbufs, vs, vr, vcs.at[0], vcr.at[0])
    ffscatter.begin()
    wscatter.cross()

    def extend_grad(side, grads, context):
        for k in range(2):
            rows, cols = slice(512 * k, 512 * k + 512), slice(128 * k, 128 * k + 128)
            grad = grads[0:512, cols]
            delta = jnp.sum(grad.astype(F32) * context[0:512, cols].astype(F32), axis=1, keepdims=True)
            dox[side, rows, 0:128] = grad
            dox[side, rows, 128:256] = split3(jnp.broadcast_to(delta, (512, 128))).astype(BF16)

    extend_grad(0, grad_all.at[pl.ds(far, 512)], far_ctx)
    loop(2, lambda i: clear(i))

    back0 = ((1, 2), (1, 1), (1, -1), (1, 0), (0, 1), (0, 2), (0, -1), (0, 0))
    back1 = ((1, 2), (0, 2), (0, 1), (0, -1), (1, 1), (1, -1), (1, 0), (0, 0))

    def attend_back(side, jb, masked):
        at = chunk(jb, 1024)
        keys = kv[at, 0:128]
        kx = jnp.concatenate([keys, ones], axis=1)
        vx = jnp.concatenate([kv[at, 128:256], ones], axis=1)
        source = qx if masked else qfar
        cols = pl.ds(pl.multiple_of(side * 128, 128), 128)
        for c in range(4):
            rows = slice(c * 256, c * 256 + 256)
            p = jnp.exp2(nt(kx, source[side, rows, :]))
            if masked:
                p = jnp.where(mask(side, jb, c, 256, True), p, 0.0)
            ds = (p * nt(vx, dox[side, rows, :])).astype(BF16)
            accum[0, :, 0:128] += nn(ds, source[side, rows, 0:128])
            accum[0, :, 128:256] += nn(p.astype(BF16), dox[side, rows, 0:128])
            accum[1, rows, cols] += tn(ds, keys)

    kvscatter = Scatter(blk, kvboth, kvbufs, xss, xrr)

    def crossing(s):
        return remote(xs.at[s % 2], kvboth.at[blk.plane(*along(s, back0, back1))], xcs.at[s], xcr.at[s], blk.sibling())

    sc = kvscatter
    actions0 = {
        0: lambda: sc.send(0), 1: lambda: sc.send(1), 2: lambda: sc.send(2), 4: sc.home, 5: sc.opposite,
        6: lambda: (sc.up(), sc.down()),
    }
    actions1 = {
        0: lambda: sc.send(0), 3: sc.opposite, 4: lambda: (sc.send(1), sc.up(), sc.down()), 5: lambda: sc.send(2),
        6: sc.home,
    }
    others = {
        0: lambda: (wscatter.merge(), wscatter.begin()),
        2: lambda: (wscatter.opposite(), ffscatter.opposite()),
        4: lambda: (wscatter.up(), wscatter.down(), wscatter.home(), ffscatter.up(), ffscatter.down(), ffscatter.home()),
        6: lambda: (wscatter.end(), ffscatter.end()),
    }

    def reached(plane):
        even = block - blk.c
        return 2 * plane <= jnp.maximum(even + 1, 15 - even)

    def plane_at(s):
        return blk.plane(*along(s, back0, back1))

    def back_step(t):
        s, core = lax.div(t, 2), 1 - lax.rem(t, 2)
        plane = plane_at(s)
        jb = plane * 2 + lax.rem(blk.c + core, 2)
        some = reached(plane)

        def compute():
            accum[0] = jnp.zeros((1024, 256), F32)
            loop(2, one)

        def one(side):
            when((t == 0) & (side == 1), lambda: (gswap.wait_recv(), extend_grad(1, grad_far, ctxb)))
            limit = limit_of(side)
            careful = (jb == 0) | (jb == limit)
            when((jb <= limit) & jnp.logical_not(careful), lambda: attend_back(side, jb, False))
            when((jb <= limit) & careful, lambda: attend_back(side, jb, True))

        when(some | (t == 0), compute)
        for i in range(8):

            def out(i=i):
                if i >= 2:
                    when(reached(plane_at(i - 2)), lambda: crossing(i - 2).wait_send())

                def give():
                    xs[i % 2] = accum[0].astype(BF16)
                    crossing(i).start()

                when(some, give)
                if i in others:
                    others[i]()

            def merge(i=i):
                def take():
                    crossing(i).wait_recv()
                    kvboth[plane] = (kvboth[plane].astype(F32) + accum[0]).astype(BF16)

                def none():
                    kvboth[plane] = jnp.zeros((1024, 256), BF16)

                when(some, take)
                when(jnp.logical_not(some), none)

            when(t == 2 * i, out)
            when(t == 2 * i + 1, merge)
            for p, actions in enumerate((actions0, actions1)):
                if i in actions:
                    when((t == 2 * i + 1) & (blk.p == p), actions[i])

    loop(16, back_step)
    for i in (6, 7):
        when(reached(plane_at(i)), crossing(i).wait_send)

    for k in range(2):
        dqsend[:, 128 * k : 128 * k + 128] = (accum[1, 512 * k : 512 * k + 512, 128:256] * SCALE).astype(BF16)
    dswap = remote(dqsend, dqhome, ms.at[3], mr.at[3], blk.mirror())
    dswap.start()
    reload.wait()
    gswap.wait_send()
    gvec[:, 2048:2304] = jnp.zeros((1, 256), F32)

    def back(raw, grad, at, gains):
        return norm_back(raw, gains, rope_back(grad, cosine[at, :], sine[at, :]))

    def query_back(base, i, grads):
        at = pl.ds(pl.multiple_of(base + 256 * i, 256), 256)
        for k in range(2):
            cols = slice(128 * k, 128 * k + 128)
            terms, out = back(qraw[at, cols], grads(i, k), at, qgain)
            acts[at, cols] = out.astype(BF16)
            gvec[:, 2048:2176] += jnp.sum(terms, axis=0, keepdims=True)

    def put_vterms(i, out, cols):
        for k in range(2):
            vpart[2 * i + k, 0, :, cols] = out[128 * k : 128 * k + 64]
            vpart[2 * i + k, 1, :, cols] = out[128 * k + 64 : 128 * k + 128]

    def output_grads(i):
        put_vterms(i, tn(block_a[:, chunk(i, 256)], ctx[...]).astype(BF16), slice(512, 768))

    def query_grads(i):
        put_vterms(i, tn(block_b[:, chunk(i, 256)], acts[:, 0:256]).astype(BF16), slice(0, 256))

    def key_value_grads(i):
        put_vterms(i, tn(block_b[:, chunk(i, 256)], acts[:, 256:512]).astype(BF16), slice(256, 512))

    for i in range(2):
        query_back(far, i, lambda i, k: accum[1, 512 * k + 256 * i : 512 * k + 256 * i + 256, 0:128] * SCALE)
    loop(4, output_grads)
    layer_out[...] = (middle[...] + ffscatter.total()).astype(BF16)
    wsum = wscatter.total()
    gate_out[...] = wsum[:, 0:384]
    up_out[...] = wsum[:, 384:768]
    down_out[...] = wsum[:, 768:1152]
    dswap.wait_recv()
    for i in range(2):
        query_back(near, i, lambda i, k: dqhome[256 * i : 256 * i + 256, 128 * k : 128 * k + 128].astype(F32))
    loop(4, query_grads)
    kvscatter.end()
    accum[2] = kvscatter.total()

    def key_back(i):
        at = slice(256 * i, 256 * i + 256)
        terms, out = back(kraw[at, :], accum[2, at, 0:128] * LN2, at, kgain)
        acts[at, 256:384] = out.astype(BF16)
        gvec[:, 2176:2304] += jnp.sum(terms, axis=0, keepdims=True)
        acts[at, 384:512] = accum[2, at, 128:256].astype(BF16)

    for i in range(4):
        key_back(i)
    dswap.wait_send()

    gvec[:, 0:1024] = jnp.zeros((1, 1024), F32)

    def input_rows(base, i):
        at = pl.ds(pl.multiple_of(base + i * 256, 256), 256)
        out = nt(acts[at, 0:512], weights[:, QC:OC])
        gvec[:, 0:1024] += jnp.sum(out * block_b[at, :].astype(F32), axis=0, keepdims=True)
        out = out.astype(BF16)
        first = lax.div(base, 128) + 2 * i
        part[first] = out[0:128]
        part[first + 1] = out[128:256]

    loop(2, lambda i: input_rows(far, i))
    one, two = scatters(rs3, rr3)
    one.begin()
    two.begin()

    loop(2, lambda i: input_rows(near, i))
    gvec[:, 0:1024] = gvec[:, 0:1024] / gain1
    first = [remote(gvec, gin.at[i], g1s.at[i], g1r.at[i], d) for i, d in enumerate(head.peers())]
    for copy in first:
        copy.start()
    loop(4, key_value_grads)
    vscatter = BlkScatter(blk, vpart, vboth, vbufs, qs_s, qr_r, qcs.at[0], qcr.at[0])
    vscatter.cross()
    one.opposite()
    two.opposite()
    vscatter.merge()
    vscatter.begin()
    one.late()
    two.late()

    for copy in first:
        copy.wait()
    summed = gvec[...]
    for i in range(7):
        summed = summed + gin[i]
    for k in range(8):
        gstage[k, :, 0:128] = summed[:, 128 * k : 128 * k + 128]
        gstage[k, :, 128:256] = summed[:, 1024 + 128 * k : 1152 + 128 * k]
        gstage[k, :, 256:512] = summed[:, 2048:2304]
    every = [(dp, dr, dc) for dp in range(2) for dr in range(4) for dc in range(2)][1:]
    second = [
        remote(gstage.at[blk.plane(d[0], d[1])], gin2.at[i], g2s.at[i], g2r.at[i], blk.dev(*d))
        for i, d in enumerate(every)
    ]
    for copy in second:
        copy.start()
    vscatter.opposite()
    for q, item in enumerate((one, two)):
        item.end()
        rows = slice(64 * q, 64 * q + 64)
        _, input_part = norm_back(tok[rows, :].astype(F32), gain1, item.total())
        for i in range(4):
            cols = slice(256 * i, 256 * i + 256)
            mid_grad = accum[3, 128 * i + 64 * q : 128 * i + 64 * q + 64, :]
            tokens_grad[rows, cols] = (mid_grad + input_part[:, cols]).astype(BF16)
        if q == 0:
            vscatter.late()
    vscatter.end()
    vsum = vscatter.total()
    query_out[...] = vsum[:, 0:256]
    key_out[...] = vsum[:, 256:384]
    value_out[...] = vsum[:, 384:512]
    output_out[...] = vsum[:, 512:768]
    for copy in second:
        copy.wait()
    out = gstage[blk.plane(0, 0)]
    for i in range(15):
        out = out + gin2[i]
    offset = blk.c * 64 + head.h * 8
    lane = block * 8 + head.h
    first_out[...] = pltpu.roll(out[:, 0:128], lax.rem(128 - offset, 128), 1)[:, 0:8]
    second_out[...] = pltpu.roll(out[:, 128:256], lax.rem(128 - offset, 128), 1)[:, 0:8]
    qn_out[...] = pltpu.roll(out[:, 256:384], lax.rem(128 - lane, 128), 1)[:, 0:1]
    kn_out[...] = pltpu.roll(out[:, 384:512], lax.rem(128 - lane, 128), 1)[:, 0:1]


def hand_over_kernel(*refs):
    count = len(refs) // 2
    for i in range(count):
        refs[count + i][...] = refs[i][...]


def sems(*counts):
    return [pltpu.SemaphoreType.DMA((c,)) for c in counts]


def per_device(
    tokens, doc_starts, first_gain, query_weight, key_matrix, value_matrix, querynorm, keynorm,
    output_weight, second_gain, gate_weight, up_weight, down_weight, grad_out,
):
    freqs = np.tile(THETA ** (-np.arange(64, dtype=np.float64) / 64), 2).astype(np.float32)
    vm = pl.BlockSpec(memory_space=pltpu.VMEM)
    hbm = pl.BlockSpec(memory_space=pl.ANY)
    outs = [
        ((128, 1024), BF16), ((128, 1024), BF16), ((64, 256), F32), ((64, 128), F32), ((64, 128), F32),
        ((64, 256), F32), ((64, 384), F32), ((64, 384), F32), ((64, 384), F32),
        ((1, 8), F32), ((1, 8), F32), ((1, 1), F32), ((1, 1), F32), ((1024, 1024), BF16),
    ]
    scratch = [
        ((1024, 128), F32), ((1024, 128), F32),
        ((1024, 1920), BF16), ((1024, 1024), BF16), ((1024, 1024), BF16), ((1024, 1024), BF16), ((16384, 256), BF16),
        ((2, 1024, 128), BF16), ((1024, 128), BF16), ((1024, 256), F32), ((1024, 128), F32), ((4, 1024, 256), F32),
        ((1024, 256), BF16), ((512, 256), BF16), ((2, 1024, 256), BF16), ((2, 1024, 256), BF16), ((128, 1024), F32),
        ((8, 128, 1024), BF16), ((7, 128, 1024), BF16), ((8, 128, 1024), BF16), ((7, 128, 1024), BF16),
        ((1024, 1152), BF16), ((1024, 256), BF16), ((512, 256), BF16), ((2, 1024, 256), BF16),
        ((8, 2, 64, 1152), BF16), ((8, 64, 1152), BF16), ((7, 64, 1152), BF16),
        ((8, 2, 64, 768), BF16), ((8, 64, 768), BF16), ((7, 64, 768), BF16),
        ((2, 1024, 256), BF16), ((8, 1024, 256), BF16), ((7, 1024, 256), BF16), ((512, 256), BF16), ((512, 256), BF16),
        ((1, 2304), F32), ((7, 1, 2304), F32), ((8, 1, 512), F32), ((15, 1, 512), F32),
    ]
    counts = (13, 13, 13, 13, 8, 8, 13, 13, 8, 8, 13, 13, 4, 4, 16, 16, 26, 26, 16, 16, 26, 26, 16, 16)
    counts += (8, 8, 8, 8, 1, 1, 8, 8, 1, 1, 8, 8, 8, 8, 7, 7, 15, 15, 2)
    made = pl.pallas_call(
        layer_kernel,
        out_shape=[jax.ShapeDtypeStruct(s, d) for s, d in outs],
        in_specs=[pl.BlockSpec(memory_space=pltpu.SMEM)] + [vm] * 14,
        out_specs=[vm] * 13 + [hbm],
        scratch_shapes=[pltpu.VMEM(s, d) for s, d in scratch] + sems(*counts),
        compiler_params=pltpu.CompilerParams(vmem_limit_bytes=VMEM_LIMIT, collective_id=1, has_side_effects=True),
    )(
        doc_starts, tokens, grad_out, query_weight, key_matrix, value_matrix, output_weight.T, gate_weight, up_weight,
        down_weight.T, first_gain.reshape(8, 128), second_gain.reshape(8, 128), querynorm[None, :], keynorm[None, :], freqs[None, :],
    )
    made = pl.pallas_call(
        hand_over_kernel,
        out_shape=[jax.ShapeDtypeStruct(s, d) for s, d in outs[:13]],
        in_specs=[vm] * 13,
        out_specs=[vm] * 13,
    )(*made[:13])
    layer_out, tokens_grad, query, key, value, output, gate, up, down, first, second, qn, kn = made
    return (
        layer_out, tokens_grad, first.reshape(8), query, key, value, qn.reshape(1), kn.reshape(1),
        output.T, second.reshape(8), gate, up, down.T,
    )


def solution(mesh):
    return jax.shard_map(
        per_device,
        mesh=mesh,
        in_specs=(
            P(("blk", "head"), None),
            P(),
            P(),
            P("blk", "head"),
            P("blk", "head"),
            P("blk", "head"),
            P(),
            P(),
            P("head", "blk"),
            P(),
            P("blk", "head"),
            P("blk", "head"),
            P("head", "blk"),
            P(("blk", "head"), None),
        ),
        out_specs=(
            P(("blk", "head"), None),
            P(("blk", "head"), None),
            P(("blk", "head")),
            P("blk", "head"),
            P("blk", "head"),
            P("blk", "head"),
            P(("blk", "head")),
            P(("blk", "head")),
            P("head", "blk"),
            P(("blk", "head")),
            P("blk", "head"),
            P("blk", "head"),
            P("head", "blk"),
        ),
        check_vma=False,
    )
```

```python
import functools

import jax
import jax.numpy as jnp
from jax import lax
from jax.experimental import pallas as pl
from jax.experimental.pallas import tpu as pltpu
import numpy as np
from jax.sharding import PartitionSpec as P

EPS = 1e-06
THETA = 1000000.0
MESH = pl.DeviceIdType.MESH
F32 = jnp.float32
BF16 = jnp.bfloat16
LOG2E = 1.4426950408889634
LN2 = 0.6931471805599453
HEAD_DIM = 128
PARTS = 4
SCALE = HEAD_DIM**-0.5
VMEM_LIMIT = 64 * 2**20 - 2**16

QC, KC, VC, OC, GC, UC, DC, END = 0, 256, 384, 512, 768, 1152, 1536, 1920


def nn(a, b):
    return jnp.dot(a, b, preferred_element_type=F32)


def nt(a, b):
    return lax.dot_general(a, b, (((1,), (1,)), ((), ())), preferred_element_type=F32)


def tn(a, b):
    return lax.dot_general(a, b, (((0,), (0,)), ((), ())), preferred_element_type=F32)


def chunk(i, size):
    return pl.ds(pl.multiple_of(i * size, size), size)


def loop(count, body):
    def step(i, carry):
        body(i)
        return carry

    lax.fori_loop(0, count, step, 0)


def run_all(*actions):
    def run():
        for action in actions:
            action()

    return run


def when(condition, action):
    def run():
        action()

    pl.when(condition)(run)


class HeadRing:
    def __init__(self):
        self.b = lax.axis_index("blk")
        h = lax.axis_index("head")
        self.h = h
        self.p, self.r = lax.div(h, 4), lax.rem(h, 4)

    def plane(self, dp, dr):
        return lax.rem(self.p + dp, 2) * 4 + lax.rem(self.r + dr + 4, 4)

    slot = plane

    def dev(self, dp, dr):
        return (self.b, self.plane(dp, dr))

    def near(self):
        return [self.dev(1, 0), self.dev(0, 1), self.dev(0, -1)]


class BlkRing:
    def __init__(self):
        b = lax.axis_index("blk")
        self.h = lax.axis_index("head")
        self.b = b
        self.p, self.r, self.c = lax.div(b, 8), lax.rem(lax.div(b, 2), 4), lax.rem(b, 2)

    def plane(self, dp, dr):
        return lax.rem(self.p + dp, 2) * 4 + lax.rem(self.r + dr + 4, 4)

    def slot(self, dp, dr, dc=0):
        return self.plane(dp, dr) * 2 + lax.rem(self.c + dc, 2)

    def dev(self, dp, dr, dc=0):
        return (self.slot(dp, dr, dc), self.h)

    def sibling(self):
        return self.dev(0, 0, 1)

    def mirror(self):
        return (15 - self.b, self.h)

    def near(self):
        return [self.dev(1, 0), self.dev(0, 1), self.dev(0, -1)]


def greet(devices):
    for d in devices:
        pl.semaphore_signal(pltpu.get_barrier_semaphore(), inc=1, device_id=d, device_id_type=MESH)


def remote(src, dst, ss, rs, dev):
    return pltpu.make_async_remote_copy(
        src_ref=src, dst_ref=dst, send_sem=ss, recv_sem=rs, device_id=dev, device_id_type=MESH
    )


class Gather:
    ORDER = ((0, 0), (1, 0), (0, -1), (0, 1), (0, 2), (1, -1), (1, 1), (1, 2))

    def __init__(self, ring, full, n, ss, rs, sib=None, on_ring=False, off=0, stride=None, k0=0):
        self.ring, self.full, self.n, self.ss, self.rs, self.sib = ring, full, n, ss, rs, sib
        self.on_ring, self.off, self.stride, self.k0 = on_ring, off, stride or n, k0

    def rows(self, dp, dr, part=None):
        base = self.ring.slot(dp, dr) * self.stride + self.off
        size = self.n
        if part is not None:
            size = self.n // 2
            base = base + part * size
        return self.full.at[pl.ds(pl.multiple_of(base, size), size)]

    def copy(self, k):
        ring, rows = self.ring, self.rows
        ref, dev = (
            lambda: (rows(0, 0), ring.dev(1, 0)),
            lambda: (rows(0, 0, 0), ring.dev(0, 1)),
            lambda: (rows(0, 0, 1), ring.dev(0, -1)),
            lambda: (rows(0, 0, 1), ring.dev(0, 1)),
            lambda: (rows(0, 0, 0), ring.dev(0, -1)),
            lambda: (rows(0, -1, 0), ring.dev(0, 1)),
            lambda: (rows(0, 1, 1), ring.dev(0, -1)),
            lambda: (rows(1, 0), ring.dev(0, 1)),
            lambda: (rows(1, 0), ring.dev(0, -1)),
            lambda: (rows(1, -1, 0), ring.dev(0, 1)) if self.on_ring else (rows(0, 2, 0), ring.dev(1, 0)),
            lambda: (rows(1, 1, 1), ring.dev(0, -1)) if self.on_ring else (rows(0, 2, 1), ring.dev(1, 0)),
        )[k]()
        return remote(ref, ref, self.ss.at[self.k0 + k], self.rs.at[self.k0 + k], dev)

    def send(self, *ks):
        for k in ks:
            self.copy(k).start()

    def wait(self, *ks):
        for k in ks:
            self.copy(k).wait_recv()

    def crossing(self, dp, dr):
        k = self.ORDER.index((dp, dr))
        ref = self.rows(dp, dr)
        return remote(ref, ref, self.sib[0].at[k], self.sib[1].at[k], self.ring.sibling())

    def cross(self, *which):
        if self.sib is not None:
            for w in which:
                self.crossing(*w).start()

    def crossed(self, *which):
        if self.sib is not None:
            for w in which:
                self.crossing(*w).wait_recv()

    def begin(self):
        self.send(1, 2, 0, 3, 4)
        self.cross((0, 0))

    def travel(self):
        self.wait(1)
        self.send(5)
        self.wait(2)
        self.send(6)

    def pair_on(self):
        self.wait(0)
        self.send(7, 8)
        self.cross((1, 0))

    def step1(self):
        self.travel()
        self.pair_on()

    def opposite_on(self):
        self.wait(5)
        if not self.on_ring:
            self.send(9)
        self.wait(6)
        if not self.on_ring:
            self.send(10)
        self.cross((0, 2))

    def ring_done(self):
        self.wait(3, 4)
        self.cross((0, -1), (0, 1))

    def step2(self):
        self.opposite_on()
        self.ring_done()

    def step3(self):
        self.wait(7)
        if self.on_ring:
            self.send(9)
        self.wait(8)
        if self.on_ring:
            self.send(10)
        self.cross((1, -1), (1, 1))

    def step4(self):
        self.wait(9, 10)
        self.cross((1, 2))

    def end(self):
        for k in range(11):
            self.copy(k).wait_send()
        if self.sib is not None:
            for w in self.ORDER:
                self.crossing(*w).wait_send()

    def finish(self):
        self.crossed(*self.ORDER)
        self.end()

    def steps(self):
        return [self.begin, self.step1, self.step2, self.step3, self.step4, self.finish]


class Scatter:
    def __init__(self, ring, part, bufs, ss, rs, off=0, n=None, k0=0):
        self.ring, self.part, self.bufs, self.ss, self.rs = ring, part, bufs, ss, rs
        self.off, self.n, self.k0 = off, n or part.shape[1], k0

    def span(self, half):
        if half is None:
            return pl.ds(self.off, self.n)
        return pl.ds(self.off + half * (self.n // 2), self.n // 2)

    def own(self, dp, dr, half=None):
        return self.part.at[self.ring.plane(dp, dr), self.span(half)]

    def buf(self, i, half=None):
        return self.bufs.at[i, self.span(half)]

    def copy(self, k):
        ring, own, buf = self.ring, self.own, self.buf
        src, dst, dev = (
            lambda: (own(1, 2), buf(0), ring.dev(1, 0)),
            lambda: (own(1, 1), buf(1), ring.dev(0, 1)),
            lambda: (own(1, -1), buf(2), ring.dev(0, -1)),
            lambda: (own(0, 2, 0), buf(6, 0), ring.dev(0, 1)),
            lambda: (own(0, 2, 1), buf(6, 1), ring.dev(0, -1)),
            lambda: (own(1, 0), buf(3), ring.dev(1, 0)),
            lambda: (own(0, 1), buf(4), ring.dev(0, 1)),
            lambda: (own(0, -1), buf(5), ring.dev(0, -1)),
        )[k]()
        return remote(src, dst, self.ss.at[self.k0 + k], self.rs.at[self.k0 + k], dev)

    def send(self, *ks):
        for k in ks:
            self.copy(k).start()

    def wait(self, *ks):
        for k in ks:
            self.copy(k).wait_recv()

    def add(self, dst, *srcs):
        value = dst[...].astype(F32)
        for src in srcs:
            value = value + src[...].astype(F32)
        dst[...] = value.astype(dst.dtype)

    def begin(self):
        self.send(1, 2, 0)

    def opposite(self):
        self.wait(0)
        self.add(self.own(0, 2), self.buf(0))
        self.send(3, 4)

    def home(self):
        self.wait(1, 2)
        self.add(self.own(1, 0), self.buf(1), self.buf(2))
        self.send(5)

    def up(self):
        self.wait(3)
        self.add(self.own(0, 1, 0), self.buf(6, 0))
        self.send(6)

    def down(self):
        self.wait(4)
        self.add(self.own(0, -1, 1), self.buf(6, 1))
        self.send(7)

    def end(self):
        self.wait(5, 6, 7)
        for k in range(8):
            self.copy(k).wait_send()

    def late(self):
        self.up()
        self.down()
        self.home()

    def total(self):
        out = self.own(0, 0)[...].astype(F32)
        for i in (3, 4, 5):
            out = out + self.buf(i)[...].astype(F32)
        return out


class BlkScatter(Scatter):
    def __init__(self, ring, terms, part, bufs, ss, rs, cs, cr):
        super().__init__(ring, part, bufs, ss, rs)
        self.terms, self.cs, self.cr = terms, cs, cr

    def crossing(self):
        return remote(self.terms.at[:, 1 - self.ring.c], self.part, self.cs, self.cr, self.ring.sibling())

    def cross(self):
        self.crossing().start()

    def merge(self):
        self.crossing().wait_recv()

        def body(k):
            self.part[k] = (self.part[k].astype(F32) + self.terms[k, self.ring.c].astype(F32)).astype(BF16)

        loop(8, body)
        self.crossing().wait_send()


def weave(*lists):
    for i in range(max(len(item) for item in lists)):
        for item in lists:
            if i < len(item):
                item[i]()


def rope(v, cosine, sine):
    return v * cosine + pltpu.roll(v, 64, 1) * sine


def rope_back(g, cosine, sine):
    return g * cosine + pltpu.roll(g * sine, 64, 1)


def inverse(v):
    return lax.rsqrt(jnp.mean(v * v, axis=-1, keepdims=True) + EPS)


def norm_back(v, gain, grad):
    r = inverse(v)
    n = v * r
    scaled = grad * gain
    return grad * n, r * (scaled - n * jnp.mean(scaled * n, axis=-1, keepdims=True))


def split3(v):
    a = (-v).astype(BF16).astype(F32)
    rest = -v - a
    b = rest.astype(BF16).astype(F32)
    lane = lax.broadcasted_iota(jnp.int32, v.shape, 1)
    return jnp.where(lane == 0, a, jnp.where(lane == 1, b, jnp.where(lane == 2, rest - b, 0.0)))


def begin_of(starts, index):
    begin = jnp.zeros_like(index)
    for k in range(1, 4):
        begin = jnp.where(index >= starts[k], starts[k], begin)
    return begin


def pick(index, values):
    out = jnp.int32(values[-1])
    for k in range(len(values) - 2, -1, -1):
        out = jnp.where(index == k, jnp.int32(values[k]), out)
    return out


def layer_kernel(
    starts, tok, dy, wq, wk, wv, wo, wg, wu, wd, gain_one, gain_two, gain_q, gain_k, freqs,
    layer_out, tokens_grad, query_out, key_out, value_out, output_out, gate_out, up_out, down_out,
    first_out, second_out, qn_out, kn_out, saved,
    cosine, sine, weights, block_a, block_b, block_dy, kv, qs, qsend, qraw, kraw, accum, ctx, ctxb, qx, qfar, middle,
    part, bufs, ffpart, ffbufs, acts, grad_all, grad_far, dox, wpart, wboth, wbufs, vpart, vboth, vbufs,
    xs, kvboth, kvbufs, dqsend, dqhome, gvec, gin, gsum,
    ws, wr, wcs, wcr, ks, kr, kcs, kcr, ms, mr, rs, rr, gs, gr, ds_, dr_,
    fs, fr, vs, vr, vcs, vcr, w2s, w2r, w2cs, w2cr, qs_s, qr_r, qcs, qcr, xss, xrr, xcs, xcr, gns, gnr, local,
):
    head, blk = HeadRing(), BlkRing()
    partners = head.near() + blk.near() + [blk.sibling(), blk.mirror()]
    greet(partners)
    block = blk.b

    def line(ref):
        value = ref[...].astype(F32)
        return jnp.concatenate([value[i : i + 1] for i in range(8)], axis=1)

    gain1, gain2 = line(gain_one), line(gain_two)
    qgain, kgain = gain_q[...].astype(F32), gain_k[...].astype(F32)
    x = tok[...].astype(F32)
    block_a[chunk(head.slot(0, 0), 128), :] = (x * inverse(x) * gain1).astype(BF16)
    mine = chunk(blk.slot(0, 0), 64)
    for ref, first in ((wq, QC), (wk, KC), (wv, VC), (wo, OC), (wg, GC), (wu, UC), (wd, DC)):
        weights[mine, first : first + ref.shape[1]] = ref[...]
    block_dy[chunk(head.slot(0, 0), 128), :] = dy[...]
    pl.semaphore_wait(pltpu.get_barrier_semaphore(), len(partners))
    wone = Gather(blk, weights.at[:, QC:GC], 64, ws, wr, (wcs, wcr))
    wtwo = Gather(blk, weights.at[:, GC:END], 64, w2s, w2r, (w2cs, w2cr), on_ring=True)
    normed = Gather(head, block_a, 128, gs, gr)
    normed.begin()
    wone.begin()
    wtwo.begin()
    for i in range(4):
        at = slice(256 * i, 256 * i + 256)
        index = block * 1024 + 256 * i + lax.broadcasted_iota(jnp.int32, (256, 1), 0)
        angle = (index - begin_of(starts, index)).astype(F32) * freqs[...]
        lane = lax.broadcasted_iota(jnp.int32, (256, 128), 1)
        cosine[at, :] = jnp.cos(angle)
        turn = jnp.sin(angle)
        sine[at, :] = jnp.where(lane < 64, -turn, turn)
    normed.step1()
    wone.step1()
    wtwo.step1()
    normed.step2()
    for step in (wone.step2, wone.step3, wone.step4, wtwo.step2, wone.finish):
        step()

    base = pl.multiple_of(block * 1024, 1024)
    far, near = pl.multiple_of((1 - head.p) * 512, 512), pl.multiple_of(head.p * 512, 512)

    def query_rows(base, dst):
        for i in range(2):
            at = pl.ds(pl.multiple_of(base + 256 * i, 256), 256)
            out = nn(block_a[at, :], weights[:, QC:KC])
            for k in range(2):
                v = out[:, 128 * k : 128 * k + 128]
                qraw[at, 128 * k : 128 * k + 128] = v
                v = rope(v * inverse(v) * qgain, cosine[at, :], sine[at, :]) * (SCALE * LOG2E)
                dst[512 * k + 256 * i : 512 * k + 256 * i + 256, :] = v.astype(BF16)

    def keys_rows(first, i):
        at = pl.ds(pl.multiple_of(first + i * 256, 256), 256)
        out = nn(block_a[at, :], weights[:, KC:OC])
        v = out[:, 0:128]
        kraw[at, :] = v
        to = pl.ds(pl.multiple_of(base + first + i * 256, 256), 256)
        kv[to, 0:128] = rope(v * inverse(v) * kgain, cosine[at, :], sine[at, :]).astype(BF16)
        kv[to, 128:256] = out[:, 128:256].astype(BF16)

    query_rows(near, qsend)
    qswap = remote(qsend, qs.at[1], ms.at[0], mr.at[0], blk.mirror())
    qswap.start()
    loop(2, lambda i: keys_rows(near, i))
    wtwo.step3()
    for step in (normed.step3, normed.step4, normed.finish):
        step()
    keep = pltpu.make_async_copy(block_a, saved, local.at[0])
    keep.start()
    loop(2, lambda i: keys_rows(far, i))
    kvgather = Gather(blk, kv, 1024, ks, kr, (kcs, kcr))
    kvgather.send(1, 2, 0)
    kvgather.cross((0, 0))
    query_rows(far, qs.at[0])
    dygather = Gather(head, block_dy, 128, ds_, dr_, on_ring=True)
    dygather.begin()

    def clear(i):
        accum[i] = jnp.zeros((1024, 256), F32)

    loop(4, clear)
    ones = jnp.ones((1024, 128), BF16)

    def limit_of(side):
        return jnp.where(side == 0, block, 15 - block)

    def half_of(side):
        return jnp.where(side == 0, 2 * block + 1 - head.p, 30 - 2 * block + head.p)

    def mask(side, jb, c, rows, transposed):
        first = half_of(side) * 512 + lax.rem(c * rows, 512)
        shape_q, shape_k = ((1, rows), (1024, 1)) if transposed else ((rows, 1), (1, 1024))
        qi = first + lax.broadcasted_iota(jnp.int32, shape_q, 1 if transposed else 0)
        ki = jb * 1024 + lax.broadcasted_iota(jnp.int32, shape_k, 0 if transposed else 1)
        return (ki >= begin_of(starts, qi)) & (ki <= qi)

    def attend(sides, jb, masked):
        at = chunk(jb, 1024)
        keys = kv[at, 0:128]
        values = jnp.concatenate([kv[at, 128:256], ones], axis=1)
        for side in sides:
            row = 2 * side + masked
            for c in range(4):
                rows = slice(c * 256, c * 256 + 256)
                p = jnp.exp2(nt(qs[side, rows, :], keys))
                if masked:
                    p = jnp.where(mask(side, jb, c, 256, False), p, 0.0)
                accum[row, rows, :] += nn(p.astype(BF16), values)

    def work(jb, unit):
        clear_of = [(jb != 0) & (jb < limit_of(side)) for side in range(2)]
        both = clear_of[0] & clear_of[1]

        def one(side):
            limit = limit_of(side)
            careful = (jb == 0) | (jb == limit)
            when((jb <= limit) & jnp.logical_not(careful), lambda: unit((side,), jb, False))
            when((jb <= limit) & careful, lambda: unit((side,), jb, True))

        when(both, lambda: unit((0, 1), jb, False))
        when(jnp.logical_not(both), lambda: loop(2, one))

    order0 = ((0, 0), (0, 2), (1, 0), (0, -1), (0, 1), (1, 2), (1, -1), (1, 1))
    order1 = ((0, 0), (1, 0), (0, 2), (1, -1), (1, 1), (1, 2), (0, -1), (0, 1))
    g = kvgather
    every_step = {
        0: qswap.wait_recv,
        1: lambda: (g.crossed((0, 0)), g.travel()),
        4: lambda: (dygather.step1(), wtwo.step4()),
        7: dygather.step2,
        10: dygather.step3,
    }
    step_p0 = {
        2: lambda: (g.opposite_on(), g.send(3, 4), g.wait(0), g.cross((1, 0))),
        6: lambda: (g.ring_done(), g.send(7, 8)),
        10: g.step4,
        12: lambda: (g.wait(7, 8), g.cross((1, -1), (1, 1))),
    }
    step_p1 = {
        2: lambda: (g.pair_on(), g.opposite_on()),
        6: lambda: (g.wait(7, 8), g.cross((1, -1), (1, 1)), g.send(3, 4)),
        8: g.step4,
        12: g.ring_done,
    }
    for i in range(1, 8):
        for steps, order in ((step_p0, order0), (step_p1, order1)):
            steps[2 * i + 1] = functools.partial(g.crossed, order[i])

    def along(s, first, second):
        return tuple(
            jnp.where(blk.p == 0, pick(s, [d[i] for d in first]), pick(s, [d[i] for d in second])) for i in range(2)
        )

    def attend_step(t):
        s, core = lax.div(t, 2), lax.rem(t, 2)
        jb = blk.slot(*along(s, order0, order1), core)
        for k, action in step_p0.items():
            when((t == k) & (blk.p == 0), action)
        for k, action in step_p1.items():
            when((t == k) & (blk.p == 1), action)
        for k, action in every_step.items():
            when(t == k, action)
        work(jb, attend)

    loop(16, attend_step)

    def context_of(side, dst):
        for k in range(2):
            rows = slice(512 * k, 512 * k + 512)
            qi = half_of(side) * 512 + lax.broadcasted_iota(jnp.int32, (512, 1), 0)
            here = qi < starts[2]
            both = accum[2 * side + 1, rows, :] + jnp.where(here, accum[2 * side, rows, :], 0.0)
            dst[:, 128 * k : 128 * k + 128] = (both[:, 0:128] / both[:, 128:256]).astype(BF16)
            accum[2 * side, rows, 0:128] = both[:, 128:256]

    def extend(side):
        for k in range(2):
            rows = slice(512 * k, 512 * k + 512)
            terms = split3(jnp.log2(accum[2 * side, rows, 0:128]))
            qi = half_of(side) * 512 + lax.broadcasted_iota(jnp.int32, (512, 128), 0)
            lane = lax.broadcasted_iota(jnp.int32, (512, 128), 1)
            gone = jnp.where(lane == 0, -1e30, 0.0)
            qx[side, rows, 0:128] = qs[side, rows, :]
            qx[side, rows, 128:256] = terms.astype(BF16)
            qfar[side, rows, 0:128] = qs[side, rows, :]
            qfar[side, rows, 128:256] = jnp.where(qi < starts[2], terms, gone).astype(BF16)

    context_of(1, ctxb)
    near_ctx, far_ctx = ctx.at[pl.ds(near, 512)], ctx.at[pl.ds(far, 512)]
    cswap = remote(ctxb, near_ctx, ms.at[1], mr.at[1], blk.mirror())
    cswap.start()
    context_of(0, far_ctx)

    def output_rows(base, i):
        at = pl.ds(pl.multiple_of(base + i * 256, 256), 256)
        out = nt(ctx[at, :], weights[:, OC:GC]).astype(BF16)
        first = lax.div(base, 128) + 2 * i
        part[first] = out[0:128]
        part[first + 1] = out[128:256]

    size = 128 // PARTS

    def scatters(ss, rs):
        return [Scatter(head, part, bufs, ss, rs, off=size * q, n=size, k0=8 * q) for q in range(PARTS)]

    def gathers(full, ss, rs):
        return [Gather(head, full, size, ss, rs, off=size * q, stride=128, k0=11 * q) for q in range(PARTS)]

    def all_of(items, *names):
        for name in names:
            for item in items:
                getattr(item, name)()

    loop(2, lambda i: output_rows(far, i))
    sums = scatters(rs, rr)
    all_of(sums, "begin")
    dygather.step4()
    extend(1)
    cswap.wait_recv()
    loop(2, lambda i: output_rows(near, i))
    all_of(sums, "opposite")
    extend(0)
    dygather.end()
    shards = gathers(block_b, gs, gr)
    own = pl.multiple_of(head.slot(0, 0) * 128, 128)
    all_of(sums, "late")
    for q, (item, collect) in enumerate(zip(sums, shards)):
        item.end()
        rows = slice(size * q, size * q + size)
        mid = tok[rows, :].astype(F32) + item.total()
        middle[rows, :] = mid
        block_b[pl.ds(own + size * q, size), :] = (mid * inverse(mid) * gain2).astype(BF16)
        collect.begin()
    qswap.wait_send()
    cswap.wait_send()
    kvgather.end()
    wtwo.finish()
    keep.wait()
    all_of(shards, "step1", "step2")

    def forward_rows(base, i):
        at = pl.ds(pl.multiple_of(base + i * 256, 256), 256)
        both = nn(block_b[at, :], weights[:, GC:DC])
        gate, upper = both[:, 0:384], both[:, 384:768]
        sigma = 1.0 / (1.0 + jnp.exp(-gate))
        silu = gate * sigma
        act_grad = nn(block_dy[at, :], weights[:, DC:END])
        gate_low = (act_grad * upper * sigma * (1.0 + gate * (1.0 - sigma))).astype(BF16)
        low = jnp.concatenate([gate_low, (act_grad * silu).astype(BF16)], axis=1)
        acts[at, 0:768] = low
        acts[at, 768:1152] = (silu * upper).astype(BF16)
        out = nt(low, weights[:, GC:DC]).astype(BF16)
        first = lax.div(base, 128) + 2 * i
        part[first] = out[0:128]
        part[first + 1] = out[128:256]

    loop(2, lambda i: forward_rows(near, i))
    all_of(shards, "step3", "step4", "finish")
    loop(2, lambda i: forward_rows(far, i))
    sums = scatters(rs, rr)
    all_of(sums, "begin")

    def down_rows(i):
        out = nt(acts[chunk(i, 256), 768:1152], weights[:, DC:END]).astype(BF16)
        ffpart[2 * i] = out[0:128]
        ffpart[2 * i + 1] = out[128:256]

    loop(4, down_rows)
    all_of(sums, "opposite")

    def put_terms(i, out, cols):
        for k in range(2):
            wpart[2 * i + k, 0, :, cols] = out[128 * k : 128 * k + 64]
            wpart[2 * i + k, 1, :, cols] = out[128 * k + 64 : 128 * k + 128]

    def gate_up_grads(i):
        put_terms(i, tn(block_b[:, chunk(i, 256)], acts[:, 0:768]).astype(BF16), slice(0, 768))

    loop(2, gate_up_grads)
    all_of(sums, "late")
    loop(2, lambda i: gate_up_grads(i + 2))
    shards = gathers(block_a, gs, gr)
    gvec[:, 1024:2048] = jnp.zeros((1, 1024), F32)
    for q, (item, collect) in enumerate(zip(sums, shards)):
        item.end()
        rows = slice(size * q, size * q + size)
        terms, part_grad = norm_back(middle[rows, :], gain2, item.total())
        mid_grad = dy[rows, :].astype(F32) + part_grad
        block_a[pl.ds(own + size * q, size), :] = mid_grad.astype(BF16)
        collect.begin()
        gvec[:, 1024:2048] += jnp.sum(terms, axis=0, keepdims=True)
        for i in range(4):
            accum[3, 128 * i + size * q : 128 * i + size * q + size, :] = mid_grad[:, 256 * i : 256 * i + 256]

    def down_grads(i):
        put_terms(i, tn(block_dy[:, chunk(i, 256)], acts[:, 768:1152]).astype(BF16), slice(768, 1152))

    loop(2, down_grads)
    all_of(shards, "step1", "step2")
    def context_grads(base, i):
        at = pl.ds(pl.multiple_of(base + 256 * i, 256), 256)
        grad_all[at, :] = nn(block_a[at, :], weights[:, OC:GC]).astype(BF16)

    loop(2, lambda i: context_grads(near, i))
    gswap = remote(grad_all.at[pl.ds(near, 512)], grad_far, ms.at[2], mr.at[2], blk.mirror())
    gswap.start()
    loop(2, lambda i: down_grads(i + 2))
    all_of(shards, "step3", "step4", "finish")

    loop(2, lambda i: context_grads(far, i))
    reload = pltpu.make_async_copy(saved, block_b, local.at[1])
    reload.start()
    ffscatter = Scatter(head, ffpart, ffbufs, fs, fr)
    wscatter = BlkScatter(blk, wpart, wboth, wbufs, vs, vr, vcs.at[0], vcr.at[0])
    ffscatter.begin()
    wscatter.cross()

    def extend_grad(side, grads, context):
        for k in range(2):
            rows, cols = slice(512 * k, 512 * k + 512), slice(128 * k, 128 * k + 128)
            grad = grads[0:512, cols]
            delta = jnp.sum(grad.astype(F32) * context[0:512, cols].astype(F32), axis=1, keepdims=True)
            dox[side, rows, 0:128] = grad
            dox[side, rows, 128:256] = split3(jnp.broadcast_to(delta, (512, 128))).astype(BF16)

    extend_grad(0, grad_all.at[pl.ds(far, 512)], far_ctx)
    loop(2, lambda i: clear(i))

    back0 = ((1, 2), (1, 1), (1, -1), (1, 0), (0, 1), (0, 2), (0, -1), (0, 0))
    back1 = ((1, 2), (0, 2), (0, 1), (0, -1), (1, 1), (1, -1), (1, 0), (0, 0))

    def attend_back(sides, jb, masked):
        at = chunk(jb, 1024)
        keys = kv[at, 0:128]
        kx = jnp.concatenate([keys, ones], axis=1)
        vx = jnp.concatenate([kv[at, 128:256], ones], axis=1)
        source = qx if masked else qfar
        for side in sides:
            for c in range(4):
                rows = slice(c * 256, c * 256 + 256)
                p = jnp.exp2(nt(kx, source[side, rows, :]))
                if masked:
                    p = jnp.where(mask(side, jb, c, 256, True), p, 0.0)
                ds = (p * nt(vx, dox[side, rows, :])).astype(BF16)
                accum[0, :, 0:128] += nn(ds, source[side, rows, 0:128])
                accum[0, :, 128:256] += nn(p.astype(BF16), dox[side, rows, 0:128])
                accum[1, chunk(4 * side + c, 128), :] += tn(keys, ds)

    kvscatter = Scatter(blk, kvboth, kvbufs, xss, xrr)

    def crossing(s):
        return remote(xs.at[s % 2], kvboth.at[blk.plane(*along(s, back0, back1))], xcs.at[s], xcr.at[s], blk.sibling())

    sc = kvscatter
    actions0 = {
        0: lambda: sc.send(0), 1: lambda: sc.send(1), 2: lambda: sc.send(2), 4: sc.home, 5: sc.opposite,
        6: lambda: (sc.up(), sc.down()),
    }
    actions1 = {
        0: lambda: sc.send(0), 3: sc.opposite, 4: lambda: (sc.send(1), sc.up(), sc.down()), 5: lambda: sc.send(2),
        6: sc.home,
    }
    others = {
        0: lambda: (wscatter.merge(), wscatter.begin()),
        2: lambda: (wscatter.opposite(), ffscatter.opposite()),
        4: lambda: (wscatter.up(), wscatter.down(), wscatter.home(), ffscatter.up(), ffscatter.down(), ffscatter.home()),
        6: lambda: (wscatter.end(), ffscatter.end()),
    }

    def reached(plane):
        even = block - blk.c
        return 2 * plane <= jnp.maximum(even + 1, 15 - even)

    def plane_at(s):
        return blk.plane(*along(s, back0, back1))

    def back_step(t):
        s, core = lax.div(t, 2), 1 - lax.rem(t, 2)
        plane = plane_at(s)
        jb = plane * 2 + lax.rem(blk.c + core, 2)
        some = reached(plane)

        def compute():
            accum[0] = jnp.zeros((1024, 256), F32)
            when(t == 0, lambda: (gswap.wait_recv(), extend_grad(1, grad_far, ctxb)))
            work(jb, attend_back)

        when(some | (t == 0), compute)
        for i in range(8):

            def out(i=i):
                if i >= 2:
                    when(reached(plane_at(i - 2)), lambda: crossing(i - 2).wait_send())

                def give():
                    xs[i % 2] = accum[0].astype(BF16)
                    crossing(i).start()

                when(some, give)
                if i in others:
                    others[i]()

            def merge(i=i):
                def take():
                    crossing(i).wait_recv()
                    kvboth[plane] = (kvboth[plane].astype(F32) + accum[0]).astype(BF16)

                def none():
                    kvboth[plane] = jnp.zeros((1024, 256), BF16)

                when(some, take)
                when(jnp.logical_not(some), none)

            when(t == 2 * i, out)
            when(t == 2 * i + 1, merge)
            for p, actions in enumerate((actions0, actions1)):
                if i in actions:
                    when((t == 2 * i + 1) & (blk.p == p), actions[i])

    loop(16, back_step)
    for i in (6, 7):
        when(reached(plane_at(i)), crossing(i).wait_send)

    def dq_of(side, k, i):
        first = 128 * (4 * side + 2 * k + i)
        return jnp.transpose(accum[1, first : first + 128, :]) * SCALE

    for k in range(2):
        for i in range(2):
            dqsend[256 * i : 256 * i + 256, 128 * k : 128 * k + 128] = dq_of(1, k, i).astype(BF16)
    dswap = remote(dqsend, dqhome, ms.at[3], mr.at[3], blk.mirror())
    dswap.start()
    reload.wait()
    gswap.wait_send()
    gvec[:, 2048:2304] = jnp.zeros((1, 256), F32)

    def back(raw, grad, at, gains):
        return norm_back(raw, gains, rope_back(grad, cosine[at, :], sine[at, :]))

    def query_back(base, i, grads):
        at = pl.ds(pl.multiple_of(base + 256 * i, 256), 256)
        for k in range(2):
            cols = slice(128 * k, 128 * k + 128)
            terms, out = back(qraw[at, cols], grads(i, k), at, qgain)
            acts[at, cols] = out.astype(BF16)
            gvec[:, 2048:2176] += jnp.sum(terms, axis=0, keepdims=True)

    def put_vterms(i, out, cols):
        for k in range(2):
            vpart[2 * i + k, 0, :, cols] = out[128 * k : 128 * k + 64]
            vpart[2 * i + k, 1, :, cols] = out[128 * k + 64 : 128 * k + 128]

    def output_grads(i):
        put_vterms(i, tn(block_a[:, chunk(i, 256)], ctx[...]).astype(BF16), slice(512, 768))

    def query_grads(i):
        put_vterms(i, tn(block_b[:, chunk(i, 256)], acts[:, 0:256]).astype(BF16), slice(0, 256))

    def key_value_grads(i):
        put_vterms(i, tn(block_b[:, chunk(i, 256)], acts[:, 256:512]).astype(BF16), slice(256, 512))

    for i in range(2):
        query_back(far, i, lambda i, k: dq_of(0, k, i))
    loop(4, output_grads)
    layer_out[...] = (middle[...] + ffscatter.total()).astype(BF16)
    wsum = wscatter.total()
    gate_out[...] = wsum[:, 0:384]
    up_out[...] = wsum[:, 384:768]
    down_out[...] = wsum[:, 768:1152]
    dswap.wait_recv()
    for i in range(2):
        query_back(near, i, lambda i, k: dqhome[256 * i : 256 * i + 256, 128 * k : 128 * k + 128].astype(F32))
    loop(4, query_grads)
    kvscatter.end()
    accum[2] = kvscatter.total()

    def key_back(i):
        at = slice(256 * i, 256 * i + 256)
        terms, out = back(kraw[at, :], accum[2, at, 0:128] * LN2, at, kgain)
        acts[at, 256:384] = out.astype(BF16)
        gvec[:, 2176:2304] += jnp.sum(terms, axis=0, keepdims=True)
        acts[at, 384:512] = accum[2, at, 128:256].astype(BF16)

    for i in range(4):
        key_back(i)
    dswap.wait_send()

    gvec[:, 0:1024] = jnp.zeros((1, 1024), F32)

    def input_rows(base, i):
        at = pl.ds(pl.multiple_of(base + i * 256, 256), 256)
        out = nt(acts[at, 0:512], weights[:, QC:OC])
        gvec[:, 0:1024] += jnp.sum(out * block_b[at, :].astype(F32), axis=0, keepdims=True)
        out = out.astype(BF16)
        first = lax.div(base, 128) + 2 * i
        part[first] = out[0:128]
        part[first + 1] = out[128:256]

    loop(2, lambda i: input_rows(far, i))
    sums = scatters(rs, rr)
    all_of(sums, "begin")

    loop(2, lambda i: input_rows(near, i))
    gvec[:, 0:1024] = gvec[:, 0:1024] / gain1

    def tell(k):
        src, dev = (
            lambda: (gvec, head.dev(1, 0)),
            lambda: (gsum.at[0], head.dev(0, 1)),
            lambda: (gsum.at[0], head.dev(0, -1)),
            lambda: (gin.at[1], head.dev(0, 1)),
            lambda: (gsum.at[1], blk.sibling()),
            lambda: (gsum.at[2], blk.dev(1, 0)),
            lambda: (gsum.at[3], blk.dev(0, 1)),
            lambda: (gsum.at[3], blk.dev(0, -1)),
            lambda: (gin.at[6], blk.dev(0, 1)),
        )[k]()
        return remote(src, gin.at[k], gns.at[k], gnr.at[k], dev)

    def gather_gains(target, source, *ks):
        value = source[...]
        for k in ks:
            value = value + gin[k]
        gsum[target] = value

    tell(0).start()
    loop(4, key_value_grads)
    tell(0).wait_recv()
    gather_gains(0, gvec, 0)
    tell(1).start()
    tell(2).start()
    vscatter = BlkScatter(blk, vpart, vboth, vbufs, qs_s, qr_r, qcs.at[0], qcr.at[0])
    vscatter.cross()
    all_of(sums, "opposite")
    tell(1).wait_recv()
    tell(3).start()
    vscatter.merge()
    vscatter.begin()
    tell(2).wait_recv()
    tell(3).wait_recv()
    gather_gains(1, gsum.at[0], 1, 2, 3)
    tell(4).start()
    all_of(sums, "late")
    tell(4).wait_recv()
    gather_gains(2, gsum.at[1], 4)
    tell(5).start()
    vscatter.opposite()
    tell(5).wait_recv()
    gather_gains(3, gsum.at[2], 5)
    tell(6).start()
    tell(7).start()
    vscatter.late()
    tell(6).wait_recv()
    tell(8).start()
    for q, item in enumerate(sums):
        item.end()
        rows = slice(size * q, size * q + size)
        _, input_part = norm_back(tok[rows, :].astype(F32), gain1, item.total())
        for i in range(4):
            cols = slice(256 * i, 256 * i + 256)
            mid_grad = accum[3, 128 * i + size * q : 128 * i + size * q + size, :]
            tokens_grad[rows, cols] = (mid_grad + input_part[:, cols]).astype(BF16)
    tell(7).wait_recv()
    tell(8).wait_recv()
    gather_gains(4, gsum.at[3], 6, 7, 8)
    place = blk.plane(0, 0)
    offset = blk.c * 64 + head.h * 8
    lane = block * 8 + head.h

    def turned(first, shift):
        return pltpu.roll(gsum[4, :, pl.ds(pl.multiple_of(first, 128), 128)], lax.rem(128 - shift, 128), 1)

    first_out[...] = turned(place * 128, offset)[:, 0:8]
    second_out[...] = turned(1024 + place * 128, offset)[:, 0:8]
    qn_out[...] = turned(2048, lane)[:, 0:1]
    kn_out[...] = turned(2176, lane)[:, 0:1]
    vscatter.end()
    vsum = vscatter.total()
    query_out[...] = vsum[:, 0:256]
    key_out[...] = vsum[:, 256:384]
    value_out[...] = vsum[:, 384:512]
    output_out[...] = vsum[:, 512:768]
    for k in range(9):
        tell(k).wait_send()


def hand_over_kernel(*refs):
    count = len(refs) // 2
    for i in range(count):
        refs[count + i][...] = refs[i][...]


def sems(*counts):
    return [pltpu.SemaphoreType.DMA((c,)) for c in counts]


def per_device(
    tokens, doc_starts, first_gain, query_weight, key_matrix, value_matrix, querynorm, keynorm,
    output_weight, second_gain, gate_weight, up_weight, down_weight, grad_out,
):
    freqs = np.tile(THETA ** (-np.arange(64, dtype=np.float64) / 64), 2).astype(np.float32)
    vm = pl.BlockSpec(memory_space=pltpu.VMEM)
    hbm = pl.BlockSpec(memory_space=pl.ANY)
    outs = [
        ((128, 1024), BF16), ((128, 1024), BF16), ((64, 256), F32), ((64, 128), F32), ((64, 128), F32),
        ((64, 256), F32), ((64, 384), F32), ((64, 384), F32), ((64, 384), F32),
        ((1, 8), F32), ((1, 8), F32), ((1, 1), F32), ((1, 1), F32), ((1024, 1024), BF16),
    ]
    scratch = [
        ((1024, 128), F32), ((1024, 128), F32),
        ((1024, 1920), BF16), ((1024, 1024), BF16), ((1024, 1024), BF16), ((1024, 1024), BF16), ((16384, 256), BF16),
        ((2, 1024, 128), BF16), ((1024, 128), BF16), ((1024, 256), F32), ((1024, 128), F32), ((4, 1024, 256), F32),
        ((1024, 256), BF16), ((512, 256), BF16), ((2, 1024, 256), BF16), ((2, 1024, 256), BF16), ((128, 1024), F32),
        ((8, 128, 1024), BF16), ((7, 128, 1024), BF16), ((8, 128, 1024), BF16), ((7, 128, 1024), BF16),
        ((1024, 1152), BF16), ((1024, 256), BF16), ((512, 256), BF16), ((2, 1024, 256), BF16),
        ((8, 2, 64, 1152), BF16), ((8, 64, 1152), BF16), ((7, 64, 1152), BF16),
        ((8, 2, 64, 768), BF16), ((8, 64, 768), BF16), ((7, 64, 768), BF16),
        ((2, 1024, 256), BF16), ((8, 1024, 256), BF16), ((7, 1024, 256), BF16), ((512, 256), BF16), ((512, 256), BF16),
        ((1, 2304), F32), ((9, 1, 2304), F32), ((5, 1, 2304), F32),
    ]
    counts = (11, 11, 8, 8, 11, 11, 8, 8, 4, 4, 8 * PARTS, 8 * PARTS, 11 * PARTS, 11 * PARTS, 11, 11)
    counts += (8, 8, 8, 8, 1, 1, 11, 11, 8, 8, 8, 8, 1, 1, 8, 8, 8, 8, 9, 9, 2)
    made = pl.pallas_call(
        layer_kernel,
        out_shape=[jax.ShapeDtypeStruct(s, d) for s, d in outs],
        in_specs=[pl.BlockSpec(memory_space=pltpu.SMEM)] + [vm] * 14,
        out_specs=[vm] * 13 + [hbm],
        scratch_shapes=[pltpu.VMEM(s, d) for s, d in scratch] + sems(*counts),
        compiler_params=pltpu.CompilerParams(vmem_limit_bytes=VMEM_LIMIT, collective_id=1, has_side_effects=True),
    )(
        doc_starts, tokens, grad_out, query_weight, key_matrix, value_matrix, output_weight.T, gate_weight, up_weight,
        down_weight.T, first_gain.reshape(8, 128), second_gain.reshape(8, 128), querynorm[None, :], keynorm[None, :], freqs[None, :],
    )
    made = pl.pallas_call(
        hand_over_kernel,
        out_shape=[jax.ShapeDtypeStruct(s, d) for s, d in outs[:13]],
        in_specs=[vm] * 13,
        out_specs=[vm] * 13,
    )(*made[:13])
    layer_out, tokens_grad, query, key, value, output, gate, up, down, first, second, qn, kn = made
    return (
        layer_out, tokens_grad, first.reshape(8), query, key, value, qn.reshape(1), kn.reshape(1),
        output.T, second.reshape(8), gate, up, down.T,
    )


def solution(mesh):
    return jax.shard_map(
        per_device,
        mesh=mesh,
        in_specs=(
            P(("blk", "head"), None),
            P(),
            P(),
            P("blk", "head"),
            P("blk", "head"),
            P("blk", "head"),
            P(),
            P(),
            P("head", "blk"),
            P(),
            P("blk", "head"),
            P("blk", "head"),
            P("head", "blk"),
            P(("blk", "head"), None),
        ),
        out_specs=(
            P(("blk", "head"), None),
            P(("blk", "head"), None),
            P(("blk", "head")),
            P("blk", "head"),
            P("blk", "head"),
            P("blk", "head"),
            P(("blk", "head")),
            P(("blk", "head")),
            P("head", "blk"),
            P(("blk", "head")),
            P("blk", "head"),
            P("blk", "head"),
            P("head", "blk"),
        ),
        check_vma=False,
    )
```

```python
import functools

import jax
import jax.numpy as jnp
from jax import lax
from jax.experimental import pallas as pl
from jax.experimental.pallas import tpu as pltpu
import numpy as np
from jax.sharding import PartitionSpec as P

EPS = 1e-06
THETA = 1000000.0
MESH = pl.DeviceIdType.MESH
F32 = jnp.float32
BF16 = jnp.bfloat16
LOG2E = 1.4426950408889634
LN2 = 0.6931471805599453
HEAD_DIM = 128
PARTS = 2
SCALE = HEAD_DIM**-0.5
VMEM_LIMIT = 64 * 2**20 - 2**16

QC, KC, VC, OC, GC, UC, DC, END = 0, 256, 384, 512, 768, 1152, 1536, 1920


def nn(a, b):
    return jnp.dot(a, b, preferred_element_type=F32)


def nt(a, b):
    return lax.dot_general(a, b, (((1,), (1,)), ((), ())), preferred_element_type=F32)


def tn(a, b):
    return lax.dot_general(a, b, (((0,), (0,)), ((), ())), preferred_element_type=F32)


def chunk(i, size):
    return pl.ds(pl.multiple_of(i * size, size), size)


def loop(count, body):
    def step(i, carry):
        body(i)
        return carry

    lax.fori_loop(0, count, step, 0)


def run_all(*actions):
    def run():
        for action in actions:
            action()

    return run


def when(condition, action):
    def run():
        action()

    pl.when(condition)(run)


class HeadRing:
    def __init__(self):
        self.b = lax.axis_index("blk")
        h = lax.axis_index("head")
        self.h = h
        self.p, self.r = lax.div(h, 4), lax.rem(h, 4)

    def plane(self, dp, dr):
        return lax.rem(self.p + dp, 2) * 4 + lax.rem(self.r + dr + 4, 4)

    slot = plane

    def dev(self, dp, dr):
        return (self.b, self.plane(dp, dr))

    def near(self):
        return [self.dev(1, 0), self.dev(0, 1), self.dev(0, -1)]


class BlkRing:
    def __init__(self):
        b = lax.axis_index("blk")
        self.h = lax.axis_index("head")
        self.b = b
        self.p, self.r, self.c = lax.div(b, 8), lax.rem(lax.div(b, 2), 4), lax.rem(b, 2)

    def plane(self, dp, dr):
        return lax.rem(self.p + dp, 2) * 4 + lax.rem(self.r + dr + 4, 4)

    def slot(self, dp, dr, dc=0):
        return self.plane(dp, dr) * 2 + lax.rem(self.c + dc, 2)

    def dev(self, dp, dr, dc=0):
        return (self.slot(dp, dr, dc), self.h)

    def sibling(self):
        return self.dev(0, 0, 1)

    def mirror(self):
        return (15 - self.b, self.h)

    def near(self):
        return [self.dev(1, 0), self.dev(0, 1), self.dev(0, -1)]


def greet(devices):
    for d in devices:
        pl.semaphore_signal(pltpu.get_barrier_semaphore(), inc=1, device_id=d, device_id_type=MESH)


def remote(src, dst, ss, rs, dev):
    return pltpu.make_async_remote_copy(
        src_ref=src, dst_ref=dst, send_sem=ss, recv_sem=rs, device_id=dev, device_id_type=MESH
    )


class Gather:
    ORDER = ((0, 0), (1, 0), (0, -1), (0, 1), (0, 2), (1, -1), (1, 1), (1, 2))

    def __init__(self, ring, full, n, ss, rs, sib=None, on_ring=False, off=0, stride=None, k0=0):
        self.ring, self.full, self.n, self.ss, self.rs, self.sib = ring, full, n, ss, rs, sib
        self.on_ring, self.off, self.stride, self.k0 = on_ring, off, stride or n, k0

    def rows(self, dp, dr, part=None):
        base = self.ring.slot(dp, dr) * self.stride + self.off
        size = self.n
        if part is not None:
            size = self.n // 2
            base = base + part * size
        return self.full.at[pl.ds(pl.multiple_of(base, size), size)]

    def copy(self, k):
        ring, rows = self.ring, self.rows
        ref, dev = (
            lambda: (rows(0, 0), ring.dev(1, 0)),
            lambda: (rows(0, 0, 0), ring.dev(0, 1)),
            lambda: (rows(0, 0, 1), ring.dev(0, -1)),
            lambda: (rows(0, 0, 1), ring.dev(0, 1)),
            lambda: (rows(0, 0, 0), ring.dev(0, -1)),
            lambda: (rows(0, -1, 0), ring.dev(0, 1)),
            lambda: (rows(0, 1, 1), ring.dev(0, -1)),
            lambda: (rows(1, 0), ring.dev(0, 1)),
            lambda: (rows(1, 0), ring.dev(0, -1)),
            lambda: (rows(1, -1, 0), ring.dev(0, 1)) if self.on_ring else (rows(0, 2, 0), ring.dev(1, 0)),
            lambda: (rows(1, 1, 1), ring.dev(0, -1)) if self.on_ring else (rows(0, 2, 1), ring.dev(1, 0)),
        )[k]()
        return remote(ref, ref, self.ss.at[self.k0 + k], self.rs.at[self.k0 + k], dev)

    def send(self, *ks):
        for k in ks:
            self.copy(k).start()

    def wait(self, *ks):
        for k in ks:
            self.copy(k).wait_recv()

    def crossing(self, dp, dr):
        k = self.ORDER.index((dp, dr))
        ref = self.rows(dp, dr)
        return remote(ref, ref, self.sib[0].at[k], self.sib[1].at[k], self.ring.sibling())

    def cross(self, *which):
        if self.sib is not None:
            for w in which:
                self.crossing(*w).start()

    def crossed(self, *which):
        if self.sib is not None:
            for w in which:
                self.crossing(*w).wait_recv()

    def begin(self):
        self.send(1, 2, 0, 3, 4)
        self.cross((0, 0))

    def travel(self):
        self.wait(1)
        self.send(5)
        self.wait(2)
        self.send(6)

    def pair_on(self):
        self.wait(0)
        self.send(7, 8)
        self.cross((1, 0))

    def step1(self):
        self.travel()
        self.pair_on()

    def opposite_on(self):
        self.wait(5)
        if not self.on_ring:
            self.send(9)
        self.wait(6)
        if not self.on_ring:
            self.send(10)
        self.cross((0, 2))

    def ring_done(self):
        self.wait(3, 4)
        self.cross((0, -1), (0, 1))

    def step2(self):
        self.opposite_on()
        self.ring_done()

    def step3(self):
        self.wait(7)
        if self.on_ring:
            self.send(9)
        self.wait(8)
        if self.on_ring:
            self.send(10)
        self.cross((1, -1), (1, 1))

    def step4(self):
        self.wait(9, 10)
        self.cross((1, 2))

    def end(self):
        for k in range(11):
            self.copy(k).wait_send()
        if self.sib is not None:
            for w in self.ORDER:
                self.crossing(*w).wait_send()

    def finish(self):
        self.crossed(*self.ORDER)
        self.end()

    def steps(self):
        return [self.begin, self.step1, self.step2, self.step3, self.step4, self.finish]


class Scatter:
    def __init__(self, ring, part, bufs, ss, rs, off=0, n=None, k0=0):
        self.ring, self.part, self.bufs, self.ss, self.rs = ring, part, bufs, ss, rs
        self.off, self.n, self.k0 = off, n or part.shape[1], k0

    def span(self, half):
        if half is None:
            return pl.ds(self.off, self.n)
        return pl.ds(self.off + half * (self.n // 2), self.n // 2)

    def own(self, dp, dr, half=None):
        return self.part.at[self.ring.plane(dp, dr), self.span(half)]

    def buf(self, i, half=None):
        return self.bufs.at[i, self.span(half)]

    def copy(self, k):
        ring, own, buf = self.ring, self.own, self.buf
        src, dst, dev = (
            lambda: (own(1, 2), buf(0), ring.dev(1, 0)),
            lambda: (own(1, 1), buf(1), ring.dev(0, 1)),
            lambda: (own(1, -1), buf(2), ring.dev(0, -1)),
            lambda: (own(0, 2, 0), buf(6, 0), ring.dev(0, 1)),
            lambda: (own(0, 2, 1), buf(6, 1), ring.dev(0, -1)),
            lambda: (own(1, 0), buf(3), ring.dev(1, 0)),
            lambda: (own(0, 1), buf(4), ring.dev(0, 1)),
            lambda: (own(0, -1), buf(5), ring.dev(0, -1)),
        )[k]()
        return remote(src, dst, self.ss.at[self.k0 + k], self.rs.at[self.k0 + k], dev)

    def send(self, *ks):
        for k in ks:
            self.copy(k).start()

    def wait(self, *ks):
        for k in ks:
            self.copy(k).wait_recv()

    def add(self, dst, *srcs):
        value = dst[...].astype(F32)
        for src in srcs:
            value = value + src[...].astype(F32)
        dst[...] = value.astype(dst.dtype)

    def begin(self):
        self.send(1, 2, 0)

    def opposite(self):
        self.wait(0)
        self.add(self.own(0, 2), self.buf(0))
        self.send(3, 4)

    def home(self):
        self.wait(1, 2)
        self.add(self.own(1, 0), self.buf(1), self.buf(2))
        self.send(5)

    def up(self):
        self.wait(3)
        self.add(self.own(0, 1, 0), self.buf(6, 0))
        self.send(6)

    def down(self):
        self.wait(4)
        self.add(self.own(0, -1, 1), self.buf(6, 1))
        self.send(7)

    def end(self):
        self.wait(5, 6, 7)
        for k in range(8):
            self.copy(k).wait_send()

    def late(self):
        self.up()
        self.down()
        self.home()

    def total(self):
        out = self.own(0, 0)[...].astype(F32)
        for i in (3, 4, 5):
            out = out + self.buf(i)[...].astype(F32)
        return out


class BlkScatter(Scatter):
    def __init__(self, ring, terms, part, bufs, ss, rs, cs, cr):
        super().__init__(ring, part, bufs, ss, rs)
        self.terms, self.cs, self.cr = terms, cs, cr

    def crossing(self):
        return remote(self.terms.at[:, 1 - self.ring.c], self.part, self.cs, self.cr, self.ring.sibling())

    def cross(self):
        self.crossing().start()

    def merge(self):
        self.crossing().wait_recv()

        def body(k):
            self.part[k] = (self.part[k].astype(F32) + self.terms[k, self.ring.c].astype(F32)).astype(BF16)

        loop(8, body)
        self.crossing().wait_send()


def weave(*lists):
    for i in range(max(len(item) for item in lists)):
        for item in lists:
            if i < len(item):
                item[i]()


def rope(v, cosine, sine):
    return v * cosine + pltpu.roll(v, 64, 1) * sine


def rope_back(g, cosine, sine):
    return g * cosine + pltpu.roll(g * sine, 64, 1)


def inverse(v):
    return lax.rsqrt(jnp.mean(v * v, axis=-1, keepdims=True) + EPS)


def norm_back(v, gain, grad):
    r = inverse(v)
    n = v * r
    scaled = grad * gain
    return grad * n, r * (scaled - n * jnp.mean(scaled * n, axis=-1, keepdims=True))


def split3(v):
    a = (-v).astype(BF16).astype(F32)
    rest = -v - a
    b = rest.astype(BF16).astype(F32)
    lane = lax.broadcasted_iota(jnp.int32, v.shape, 1)
    return jnp.where(lane == 0, a, jnp.where(lane == 1, b, jnp.where(lane == 2, rest - b, 0.0)))


def begin_of(starts, index):
    begin = jnp.zeros_like(index)
    for k in range(1, 4):
        begin = jnp.where(index >= starts[k], starts[k], begin)
    return begin


def pick(index, values):
    out = jnp.int32(values[-1])
    for k in range(len(values) - 2, -1, -1):
        out = jnp.where(index == k, jnp.int32(values[k]), out)
    return out


def layer_kernel(
    starts, tok, dy, wq, wk, wv, wo, wg, wu, wd, gain_one, gain_two, gain_q, gain_k, freqs,
    layer_out, tokens_grad, query_out, key_out, value_out, output_out, gate_out, up_out, down_out,
    first_out, second_out, qn_out, kn_out, saved,
    cosine, sine, weights, block_a, block_b, block_dy, kv, qs, qsend, qraw, kraw, accum, ctx, ctxb, qx, qfar, middle,
    part, bufs, ffpart, ffbufs, acts, grad_all, grad_far, dox, wpart, wboth, wbufs, vpart, vboth, vbufs,
    xs, kvboth, kvbufs, dqsend, dqhome, gvec, gin, gsum,
    ws, wr, wcs, wcr, ks, kr, kcs, kcr, ms, mr, rs, rr, gs, gr, ds_, dr_,
    fs, fr, vs, vr, vcs, vcr, w2s, w2r, w2cs, w2cr, qs_s, qr_r, qcs, qcr, xss, xrr, xcs, xcr, gns, gnr, local,
):
    head, blk = HeadRing(), BlkRing()
    partners = head.near() + blk.near() + [blk.sibling(), blk.mirror()]
    greet(partners)
    block = blk.b

    def line(ref):
        value = ref[...].astype(F32)
        return jnp.concatenate([value[i : i + 1] for i in range(8)], axis=1)

    gain1, gain2 = line(gain_one), line(gain_two)
    qgain, kgain = gain_q[...].astype(F32), gain_k[...].astype(F32)
    x = tok[...].astype(F32)
    block_a[chunk(head.slot(0, 0), 128), :] = (x * inverse(x) * gain1).astype(BF16)
    mine = chunk(blk.slot(0, 0), 64)
    for ref, first in ((wq, QC), (wk, KC), (wv, VC), (wo, OC), (wg, GC), (wu, UC), (wd, DC)):
        weights[mine, first : first + ref.shape[1]] = ref[...]
    block_dy[chunk(head.slot(0, 0), 128), :] = dy[...]
    pl.semaphore_wait(pltpu.get_barrier_semaphore(), len(partners))
    wone = Gather(blk, weights.at[:, QC:GC], 64, ws, wr, (wcs, wcr))
    wtwo = Gather(blk, weights.at[:, GC:END], 64, w2s, w2r, (w2cs, w2cr), on_ring=True)
    normed = Gather(head, block_a, 128, gs, gr)
    normed.begin()
    wone.begin()
    wtwo.begin()
    for i in range(4):
        at = slice(256 * i, 256 * i + 256)
        index = block * 1024 + 256 * i + lax.broadcasted_iota(jnp.int32, (256, 1), 0)
        angle = (index - begin_of(starts, index)).astype(F32) * freqs[...]
        lane = lax.broadcasted_iota(jnp.int32, (256, 128), 1)
        cosine[at, :] = jnp.cos(angle)
        turn = jnp.sin(angle)
        sine[at, :] = jnp.where(lane < 64, -turn, turn)
    normed.step1()
    wone.step1()
    wtwo.step1()
    normed.step2()
    for step in (wone.step2, wone.step3, wone.step4, wtwo.step2, wone.finish):
        step()

    base = pl.multiple_of(block * 1024, 1024)
    far, near = pl.multiple_of((1 - head.p) * 512, 512), pl.multiple_of(head.p * 512, 512)

    def query_rows(base, dst):
        for i in range(2):
            at = pl.ds(pl.multiple_of(base + 256 * i, 256), 256)
            out = nn(block_a[at, :], weights[:, QC:KC])
            for k in range(2):
                v = out[:, 128 * k : 128 * k + 128]
                qraw[at, 128 * k : 128 * k + 128] = v
                v = rope(v * inverse(v) * qgain, cosine[at, :], sine[at, :]) * (SCALE * LOG2E)
                dst[512 * k + 256 * i : 512 * k + 256 * i + 256, :] = v.astype(BF16)

    def keys_rows(first, i):
        at = pl.ds(pl.multiple_of(first + i * 256, 256), 256)
        out = nn(block_a[at, :], weights[:, KC:OC])
        v = out[:, 0:128]
        kraw[at, :] = v
        to = pl.ds(pl.multiple_of(base + first + i * 256, 256), 256)
        kv[to, 0:128] = rope(v * inverse(v) * kgain, cosine[at, :], sine[at, :]).astype(BF16)
        kv[to, 128:256] = out[:, 128:256].astype(BF16)

    query_rows(near, qsend)
    qswap = remote(qsend, qs.at[1], ms.at[0], mr.at[0], blk.mirror())
    qswap.start()
    loop(2, lambda i: keys_rows(near, i))
    wtwo.step3()
    for step in (normed.step3, normed.step4, normed.finish):
        step()
    keep = pltpu.make_async_copy(block_a, saved, local.at[0])
    keep.start()
    loop(2, lambda i: keys_rows(far, i))
    kvgather = Gather(blk, kv, 1024, ks, kr, (kcs, kcr))
    kvgather.send(1, 2, 0)
    kvgather.cross((0, 0))
    query_rows(far, qs.at[0])
    dygather = Gather(head, block_dy, 128, ds_, dr_, on_ring=True)
    dygather.begin()

    def clear(i):
        accum[i] = jnp.zeros((1024, 256), F32)

    loop(4, clear)
    ones = jnp.ones((1024, 128), BF16)

    def limit_of(side):
        return jnp.where(side == 0, block, 15 - block)

    def half_of(side):
        return jnp.where(side == 0, 2 * block + 1 - head.p, 30 - 2 * block + head.p)

    def mask(side, jb, c, rows, transposed):
        first = half_of(side) * 512 + lax.rem(c * rows, 512)
        shape_q, shape_k = ((1, rows), (1024, 1)) if transposed else ((rows, 1), (1, 1024))
        qi = first + lax.broadcasted_iota(jnp.int32, shape_q, 1 if transposed else 0)
        ki = jb * 1024 + lax.broadcasted_iota(jnp.int32, shape_k, 0 if transposed else 1)
        return (ki >= begin_of(starts, qi)) & (ki <= qi)

    def attend(sides, jb, masked):
        at = chunk(jb, 1024)
        keys = kv[at, 0:128]
        values = jnp.concatenate([kv[at, 128:256], ones], axis=1)
        for side in sides:
            row = 2 * side + masked
            for c in range(4):
                rows = slice(c * 256, c * 256 + 256)
                p = jnp.exp2(nt(qs[side, rows, :], keys))
                if masked:
                    p = jnp.where(mask(side, jb, c, 256, False), p, 0.0)
                accum[row, rows, :] += nn(p.astype(BF16), values)

    def work(jb, unit):
        def one(side):
            limit = limit_of(side)
            careful = (jb == 0) | (jb == limit)
            when((jb <= limit) & jnp.logical_not(careful), lambda: unit((side,), jb, False))
            when((jb <= limit) & careful, lambda: unit((side,), jb, True))

        loop(2, one)

    order0 = ((0, 0), (0, 2), (1, 0), (0, -1), (0, 1), (1, 2), (1, -1), (1, 1))
    order1 = ((0, 0), (1, 0), (0, 2), (1, -1), (1, 1), (1, 2), (0, -1), (0, 1))
    g = kvgather
    every_step = {
        0: qswap.wait_recv,
        1: lambda: (g.crossed((0, 0)), g.travel()),
        4: lambda: (dygather.step1(), wtwo.step4()),
        7: dygather.step2,
        10: dygather.step3,
    }
    step_p0 = {
        2: lambda: (g.opposite_on(), g.send(3, 4), g.wait(0), g.cross((1, 0))),
        6: lambda: (g.ring_done(), g.send(7, 8)),
        10: g.step4,
        12: lambda: (g.wait(7, 8), g.cross((1, -1), (1, 1))),
    }
    step_p1 = {
        2: lambda: (g.pair_on(), g.opposite_on()),
        6: lambda: (g.wait(7, 8), g.cross((1, -1), (1, 1)), g.send(3, 4)),
        8: g.step4,
        12: g.ring_done,
    }
    for i in range(1, 8):
        for steps, order in ((step_p0, order0), (step_p1, order1)):
            steps[2 * i + 1] = functools.partial(g.crossed, order[i])

    def along(s, first, second):
        return tuple(
            jnp.where(blk.p == 0, pick(s, [d[i] for d in first]), pick(s, [d[i] for d in second])) for i in range(2)
        )

    def attend_step(t):
        s, core = lax.div(t, 2), lax.rem(t, 2)
        jb = blk.slot(*along(s, order0, order1), core)
        for k, action in step_p0.items():
            when((t == k) & (blk.p == 0), action)
        for k, action in step_p1.items():
            when((t == k) & (blk.p == 1), action)
        for k, action in every_step.items():
            when(t == k, action)
        work(jb, attend)

    loop(16, attend_step)

    def context_of(side, dst):
        for k in range(2):
            rows = slice(512 * k, 512 * k + 512)
            qi = half_of(side) * 512 + lax.broadcasted_iota(jnp.int32, (512, 1), 0)
            here = qi < starts[2]
            both = accum[2 * side + 1, rows, :] + jnp.where(here, accum[2 * side, rows, :], 0.0)
            dst[:, 128 * k : 128 * k + 128] = (both[:, 0:128] / both[:, 128:256]).astype(BF16)
            accum[2 * side, rows, 0:128] = both[:, 128:256]

    def extend(side):
        for k in range(2):
            rows = slice(512 * k, 512 * k + 512)
            terms = split3(jnp.log2(accum[2 * side, rows, 0:128]))
            qi = half_of(side) * 512 + lax.broadcasted_iota(jnp.int32, (512, 128), 0)
            lane = lax.broadcasted_iota(jnp.int32, (512, 128), 1)
            gone = jnp.where(lane == 0, -1e30, 0.0)
            qx[side, rows, 0:128] = qs[side, rows, :]
            qx[side, rows, 128:256] = terms.astype(BF16)
            qfar[side, rows, 0:128] = qs[side, rows, :]
            qfar[side, rows, 128:256] = jnp.where(qi < starts[2], terms, gone).astype(BF16)

    context_of(1, ctxb)
    near_ctx, far_ctx = ctx.at[pl.ds(near, 512)], ctx.at[pl.ds(far, 512)]
    cswap = remote(ctxb, near_ctx, ms.at[1], mr.at[1], blk.mirror())
    cswap.start()
    context_of(0, far_ctx)

    def output_rows(base, i):
        at = pl.ds(pl.multiple_of(base + i * 256, 256), 256)
        out = nt(ctx[at, :], weights[:, OC:GC]).astype(BF16)
        first = lax.div(base, 128) + 2 * i
        part[first] = out[0:128]
        part[first + 1] = out[128:256]

    size = 128 // PARTS

    def scatters(ss, rs):
        return [Scatter(head, part, bufs, ss, rs, off=size * q, n=size, k0=8 * q) for q in range(PARTS)]

    def gathers(full, ss, rs):
        return [Gather(head, full, size, ss, rs, off=size * q, stride=128, k0=11 * q) for q in range(PARTS)]

    def all_of(items, *names):
        for name in names:
            for item in items:
                getattr(item, name)()

    loop(2, lambda i: output_rows(far, i))
    sums = scatters(rs, rr)
    all_of(sums, "begin")
    dygather.step4()
    extend(1)
    cswap.wait_recv()
    loop(2, lambda i: output_rows(near, i))
    all_of(sums, "opposite")
    extend(0)
    dygather.end()
    shards = gathers(block_b, gs, gr)
    own = pl.multiple_of(head.slot(0, 0) * 128, 128)
    all_of(sums, "late")
    for q, (item, collect) in enumerate(zip(sums, shards)):
        item.end()
        rows = slice(size * q, size * q + size)
        mid = tok[rows, :].astype(F32) + item.total()
        middle[rows, :] = mid
        block_b[pl.ds(own + size * q, size), :] = (mid * inverse(mid) * gain2).astype(BF16)
        collect.begin()
    qswap.wait_send()
    cswap.wait_send()
    kvgather.end()
    wtwo.finish()
    keep.wait()
    all_of(shards, "step1", "step2")

    def forward_rows(base, i):
        at = pl.ds(pl.multiple_of(base + i * 256, 256), 256)
        both = nn(block_b[at, :], weights[:, GC:DC])
        gate, upper = both[:, 0:384], both[:, 384:768]
        sigma = 1.0 / (1.0 + jnp.exp(-gate))
        silu = gate * sigma
        act_grad = nn(block_dy[at, :], weights[:, DC:END])
        gate_low = (act_grad * upper * sigma * (1.0 + gate * (1.0 - sigma))).astype(BF16)
        low = jnp.concatenate([gate_low, (act_grad * silu).astype(BF16)], axis=1)
        acts[at, 0:768] = low
        acts[at, 768:1152] = (silu * upper).astype(BF16)
        out = nt(low, weights[:, GC:DC]).astype(BF16)
        first = lax.div(base, 128) + 2 * i
        part[first] = out[0:128]
        part[first + 1] = out[128:256]

    loop(2, lambda i: forward_rows(near, i))
    all_of(shards, "step3", "step4", "finish")
    loop(2, lambda i: forward_rows(far, i))
    sums = scatters(rs, rr)
    all_of(sums, "begin")

    def down_rows(i):
        out = nt(acts[chunk(i, 256), 768:1152], weights[:, DC:END]).astype(BF16)
        ffpart[2 * i] = out[0:128]
        ffpart[2 * i + 1] = out[128:256]

    loop(4, down_rows)
    all_of(sums, "opposite")

    def put_terms(i, out, cols):
        for k in range(2):
            wpart[2 * i + k, 0, :, cols] = out[128 * k : 128 * k + 64]
            wpart[2 * i + k, 1, :, cols] = out[128 * k + 64 : 128 * k + 128]

    def gate_up_grads(i):
        put_terms(i, tn(block_b[:, chunk(i, 256)], acts[:, 0:768]).astype(BF16), slice(0, 768))

    loop(2, gate_up_grads)
    all_of(sums, "late")
    loop(2, lambda i: gate_up_grads(i + 2))
    shards = gathers(block_a, gs, gr)
    gvec[:, 1024:2048] = jnp.zeros((1, 1024), F32)
    for q, (item, collect) in enumerate(zip(sums, shards)):
        item.end()
        rows = slice(size * q, size * q + size)
        terms, part_grad = norm_back(middle[rows, :], gain2, item.total())
        mid_grad = dy[rows, :].astype(F32) + part_grad
        block_a[pl.ds(own + size * q, size), :] = mid_grad.astype(BF16)
        collect.begin()
        gvec[:, 1024:2048] += jnp.sum(terms, axis=0, keepdims=True)
        for i in range(4):
            accum[3, 128 * i + size * q : 128 * i + size * q + size, :] = mid_grad[:, 256 * i : 256 * i + 256]

    def down_grads(i):
        put_terms(i, tn(block_dy[:, chunk(i, 256)], acts[:, 768:1152]).astype(BF16), slice(768, 1152))

    loop(2, down_grads)
    all_of(shards, "step1", "step2")
    def context_grads(base, i):
        at = pl.ds(pl.multiple_of(base + 256 * i, 256), 256)
        grad_all[at, :] = nn(block_a[at, :], weights[:, OC:GC]).astype(BF16)

    loop(2, lambda i: context_grads(near, i))
    gswap = remote(grad_all.at[pl.ds(near, 512)], grad_far, ms.at[2], mr.at[2], blk.mirror())
    gswap.start()
    loop(2, lambda i: down_grads(i + 2))
    all_of(shards, "step3", "step4", "finish")

    loop(2, lambda i: context_grads(far, i))
    reload = pltpu.make_async_copy(saved, block_b, local.at[1])
    reload.start()
    ffscatter = Scatter(head, ffpart, ffbufs, fs, fr)
    wscatter = BlkScatter(blk, wpart, wboth, wbufs, vs, vr, vcs.at[0], vcr.at[0])
    ffscatter.begin()
    wscatter.cross()

    def extend_grad(side, grads, context):
        for k in range(2):
            rows, cols = slice(512 * k, 512 * k + 512), slice(128 * k, 128 * k + 128)
            grad = grads[0:512, cols]
            delta = jnp.sum(grad.astype(F32) * context[0:512, cols].astype(F32), axis=1, keepdims=True)
            dox[side, rows, 0:128] = grad
            dox[side, rows, 128:256] = split3(jnp.broadcast_to(delta, (512, 128))).astype(BF16)

    extend_grad(0, grad_all.at[pl.ds(far, 512)], far_ctx)
    loop(2, lambda i: clear(i))

    back0 = ((1, 2), (1, 1), (1, -1), (1, 0), (0, 1), (0, 2), (0, -1), (0, 0))
    back1 = ((1, 2), (0, 2), (0, 1), (0, -1), (1, 1), (1, -1), (1, 0), (0, 0))

    def attend_back(sides, jb, masked):
        at = chunk(jb, 1024)
        keys = kv[at, 0:128]
        kx = jnp.concatenate([keys, ones], axis=1)
        vx = jnp.concatenate([kv[at, 128:256], ones], axis=1)
        source = qx if masked else qfar
        for side in sides:
            for c in range(4):
                rows = slice(c * 256, c * 256 + 256)
                p = jnp.exp2(nt(kx, source[side, rows, :]))
                if masked:
                    p = jnp.where(mask(side, jb, c, 256, True), p, 0.0)
                ds = (p * nt(vx, dox[side, rows, :])).astype(BF16)
                accum[0, :, 0:128] += nn(ds, source[side, rows, 0:128])
                accum[0, :, 128:256] += nn(p.astype(BF16), dox[side, rows, 0:128])
                accum[1, chunk(4 * side + c, 128), :] += tn(keys, ds)

    kvscatter = Scatter(blk, kvboth, kvbufs, xss, xrr)

    def crossing(s):
        return remote(xs.at[s % 2], kvboth.at[blk.plane(*along(s, back0, back1))], xcs.at[s], xcr.at[s], blk.sibling())

    sc = kvscatter
    actions0 = {
        0: lambda: sc.send(0), 1: lambda: sc.send(1), 2: lambda: sc.send(2), 4: sc.home, 5: sc.opposite,
        6: lambda: (sc.up(), sc.down()),
    }
    actions1 = {
        0: lambda: sc.send(0), 3: sc.opposite, 4: lambda: (sc.send(1), sc.up(), sc.down()), 5: lambda: sc.send(2),
        6: sc.home,
    }
    others = {
        0: lambda: (wscatter.merge(), wscatter.begin()),
        2: lambda: (wscatter.opposite(), ffscatter.opposite()),
        4: lambda: (wscatter.up(), wscatter.down(), wscatter.home(), ffscatter.up(), ffscatter.down(), ffscatter.home()),
        6: lambda: (wscatter.end(), ffscatter.end()),
    }

    def reached(plane):
        even = block - blk.c
        return 2 * plane <= jnp.maximum(even + 1, 15 - even)

    def plane_at(s):
        return blk.plane(*along(s, back0, back1))

    def back_step(t):
        s, core = lax.div(t, 2), 1 - lax.rem(t, 2)
        plane = plane_at(s)
        jb = plane * 2 + lax.rem(blk.c + core, 2)
        some = reached(plane)

        def compute():
            accum[0] = jnp.zeros((1024, 256), F32)
            when(t == 0, lambda: (gswap.wait_recv(), extend_grad(1, grad_far, ctxb)))
            work(jb, attend_back)

        when(some | (t == 0), compute)
        for i in range(8):

            def out(i=i):
                if i >= 2:
                    when(reached(plane_at(i - 2)), lambda: crossing(i - 2).wait_send())

                def give():
                    xs[i % 2] = accum[0].astype(BF16)
                    crossing(i).start()

                when(some, give)
                if i in others:
                    others[i]()

            def merge(i=i):
                def take():
                    crossing(i).wait_recv()
                    kvboth[plane] = (kvboth[plane].astype(F32) + accum[0]).astype(BF16)

                def none():
                    kvboth[plane] = jnp.zeros((1024, 256), BF16)

                when(some, take)
                when(jnp.logical_not(some), none)

            when(t == 2 * i, out)
            when(t == 2 * i + 1, merge)
            for p, actions in enumerate((actions0, actions1)):
                if i in actions:
                    when((t == 2 * i + 1) & (blk.p == p), actions[i])

    loop(16, back_step)
    for i in (6, 7):
        when(reached(plane_at(i)), crossing(i).wait_send)

    def dq_of(side, k, i):
        first = 128 * (4 * side + 2 * k + i)
        return jnp.transpose(accum[1, first : first + 128, :]) * SCALE

    for k in range(2):
        for i in range(2):
            dqsend[256 * i : 256 * i + 256, 128 * k : 128 * k + 128] = dq_of(1, k, i).astype(BF16)
    dswap = remote(dqsend, dqhome, ms.at[3], mr.at[3], blk.mirror())
    dswap.start()
    reload.wait()
    gswap.wait_send()
    gvec[:, 2048:2304] = jnp.zeros((1, 256), F32)

    def back(raw, grad, at, gains):
        return norm_back(raw, gains, rope_back(grad, cosine[at, :], sine[at, :]))

    def query_back(base, i, grads):
        at = pl.ds(pl.multiple_of(base + 256 * i, 256), 256)
        for k in range(2):
            cols = slice(128 * k, 128 * k + 128)
            terms, out = back(qraw[at, cols], grads(i, k), at, qgain)
            acts[at, cols] = out.astype(BF16)
            gvec[:, 2048:2176] += jnp.sum(terms, axis=0, keepdims=True)

    def put_vterms(i, out, cols):
        for k in range(2):
            vpart[2 * i + k, 0, :, cols] = out[128 * k : 128 * k + 64]
            vpart[2 * i + k, 1, :, cols] = out[128 * k + 64 : 128 * k + 128]

    def output_grads(i):
        put_vterms(i, tn(block_a[:, chunk(i, 256)], ctx[...]).astype(BF16), slice(512, 768))

    def query_grads(i):
        put_vterms(i, tn(block_b[:, chunk(i, 256)], acts[:, 0:256]).astype(BF16), slice(0, 256))

    def key_value_grads(i):
        put_vterms(i, tn(block_b[:, chunk(i, 256)], acts[:, 256:512]).astype(BF16), slice(256, 512))

    for i in range(2):
        query_back(far, i, lambda i, k: dq_of(0, k, i))
    loop(4, output_grads)
    layer_out[...] = (middle[...] + ffscatter.total()).astype(BF16)
    wsum = wscatter.total()
    gate_out[...] = wsum[:, 0:384]
    up_out[...] = wsum[:, 384:768]
    down_out[...] = wsum[:, 768:1152]
    dswap.wait_recv()
    for i in range(2):
        query_back(near, i, lambda i, k: dqhome[256 * i : 256 * i + 256, 128 * k : 128 * k + 128].astype(F32))
    loop(4, query_grads)
    kvscatter.end()
    accum[2] = kvscatter.total()

    def key_back(i):
        at = slice(256 * i, 256 * i + 256)
        terms, out = back(kraw[at, :], accum[2, at, 0:128] * LN2, at, kgain)
        acts[at, 256:384] = out.astype(BF16)
        gvec[:, 2176:2304] += jnp.sum(terms, axis=0, keepdims=True)
        acts[at, 384:512] = accum[2, at, 128:256].astype(BF16)

    for i in range(4):
        key_back(i)
    dswap.wait_send()

    gvec[:, 0:1024] = jnp.zeros((1, 1024), F32)

    def input_rows(base, i):
        at = pl.ds(pl.multiple_of(base + i * 256, 256), 256)
        out = nt(acts[at, 0:512], weights[:, QC:OC])
        gvec[:, 0:1024] += jnp.sum(out * block_b[at, :].astype(F32), axis=0, keepdims=True)
        out = out.astype(BF16)
        first = lax.div(base, 128) + 2 * i
        part[first] = out[0:128]
        part[first + 1] = out[128:256]

    loop(2, lambda i: input_rows(far, i))
    sums = scatters(rs, rr)
    all_of(sums, "begin")

    loop(2, lambda i: input_rows(near, i))
    gvec[:, 0:1024] = gvec[:, 0:1024] / gain1

    def tell(k):
        src, dev = (
            lambda: (gvec, head.dev(1, 0)),
            lambda: (gsum.at[0], head.dev(0, 1)),
            lambda: (gsum.at[0], head.dev(0, -1)),
            lambda: (gin.at[1], head.dev(0, 1)),
            lambda: (gsum.at[1], blk.sibling()),
            lambda: (gsum.at[2], blk.dev(1, 0)),
            lambda: (gsum.at[3], blk.dev(0, 1)),
            lambda: (gsum.at[3], blk.dev(0, -1)),
            lambda: (gin.at[6], blk.dev(0, 1)),
        )[k]()
        return remote(src, gin.at[k], gns.at[k], gnr.at[k], dev)

    def gather_gains(target, source, *ks):
        value = source[...]
        for k in ks:
            value = value + gin[k]
        gsum[target] = value

    tell(0).start()
    loop(4, key_value_grads)
    tell(0).wait_recv()
    gather_gains(0, gvec, 0)
    tell(1).start()
    tell(2).start()
    vscatter = BlkScatter(blk, vpart, vboth, vbufs, qs_s, qr_r, qcs.at[0], qcr.at[0])
    vscatter.cross()
    all_of(sums, "opposite")
    tell(1).wait_recv()
    tell(3).start()
    vscatter.merge()
    vscatter.begin()
    tell(2).wait_recv()
    tell(3).wait_recv()
    gather_gains(1, gsum.at[0], 1, 2, 3)
    tell(4).start()
    all_of(sums, "late")
    tell(4).wait_recv()
    gather_gains(2, gsum.at[1], 4)
    tell(5).start()
    vscatter.opposite()
    tell(5).wait_recv()
    gather_gains(3, gsum.at[2], 5)
    tell(6).start()
    tell(7).start()
    vscatter.late()
    tell(6).wait_recv()
    tell(8).start()
    for q, item in enumerate(sums):
        item.end()
        rows = slice(size * q, size * q + size)
        _, input_part = norm_back(tok[rows, :].astype(F32), gain1, item.total())
        for i in range(4):
            cols = slice(256 * i, 256 * i + 256)
            mid_grad = accum[3, 128 * i + size * q : 128 * i + size * q + size, :]
            tokens_grad[rows, cols] = (mid_grad + input_part[:, cols]).astype(BF16)
    tell(7).wait_recv()
    tell(8).wait_recv()
    gather_gains(4, gsum.at[3], 6, 7, 8)
    place = blk.plane(0, 0)
    offset = blk.c * 64 + head.h * 8
    lane = block * 8 + head.h

    def turned(first, shift):
        return pltpu.roll(gsum[4, :, pl.ds(pl.multiple_of(first, 128), 128)], lax.rem(128 - shift, 128), 1)

    first_out[...] = turned(place * 128, offset)[:, 0:8]
    second_out[...] = turned(1024 + place * 128, offset)[:, 0:8]
    qn_out[...] = turned(2048, lane)[:, 0:1]
    kn_out[...] = turned(2176, lane)[:, 0:1]
    vscatter.end()
    vsum = vscatter.total()
    query_out[...] = vsum[:, 0:256]
    key_out[...] = vsum[:, 256:384]
    value_out[...] = vsum[:, 384:512]
    output_out[...] = vsum[:, 512:768]
    for k in range(9):
        tell(k).wait_send()


def hand_over_kernel(*refs):
    count = len(refs) // 2
    for i in range(count):
        refs[count + i][...] = refs[i][...]


def sems(*counts):
    return [pltpu.SemaphoreType.DMA((c,)) for c in counts]


def per_device(
    tokens, doc_starts, first_gain, query_weight, key_matrix, value_matrix, querynorm, keynorm,
    output_weight, second_gain, gate_weight, up_weight, down_weight, grad_out,
):
    freqs = np.tile(THETA ** (-np.arange(64, dtype=np.float64) / 64), 2).astype(np.float32)
    vm = pl.BlockSpec(memory_space=pltpu.VMEM)
    hbm = pl.BlockSpec(memory_space=pl.ANY)
    outs = [
        ((128, 1024), BF16), ((128, 1024), BF16), ((64, 256), F32), ((64, 128), F32), ((64, 128), F32),
        ((64, 256), F32), ((64, 384), F32), ((64, 384), F32), ((64, 384), F32),
        ((1, 8), F32), ((1, 8), F32), ((1, 1), F32), ((1, 1), F32), ((1024, 1024), BF16),
    ]
    scratch = [
        ((1024, 128), F32), ((1024, 128), F32),
        ((1024, 1920), BF16), ((1024, 1024), BF16), ((1024, 1024), BF16), ((1024, 1024), BF16), ((16384, 256), BF16),
        ((2, 1024, 128), BF16), ((1024, 128), BF16), ((1024, 256), F32), ((1024, 128), F32), ((4, 1024, 256), F32),
        ((1024, 256), BF16), ((512, 256), BF16), ((2, 1024, 256), BF16), ((2, 1024, 256), BF16), ((128, 1024), F32),
        ((8, 128, 1024), BF16), ((7, 128, 1024), BF16), ((8, 128, 1024), BF16), ((7, 128, 1024), BF16),
        ((1024, 1152), BF16), ((1024, 256), BF16), ((512, 256), BF16), ((2, 1024, 256), BF16),
        ((8, 2, 64, 1152), BF16), ((8, 64, 1152), BF16), ((7, 64, 1152), BF16),
        ((8, 2, 64, 768), BF16), ((8, 64, 768), BF16), ((7, 64, 768), BF16),
        ((2, 1024, 256), BF16), ((8, 1024, 256), BF16), ((7, 1024, 256), BF16), ((512, 256), BF16), ((512, 256), BF16),
        ((1, 2304), F32), ((9, 1, 2304), F32), ((5, 1, 2304), F32),
    ]
    counts = (11, 11, 8, 8, 11, 11, 8, 8, 4, 4, 8 * PARTS, 8 * PARTS, 11 * PARTS, 11 * PARTS, 11, 11)
    counts += (8, 8, 8, 8, 1, 1, 11, 11, 8, 8, 8, 8, 1, 1, 8, 8, 8, 8, 9, 9, 2)
    made = pl.pallas_call(
        layer_kernel,
        out_shape=[jax.ShapeDtypeStruct(s, d) for s, d in outs],
        in_specs=[pl.BlockSpec(memory_space=pltpu.SMEM)] + [vm] * 14,
        out_specs=[vm] * 13 + [hbm],
        scratch_shapes=[pltpu.VMEM(s, d) for s, d in scratch] + sems(*counts),
        compiler_params=pltpu.CompilerParams(vmem_limit_bytes=VMEM_LIMIT, collective_id=1, has_side_effects=True),
    )(
        doc_starts, tokens, grad_out, query_weight, key_matrix, value_matrix, output_weight.T, gate_weight, up_weight,
        down_weight.T, first_gain.reshape(8, 128), second_gain.reshape(8, 128), querynorm[None, :], keynorm[None, :], freqs[None, :],
    )
    made = pl.pallas_call(
        hand_over_kernel,
        out_shape=[jax.ShapeDtypeStruct(s, d) for s, d in outs[:13]],
        in_specs=[vm] * 13,
        out_specs=[vm] * 13,
    )(*made[:13])
    layer_out, tokens_grad, query, key, value, output, gate, up, down, first, second, qn, kn = made
    return (
        layer_out, tokens_grad, first.reshape(8), query, key, value, qn.reshape(1), kn.reshape(1),
        output.T, second.reshape(8), gate, up, down.T,
    )


def solution(mesh):
    return jax.shard_map(
        per_device,
        mesh=mesh,
        in_specs=(
            P(("blk", "head"), None),
            P(),
            P(),
            P("blk", "head"),
            P("blk", "head"),
            P("blk", "head"),
            P(),
            P(),
            P("head", "blk"),
            P(),
            P("blk", "head"),
            P("blk", "head"),
            P("head", "blk"),
            P(("blk", "head"), None),
        ),
        out_specs=(
            P(("blk", "head"), None),
            P(("blk", "head"), None),
            P(("blk", "head")),
            P("blk", "head"),
            P("blk", "head"),
            P("blk", "head"),
            P(("blk", "head")),
            P(("blk", "head")),
            P("head", "blk"),
            P(("blk", "head")),
            P("blk", "head"),
            P("blk", "head"),
            P("head", "blk"),
        ),
        check_vma=False,
    )
```

```python
import functools

import jax
import jax.numpy as jnp
from jax import lax
from jax.experimental import pallas as pl
from jax.experimental.pallas import tpu as pltpu
import numpy as np
from jax.sharding import PartitionSpec as P

EPS = 1e-06
THETA = 1000000.0
MESH = pl.DeviceIdType.MESH
F32 = jnp.float32
BF16 = jnp.bfloat16
LOG2E = 1.4426950408889634
LN2 = 0.6931471805599453
HEAD_DIM = 128
PARTS = 2
SCALE = HEAD_DIM**-0.5
VMEM_LIMIT = 64 * 2**20 - 2**16

QC, KC, VC, OC, GC, UC, DC, END = 0, 256, 384, 512, 768, 1152, 1536, 1920


def nn(a, b):
    return jnp.dot(a, b, preferred_element_type=F32)


def nt(a, b):
    return lax.dot_general(a, b, (((1,), (1,)), ((), ())), preferred_element_type=F32)


def tn(a, b):
    return lax.dot_general(a, b, (((0,), (0,)), ((), ())), preferred_element_type=F32)


def chunk(i, size):
    return pl.ds(pl.multiple_of(i * size, size), size)


def loop(count, body):
    def step(i, carry):
        body(i)
        return carry

    lax.fori_loop(0, count, step, 0)


def run_all(*actions):
    def run():
        for action in actions:
            action()

    return run


def when(condition, action):
    def run():
        action()

    pl.when(condition)(run)


class HeadRing:
    def __init__(self):
        self.b = lax.axis_index("blk")
        h = lax.axis_index("head")
        self.h = h
        self.p, self.r = lax.div(h, 4), lax.rem(h, 4)

    def plane(self, dp, dr):
        return lax.rem(self.p + dp, 2) * 4 + lax.rem(self.r + dr + 4, 4)

    slot = plane

    def dev(self, dp, dr):
        return (self.b, self.plane(dp, dr))

    def near(self):
        return [self.dev(1, 0), self.dev(0, 1), self.dev(0, -1)]


class BlkRing:
    def __init__(self):
        b = lax.axis_index("blk")
        self.h = lax.axis_index("head")
        self.b = b
        self.p, self.r, self.c = lax.div(b, 8), lax.rem(lax.div(b, 2), 4), lax.rem(b, 2)

    def plane(self, dp, dr):
        return lax.rem(self.p + dp, 2) * 4 + lax.rem(self.r + dr + 4, 4)

    def slot(self, dp, dr, dc=0):
        return self.plane(dp, dr) * 2 + lax.rem(self.c + dc, 2)

    def dev(self, dp, dr, dc=0):
        return (self.slot(dp, dr, dc), self.h)

    def sibling(self):
        return self.dev(0, 0, 1)

    def mirror(self):
        return (15 - self.b, self.h)

    def near(self):
        return [self.dev(1, 0), self.dev(0, 1), self.dev(0, -1)]


def greet(devices):
    for d in devices:
        pl.semaphore_signal(pltpu.get_barrier_semaphore(), inc=1, device_id=d, device_id_type=MESH)


def remote(src, dst, ss, rs, dev):
    return pltpu.make_async_remote_copy(
        src_ref=src, dst_ref=dst, send_sem=ss, recv_sem=rs, device_id=dev, device_id_type=MESH
    )


class Gather:
    ORDER = ((0, 0), (1, 0), (0, -1), (0, 1), (0, 2), (1, -1), (1, 1), (1, 2))

    def __init__(self, ring, full, n, ss, rs, sib=None, on_ring=False, off=0, stride=None, k0=0):
        self.ring, self.full, self.n, self.ss, self.rs, self.sib = ring, full, n, ss, rs, sib
        self.on_ring, self.off, self.stride, self.k0 = on_ring, off, stride or n, k0

    def rows(self, dp, dr, part=None):
        base = self.ring.slot(dp, dr) * self.stride + self.off
        size = self.n
        if part is not None:
            size = self.n // 2
            base = base + part * size
        return self.full.at[pl.ds(pl.multiple_of(base, size), size)]

    def copy(self, k):
        ring, rows = self.ring, self.rows
        ref, dev = (
            lambda: (rows(0, 0), ring.dev(1, 0)),
            lambda: (rows(0, 0, 0), ring.dev(0, 1)),
            lambda: (rows(0, 0, 1), ring.dev(0, -1)),
            lambda: (rows(0, 0, 1), ring.dev(0, 1)),
            lambda: (rows(0, 0, 0), ring.dev(0, -1)),
            lambda: (rows(0, -1, 0), ring.dev(0, 1)),
            lambda: (rows(0, 1, 1), ring.dev(0, -1)),
            lambda: (rows(1, 0), ring.dev(0, 1)),
            lambda: (rows(1, 0), ring.dev(0, -1)),
            lambda: (rows(1, -1, 0), ring.dev(0, 1)) if self.on_ring else (rows(0, 2, 0), ring.dev(1, 0)),
            lambda: (rows(1, 1, 1), ring.dev(0, -1)) if self.on_ring else (rows(0, 2, 1), ring.dev(1, 0)),
        )[k]()
        return remote(ref, ref, self.ss.at[self.k0 + k], self.rs.at[self.k0 + k], dev)

    def send(self, *ks):
        for k in ks:
            self.copy(k).start()

    def wait(self, *ks):
        for k in ks:
            self.copy(k).wait_recv()

    def crossing(self, dp, dr):
        k = self.ORDER.index((dp, dr))
        ref = self.rows(dp, dr)
        return remote(ref, ref, self.sib[0].at[k], self.sib[1].at[k], self.ring.sibling())

    def cross(self, *which):
        if self.sib is not None:
            for w in which:
                self.crossing(*w).start()

    def crossed(self, *which):
        if self.sib is not None:
            for w in which:
                self.crossing(*w).wait_recv()

    def begin(self):
        self.send(1, 2, 0, 3, 4)
        self.cross((0, 0))

    def travel(self):
        self.wait(1)
        self.send(5)
        self.wait(2)
        self.send(6)

    def pair_on(self):
        self.wait(0)
        self.send(7, 8)
        self.cross((1, 0))

    def step1(self):
        self.travel()
        self.pair_on()

    def opposite_on(self):
        self.wait(5)
        if not self.on_ring:
            self.send(9)
        self.wait(6)
        if not self.on_ring:
            self.send(10)
        self.cross((0, 2))

    def ring_done(self):
        self.wait(3, 4)
        self.cross((0, -1), (0, 1))

    def step2(self):
        self.opposite_on()
        self.ring_done()

    def step3(self):
        self.wait(7)
        if self.on_ring:
            self.send(9)
        self.wait(8)
        if self.on_ring:
            self.send(10)
        self.cross((1, -1), (1, 1))

    def step4(self):
        self.wait(9, 10)
        self.cross((1, 2))

    def end(self):
        for k in range(11):
            self.copy(k).wait_send()
        if self.sib is not None:
            for w in self.ORDER:
                self.crossing(*w).wait_send()

    def finish(self):
        self.crossed(*self.ORDER)
        self.end()

    def steps(self):
        return [self.begin, self.step1, self.step2, self.step3, self.step4, self.finish]


class Scatter:
    def __init__(self, ring, part, bufs, ss, rs, off=0, n=None, k0=0):
        self.ring, self.part, self.bufs, self.ss, self.rs = ring, part, bufs, ss, rs
        self.off, self.n, self.k0 = off, n or part.shape[1], k0

    def span(self, half):
        if half is None:
            return pl.ds(self.off, self.n)
        return pl.ds(self.off + half * (self.n // 2), self.n // 2)

    def own(self, dp, dr, half=None):
        return self.part.at[self.ring.plane(dp, dr), self.span(half)]

    def buf(self, i, half=None):
        return self.bufs.at[i, self.span(half)]

    def copy(self, k):
        ring, own, buf = self.ring, self.own, self.buf
        src, dst, dev = (
            lambda: (own(1, 2), buf(0), ring.dev(1, 0)),
            lambda: (own(1, 1), buf(1), ring.dev(0, 1)),
            lambda: (own(1, -1), buf(2), ring.dev(0, -1)),
            lambda: (own(0, 2, 0), buf(6, 0), ring.dev(0, 1)),
            lambda: (own(0, 2, 1), buf(6, 1), ring.dev(0, -1)),
            lambda: (own(1, 0), buf(3), ring.dev(1, 0)),
            lambda: (own(0, 1), buf(4), ring.dev(0, 1)),
            lambda: (own(0, -1), buf(5), ring.dev(0, -1)),
        )[k]()
        return remote(src, dst, self.ss.at[self.k0 + k], self.rs.at[self.k0 + k], dev)

    def send(self, *ks):
        for k in ks:
            self.copy(k).start()

    def wait(self, *ks):
        for k in ks:
            self.copy(k).wait_recv()

    def add(self, dst, *srcs):
        value = dst[...].astype(F32)
        for src in srcs:
            value = value + src[...].astype(F32)
        dst[...] = value.astype(dst.dtype)

    def begin(self):
        self.send(1, 2, 0)

    def opposite(self):
        self.wait(0)
        self.add(self.own(0, 2), self.buf(0))
        self.send(3, 4)

    def home(self):
        self.wait(1, 2)
        self.add(self.own(1, 0), self.buf(1), self.buf(2))
        self.send(5)

    def up(self):
        self.wait(3)
        self.add(self.own(0, 1, 0), self.buf(6, 0))
        self.send(6)

    def down(self):
        self.wait(4)
        self.add(self.own(0, -1, 1), self.buf(6, 1))
        self.send(7)

    def end(self):
        self.wait(5, 6, 7)
        for k in range(8):
            self.copy(k).wait_send()

    def late(self):
        self.up()
        self.down()
        self.home()

    def total(self):
        out = self.own(0, 0)[...].astype(F32)
        for i in (3, 4, 5):
            out = out + self.buf(i)[...].astype(F32)
        return out


class BlkScatter(Scatter):
    def __init__(self, ring, terms, part, bufs, ss, rs, cs, cr):
        super().__init__(ring, part, bufs, ss, rs)
        self.terms, self.cs, self.cr = terms, cs, cr

    def crossing(self):
        return remote(self.terms.at[:, 1 - self.ring.c], self.part, self.cs, self.cr, self.ring.sibling())

    def cross(self):
        self.crossing().start()

    def merge(self):
        self.crossing().wait_recv()

        def body(k):
            self.part[k] = (self.part[k].astype(F32) + self.terms[k, self.ring.c].astype(F32)).astype(BF16)

        loop(8, body)
        self.crossing().wait_send()


def weave(*lists):
    for i in range(max(len(item) for item in lists)):
        for item in lists:
            if i < len(item):
                item[i]()


def rope(v, cosine, sine):
    return v * cosine + pltpu.roll(v, 64, 1) * sine


def rope_back(g, cosine, sine):
    return g * cosine + pltpu.roll(g * sine, 64, 1)


def inverse(v):
    return lax.rsqrt(jnp.mean(v * v, axis=-1, keepdims=True) + EPS)


def norm_back(v, gain, grad):
    r = inverse(v)
    n = v * r
    scaled = grad * gain
    return grad * n, r * (scaled - n * jnp.mean(scaled * n, axis=-1, keepdims=True))


def split3(v):
    a = (-v).astype(BF16).astype(F32)
    rest = -v - a
    b = rest.astype(BF16).astype(F32)
    lane = lax.broadcasted_iota(jnp.int32, v.shape, 1)
    return jnp.where(lane == 0, a, jnp.where(lane == 1, b, jnp.where(lane == 2, rest - b, 0.0)))


def begin_of(starts, index):
    begin = jnp.zeros_like(index)
    for k in range(1, 4):
        begin = jnp.where(index >= starts[k], starts[k], begin)
    return begin


def pick(index, values):
    out = jnp.int32(values[-1])
    for k in range(len(values) - 2, -1, -1):
        out = jnp.where(index == k, jnp.int32(values[k]), out)
    return out


def layer_kernel(
    starts, tok, dy, wq, wk, wv, wo, wg, wu, wd, gain_one, gain_two, gain_q, gain_k, freqs,
    layer_out, tokens_grad, query_out, key_out, value_out, output_out, gate_out, up_out, down_out,
    first_out, second_out, qn_out, kn_out, saved,
    cosine, sine, weights, block_a, block_b, block_dy, kv, qs, qsend, qraw, kraw, accum, ctx, ctxb, qx, qfar, middle,
    part, bufs, ffpart, ffbufs, acts, grad_all, grad_far, dox, wpart, wboth, wbufs, vpart, vboth, vbufs,
    xs, kvboth, kvbufs, dqsend, dqhome, gvec, gin, gsum,
    ws, wr, wcs, wcr, ks, kr, kcs, kcr, ms, mr, rs, rr, gs, gr, ds_, dr_,
    fs, fr, vs, vr, vcs, vcr, w2s, w2r, w2cs, w2cr, qs_s, qr_r, qcs, qcr, xss, xrr, xcs, xcr, gns, gnr, local,
):
    head, blk = HeadRing(), BlkRing()
    partners = head.near() + blk.near() + [blk.sibling(), blk.mirror()]
    greet(partners)
    block = blk.b

    def line(ref):
        value = ref[...].astype(F32)
        return jnp.concatenate([value[i : i + 1] for i in range(8)], axis=1)

    gain1, gain2 = line(gain_one), line(gain_two)
    qgain, kgain = gain_q[...].astype(F32), gain_k[...].astype(F32)
    x = tok[...].astype(F32)
    block_a[chunk(head.slot(0, 0), 128), :] = (x * inverse(x) * gain1).astype(BF16)
    mine = chunk(blk.slot(0, 0), 64)
    for ref, first in ((wq, QC), (wk, KC), (wv, VC), (wo, OC), (wg, GC), (wu, UC), (wd, DC)):
        weights[mine, first : first + ref.shape[1]] = ref[...]
    block_dy[chunk(head.slot(0, 0), 128), :] = dy[...]
    pl.semaphore_wait(pltpu.get_barrier_semaphore(), len(partners))
    wone = Gather(blk, weights.at[:, QC:GC], 64, ws, wr, (wcs, wcr))
    wtwo = Gather(blk, weights.at[:, GC:END], 64, w2s, w2r, (w2cs, w2cr), on_ring=True)
    normed = Gather(head, block_a, 128, gs, gr)
    normed.begin()
    wone.begin()
    for i in range(4):
        at = slice(256 * i, 256 * i + 256)
        index = block * 1024 + 256 * i + lax.broadcasted_iota(jnp.int32, (256, 1), 0)
        angle = (index - begin_of(starts, index)).astype(F32) * freqs[...]
        lane = lax.broadcasted_iota(jnp.int32, (256, 128), 1)
        cosine[at, :] = jnp.cos(angle)
        turn = jnp.sin(angle)
        sine[at, :] = jnp.where(lane < 64, -turn, turn)
    normed.step1()
    wone.step1()
    wtwo.begin()
    normed.step2()
    for step in (wone.step2, wone.step3, wone.step4, wtwo.step1, wone.finish):
        step()

    base = pl.multiple_of(block * 1024, 1024)
    far, near = pl.multiple_of((1 - head.p) * 512, 512), pl.multiple_of(head.p * 512, 512)

    def query_rows(base, dst):
        for i in range(2):
            at = pl.ds(pl.multiple_of(base + 256 * i, 256), 256)
            out = nn(block_a[at, :], weights[:, QC:KC])
            for k in range(2):
                v = out[:, 128 * k : 128 * k + 128]
                qraw[at, 128 * k : 128 * k + 128] = v
                v = rope(v * inverse(v) * qgain, cosine[at, :], sine[at, :]) * (SCALE * LOG2E)
                dst[512 * k + 256 * i : 512 * k + 256 * i + 256, :] = v.astype(BF16)

    def keys_rows(first, i):
        at = pl.ds(pl.multiple_of(first + i * 256, 256), 256)
        out = nn(block_a[at, :], weights[:, KC:OC])
        v = out[:, 0:128]
        kraw[at, :] = v
        to = pl.ds(pl.multiple_of(base + first + i * 256, 256), 256)
        kv[to, 0:128] = rope(v * inverse(v) * kgain, cosine[at, :], sine[at, :]).astype(BF16)
        kv[to, 128:256] = out[:, 128:256].astype(BF16)

    query_rows(near, qsend)
    qswap = remote(qsend, qs.at[1], ms.at[0], mr.at[0], blk.mirror())
    qswap.start()
    loop(2, lambda i: keys_rows(near, i))
    wtwo.step2()
    for step in (normed.step3, normed.step4, normed.finish):
        step()
    keep = pltpu.make_async_copy(block_a, saved, local.at[0])
    keep.start()
    loop(2, lambda i: keys_rows(far, i))
    wtwo.step3()
    kvgather = Gather(blk, kv, 1024, ks, kr, (kcs, kcr))
    kvgather.send(1, 2, 0)
    kvgather.cross((0, 0))
    query_rows(far, qs.at[0])
    dygather = Gather(head, block_dy, 128, ds_, dr_, on_ring=True)
    dygather.begin()

    def clear(i):
        accum[i] = jnp.zeros((1024, 256), F32)

    loop(4, clear)
    ones = jnp.ones((1024, 128), BF16)

    def limit_of(side):
        return jnp.where(side == 0, block, 15 - block)

    def half_of(side):
        return jnp.where(side == 0, 2 * block + 1 - head.p, 30 - 2 * block + head.p)

    def mask(side, jb, c, rows, transposed):
        first = half_of(side) * 512 + lax.rem(c * rows, 512)
        shape_q, shape_k = ((1, rows), (1024, 1)) if transposed else ((rows, 1), (1, 1024))
        qi = first + lax.broadcasted_iota(jnp.int32, shape_q, 1 if transposed else 0)
        ki = jb * 1024 + lax.broadcasted_iota(jnp.int32, shape_k, 0 if transposed else 1)
        return (ki >= begin_of(starts, qi)) & (ki <= qi)

    def attend(sides, jb, masked):
        at = chunk(jb, 1024)
        keys = kv[at, 0:128]
        values = jnp.concatenate([kv[at, 128:256], ones], axis=1)
        for side in sides:
            row = 2 * side + masked
            for c in range(4):
                rows = slice(c * 256, c * 256 + 256)
                p = jnp.exp2(nt(qs[side, rows, :], keys))
                if masked:
                    p = jnp.where(mask(side, jb, c, 256, False), p, 0.0)
                accum[row, rows, :] += nn(p.astype(BF16), values)

    def work(jb, unit):
        def one(side):
            limit = limit_of(side)
            careful = (jb == 0) | (jb == limit)
            when((jb <= limit) & jnp.logical_not(careful), lambda: unit((side,), jb, False))
            when((jb <= limit) & careful, lambda: unit((side,), jb, True))

        loop(2, one)

    order0 = ((0, 0), (0, 2), (1, 0), (0, -1), (0, 1), (1, 2), (1, -1), (1, 1))
    order1 = ((0, 0), (1, 0), (0, 2), (1, -1), (1, 1), (1, 2), (0, -1), (0, 1))
    g = kvgather
    every_step = {
        0: qswap.wait_recv,
        1: lambda: (g.crossed((0, 0)), g.travel()),
        4: lambda: (dygather.step1(), wtwo.step4()),
        7: dygather.step2,
        10: dygather.step3,
    }
    step_p0 = {
        2: lambda: (g.opposite_on(), g.send(3, 4), g.wait(0), g.cross((1, 0))),
        6: lambda: (g.ring_done(), g.send(7, 8)),
        10: g.step4,
        12: lambda: (g.wait(7, 8), g.cross((1, -1), (1, 1))),
    }
    step_p1 = {
        2: lambda: (g.pair_on(), g.opposite_on()),
        6: lambda: (g.wait(7, 8), g.cross((1, -1), (1, 1)), g.send(3, 4)),
        8: g.step4,
        12: g.ring_done,
    }
    for i in range(1, 8):
        for steps, order in ((step_p0, order0), (step_p1, order1)):
            steps[2 * i + 1] = functools.partial(g.crossed, order[i])

    def along(s, first, second):
        return tuple(
            jnp.where(blk.p == 0, pick(s, [d[i] for d in first]), pick(s, [d[i] for d in second])) for i in range(2)
        )

    def attend_step(t):
        s, core = lax.div(t, 2), lax.rem(t, 2)
        jb = blk.slot(*along(s, order0, order1), core)
        for k, action in step_p0.items():
            when((t == k) & (blk.p == 0), action)
        for k, action in step_p1.items():
            when((t == k) & (blk.p == 1), action)
        for k, action in every_step.items():
            when(t == k, action)
        work(jb, attend)

    loop(16, attend_step)

    def context_of(side, dst):
        for k in range(2):
            rows = slice(512 * k, 512 * k + 512)
            qi = half_of(side) * 512 + lax.broadcasted_iota(jnp.int32, (512, 1), 0)
            here = qi < starts[2]
            both = accum[2 * side + 1, rows, :] + jnp.where(here, accum[2 * side, rows, :], 0.0)
            dst[:, 128 * k : 128 * k + 128] = (both[:, 0:128] / both[:, 128:256]).astype(BF16)
            accum[2 * side, rows, 0:128] = both[:, 128:256]

    def extend(side):
        for k in range(2):
            rows = slice(512 * k, 512 * k + 512)
            terms = split3(jnp.log2(accum[2 * side, rows, 0:128]))
            qi = half_of(side) * 512 + lax.broadcasted_iota(jnp.int32, (512, 128), 0)
            lane = lax.broadcasted_iota(jnp.int32, (512, 128), 1)
            gone = jnp.where(lane == 0, -1e30, 0.0)
            qx[side, rows, 0:128] = qs[side, rows, :]
            qx[side, rows, 128:256] = terms.astype(BF16)
            qfar[side, rows, 0:128] = qs[side, rows, :]
            qfar[side, rows, 128:256] = jnp.where(qi < starts[2], terms, gone).astype(BF16)

    context_of(1, ctxb)
    near_ctx, far_ctx = ctx.at[pl.ds(near, 512)], ctx.at[pl.ds(far, 512)]
    cswap = remote(ctxb, near_ctx, ms.at[1], mr.at[1], blk.mirror())
    cswap.start()
    context_of(0, far_ctx)

    def output_rows(base, i):
        at = pl.ds(pl.multiple_of(base + i * 256, 256), 256)
        out = nt(ctx[at, :], weights[:, OC:GC]).astype(BF16)
        first = lax.div(base, 128) + 2 * i
        part[first] = out[0:128]
        part[first + 1] = out[128:256]

    size = 128 // PARTS

    def scatters(ss, rs):
        return [Scatter(head, part, bufs, ss, rs, off=size * q, n=size, k0=8 * q) for q in range(PARTS)]

    def gathers(full, ss, rs):
        return [Gather(head, full, size, ss, rs, off=size * q, stride=128, k0=11 * q) for q in range(PARTS)]

    def all_of(items, *names):
        for name in names:
            for item in items:
                getattr(item, name)()

    loop(2, lambda i: output_rows(far, i))
    sums = scatters(rs, rr)
    all_of(sums, "begin")
    dygather.step4()
    extend(1)
    cswap.wait_recv()
    loop(2, lambda i: output_rows(near, i))
    all_of(sums, "opposite")
    extend(0)
    dygather.end()
    shards = gathers(block_b, gs, gr)
    own = pl.multiple_of(head.slot(0, 0) * 128, 128)
    all_of(sums, "late")
    for q, (item, collect) in enumerate(zip(sums, shards)):
        item.end()
        rows = slice(size * q, size * q + size)
        mid = tok[rows, :].astype(F32) + item.total()
        middle[rows, :] = mid
        block_b[pl.ds(own + size * q, size), :] = (mid * inverse(mid) * gain2).astype(BF16)
        collect.begin()
    qswap.wait_send()
    cswap.wait_send()
    kvgather.end()
    wtwo.finish()
    keep.wait()
    all_of(shards, "step1", "step2")

    def forward_rows(base, i):
        at = pl.ds(pl.multiple_of(base + i * 256, 256), 256)
        both = nn(block_b[at, :], weights[:, GC:DC])
        gate, upper = both[:, 0:384], both[:, 384:768]
        sigma = 1.0 / (1.0 + jnp.exp(-gate))
        silu = gate * sigma
        act_grad = nn(block_dy[at, :], weights[:, DC:END])
        gate_low = (act_grad * upper * sigma * (1.0 + gate * (1.0 - sigma))).astype(BF16)
        low = jnp.concatenate([gate_low, (act_grad * silu).astype(BF16)], axis=1)
        acts[at, 0:768] = low
        acts[at, 768:1152] = (silu * upper).astype(BF16)
        out = nt(low, weights[:, GC:DC]).astype(BF16)
        first = lax.div(base, 128) + 2 * i
        part[first] = out[0:128]
        part[first + 1] = out[128:256]

    loop(2, lambda i: forward_rows(near, i))
    all_of(shards, "step3", "step4", "finish")
    loop(2, lambda i: forward_rows(far, i))
    sums = scatters(rs, rr)
    all_of(sums, "begin")

    def down_rows(i):
        out = nt(acts[chunk(i, 256), 768:1152], weights[:, DC:END]).astype(BF16)
        ffpart[2 * i] = out[0:128]
        ffpart[2 * i + 1] = out[128:256]

    loop(4, down_rows)
    all_of(sums, "opposite")

    def put_terms(i, out, cols):
        for k in range(2):
            wpart[2 * i + k, 0, :, cols] = out[128 * k : 128 * k + 64]
            wpart[2 * i + k, 1, :, cols] = out[128 * k + 64 : 128 * k + 128]

    def gate_up_grads(i):
        put_terms(i, tn(block_b[:, chunk(i, 256)], acts[:, 0:768]).astype(BF16), slice(0, 768))

    loop(2, gate_up_grads)
    all_of(sums, "late")
    loop(2, lambda i: gate_up_grads(i + 2))
    shards = gathers(block_a, gs, gr)
    gvec[:, 1024:2048] = jnp.zeros((1, 1024), F32)
    for q, (item, collect) in enumerate(zip(sums, shards)):
        item.end()
        rows = slice(size * q, size * q + size)
        terms, part_grad = norm_back(middle[rows, :], gain2, item.total())
        mid_grad = dy[rows, :].astype(F32) + part_grad
        block_a[pl.ds(own + size * q, size), :] = mid_grad.astype(BF16)
        collect.begin()
        gvec[:, 1024:2048] += jnp.sum(terms, axis=0, keepdims=True)
        for i in range(4):
            accum[3, 128 * i + size * q : 128 * i + size * q + size, :] = mid_grad[:, 256 * i : 256 * i + 256]

    def down_grads(i):
        put_terms(i, tn(block_dy[:, chunk(i, 256)], acts[:, 768:1152]).astype(BF16), slice(768, 1152))

    loop(2, down_grads)
    all_of(shards, "step1", "step2")
    def context_grads(base, i):
        at = pl.ds(pl.multiple_of(base + 256 * i, 256), 256)
        grad_all[at, :] = nn(block_a[at, :], weights[:, OC:GC]).astype(BF16)

    loop(2, lambda i: context_grads(near, i))
    gswap = remote(grad_all.at[pl.ds(near, 512)], grad_far, ms.at[2], mr.at[2], blk.mirror())
    gswap.start()
    loop(2, lambda i: down_grads(i + 2))
    all_of(shards, "step3", "step4", "finish")

    loop(2, lambda i: context_grads(far, i))
    reload = pltpu.make_async_copy(saved, block_b, local.at[1])
    reload.start()
    ffscatter = Scatter(head, ffpart, ffbufs, fs, fr)
    wscatter = BlkScatter(blk, wpart, wboth, wbufs, vs, vr, vcs.at[0], vcr.at[0])
    ffscatter.begin()
    wscatter.cross()

    def extend_grad(side, grads, context):
        for k in range(2):
            rows, cols = slice(512 * k, 512 * k + 512), slice(128 * k, 128 * k + 128)
            grad = grads[0:512, cols]
            delta = jnp.sum(grad.astype(F32) * context[0:512, cols].astype(F32), axis=1, keepdims=True)
            dox[side, rows, 0:128] = grad
            dox[side, rows, 128:256] = split3(jnp.broadcast_to(delta, (512, 128))).astype(BF16)

    extend_grad(0, grad_all.at[pl.ds(far, 512)], far_ctx)
    loop(2, lambda i: clear(i))

    back0 = ((1, 2), (1, 1), (1, -1), (1, 0), (0, 1), (0, 2), (0, -1), (0, 0))
    back1 = ((1, 2), (0, 2), (0, 1), (0, -1), (1, 1), (1, -1), (1, 0), (0, 0))

    def attend_back(sides, jb, masked):
        at = chunk(jb, 1024)
        keys = kv[at, 0:128]
        kx = jnp.concatenate([keys, ones], axis=1)
        vx = jnp.concatenate([kv[at, 128:256], ones], axis=1)
        source = qx if masked else qfar
        for side in sides:
            fresh = (side == 0) | (jb > limit_of(0))
            for c in range(2):
                rows = slice(c * 512, c * 512 + 512)
                p = jnp.exp2(nt(kx, source[side, rows, :]))
                if masked:
                    p = jnp.where(mask(side, jb, c, 512, True), p, 0.0)
                ds = (p * nt(vx, dox[side, rows, :])).astype(BF16)
                for cols, term in (
                    (slice(0, 128), nn(ds, source[side, rows, 0:128])),
                    (slice(128, 256), nn(p.astype(BF16), dox[side, rows, 0:128])),
                ):
                    before = accum[0, :, cols]
                    accum[0, :, cols] = term + (jnp.where(fresh, 0.0, before) if c == 0 else before)
                turned = tn(keys, ds)
                for k in range(2):
                    accum[1, chunk(4 * side + 2 * c + k, 128), :] += turned[:, 256 * k : 256 * k + 256]

    kvscatter = Scatter(blk, kvboth, kvbufs, xss, xrr)

    def crossing(s):
        return remote(xs.at[s % 2], kvboth.at[blk.plane(*along(s, back0, back1))], xcs.at[s], xcr.at[s], blk.sibling())

    sc = kvscatter
    actions0 = {
        0: lambda: sc.send(0), 1: lambda: sc.send(1), 2: lambda: sc.send(2), 4: sc.home, 5: sc.opposite,
        6: lambda: (sc.up(), sc.down()),
    }
    actions1 = {
        0: lambda: sc.send(0), 3: sc.opposite, 4: lambda: (sc.send(1), sc.up(), sc.down()), 5: lambda: sc.send(2),
        6: sc.home,
    }
    others = {
        0: lambda: (wscatter.merge(), wscatter.begin()),
        2: lambda: (wscatter.opposite(), ffscatter.opposite()),
        4: lambda: (wscatter.up(), wscatter.down(), wscatter.home(), ffscatter.up(), ffscatter.down(), ffscatter.home()),
        6: lambda: (wscatter.end(), ffscatter.end()),
    }

    def reached(plane):
        even = block - blk.c
        return 2 * plane <= jnp.maximum(even + 1, 15 - even)

    def plane_at(s):
        return blk.plane(*along(s, back0, back1))

    def back_step(t):
        s, core = lax.div(t, 2), 1 - lax.rem(t, 2)
        plane = plane_at(s)
        jb = plane * 2 + lax.rem(blk.c + core, 2)
        some = reached(plane)

        def compute():
            when((jb > limit_of(0)) & (jb > limit_of(1)), lambda: clear(0))
            when(t == 0, lambda: (gswap.wait_recv(), extend_grad(1, grad_far, ctxb)))
            work(jb, attend_back)

        when(some | (t == 0), compute)
        for i in range(8):

            def out(i=i):
                if i >= 2:
                    when(reached(plane_at(i - 2)), lambda: crossing(i - 2).wait_send())

                def give():
                    xs[i % 2] = accum[0].astype(BF16)
                    crossing(i).start()

                when(some, give)
                if i in others:
                    others[i]()

            def merge(i=i):
                def take():
                    crossing(i).wait_recv()
                    kvboth[plane] = (kvboth[plane].astype(F32) + accum[0]).astype(BF16)

                def none():
                    kvboth[plane] = jnp.zeros((1024, 256), BF16)

                when(some, take)
                when(jnp.logical_not(some), none)

            when(t == 2 * i, out)
            when(t == 2 * i + 1, merge)
            for p, actions in enumerate((actions0, actions1)):
                if i in actions:
                    when((t == 2 * i + 1) & (blk.p == p), actions[i])

    loop(16, back_step)
    for i in (6, 7):
        when(reached(plane_at(i)), crossing(i).wait_send)

    def dq_of(side, k, i):
        first = 128 * (4 * side + 2 * k + i)
        return jnp.transpose(accum[1, first : first + 128, :]) * SCALE

    for k in range(2):
        for i in range(2):
            dqsend[256 * i : 256 * i + 256, 128 * k : 128 * k + 128] = dq_of(1, k, i).astype(BF16)
    dswap = remote(dqsend, dqhome, ms.at[3], mr.at[3], blk.mirror())
    dswap.start()
    reload.wait()
    gswap.wait_send()
    gvec[:, 2048:2304] = jnp.zeros((1, 256), F32)

    def back(raw, grad, at, gains):
        return norm_back(raw, gains, rope_back(grad, cosine[at, :], sine[at, :]))

    def query_back(base, i, grads):
        at = pl.ds(pl.multiple_of(base + 256 * i, 256), 256)
        for k in range(2):
            cols = slice(128 * k, 128 * k + 128)
            terms, out = back(qraw[at, cols], grads(i, k), at, qgain)
            acts[at, cols] = out.astype(BF16)
            gvec[:, 2048:2176] += jnp.sum(terms, axis=0, keepdims=True)

    def put_vterms(i, out, cols):
        for k in range(2):
            vpart[2 * i + k, 0, :, cols] = out[128 * k : 128 * k + 64]
            vpart[2 * i + k, 1, :, cols] = out[128 * k + 64 : 128 * k + 128]

    def output_grads(i):
        put_vterms(i, tn(block_a[:, chunk(i, 256)], ctx[...]).astype(BF16), slice(512, 768))

    def query_grads(i):
        put_vterms(i, tn(block_b[:, chunk(i, 256)], acts[:, 0:256]).astype(BF16), slice(0, 256))

    def key_value_grads(i):
        put_vterms(i, tn(block_b[:, chunk(i, 256)], acts[:, 256:512]).astype(BF16), slice(256, 512))

    for i in range(2):
        query_back(far, i, lambda i, k: dq_of(0, k, i))
    loop(4, output_grads)
    layer_out[...] = (middle[...] + ffscatter.total()).astype(BF16)
    wsum = wscatter.total()
    gate_out[...] = wsum[:, 0:384]
    up_out[...] = wsum[:, 384:768]
    down_out[...] = wsum[:, 768:1152]
    dswap.wait_recv()
    for i in range(2):
        query_back(near, i, lambda i, k: dqhome[256 * i : 256 * i + 256, 128 * k : 128 * k + 128].astype(F32))
    loop(4, query_grads)
    kvscatter.end()
    accum[2] = kvscatter.total()

    def key_back(i):
        at = slice(256 * i, 256 * i + 256)
        terms, out = back(kraw[at, :], accum[2, at, 0:128] * LN2, at, kgain)
        acts[at, 256:384] = out.astype(BF16)
        gvec[:, 2176:2304] += jnp.sum(terms, axis=0, keepdims=True)
        acts[at, 384:512] = accum[2, at, 128:256].astype(BF16)

    for i in range(4):
        key_back(i)
    dswap.wait_send()

    gvec[:, 0:1024] = jnp.zeros((1, 1024), F32)

    def input_rows(base, i):
        at = pl.ds(pl.multiple_of(base + i * 256, 256), 256)
        out = nt(acts[at, 0:512], weights[:, QC:OC])
        gvec[:, 0:1024] += jnp.sum(out * block_b[at, :].astype(F32), axis=0, keepdims=True)
        out = out.astype(BF16)
        first = lax.div(base, 128) + 2 * i
        part[first] = out[0:128]
        part[first + 1] = out[128:256]

    loop(2, lambda i: input_rows(far, i))
    sums = scatters(rs, rr)
    all_of(sums, "begin")

    loop(2, lambda i: input_rows(near, i))
    gvec[:, 0:1024] = gvec[:, 0:1024] / gain1

    def tell(k):
        src, dev = (
            lambda: (gvec, head.dev(1, 0)),
            lambda: (gsum.at[0], head.dev(0, 1)),
            lambda: (gsum.at[0], head.dev(0, -1)),
            lambda: (gin.at[1], head.dev(0, 1)),
            lambda: (gsum.at[1], blk.sibling()),
            lambda: (gsum.at[2], blk.dev(1, 0)),
            lambda: (gsum.at[3], blk.dev(0, 1)),
            lambda: (gsum.at[3], blk.dev(0, -1)),
            lambda: (gin.at[6], blk.dev(0, 1)),
        )[k]()
        return remote(src, gin.at[k], gns.at[k], gnr.at[k], dev)

    def gather_gains(target, source, *ks):
        value = source[...]
        for k in ks:
            value = value + gin[k]
        gsum[target] = value

    tell(0).start()
    loop(4, key_value_grads)
    tell(0).wait_recv()
    gather_gains(0, gvec, 0)
    tell(1).start()
    tell(2).start()
    vscatter = BlkScatter(blk, vpart, vboth, vbufs, qs_s, qr_r, qcs.at[0], qcr.at[0])
    vscatter.cross()
    all_of(sums, "opposite")
    tell(1).wait_recv()
    tell(3).start()
    vscatter.merge()
    vscatter.begin()
    tell(2).wait_recv()
    tell(3).wait_recv()
    gather_gains(1, gsum.at[0], 1, 2, 3)
    tell(4).start()
    all_of(sums, "late")
    tell(4).wait_recv()
    gather_gains(2, gsum.at[1], 4)
    tell(5).start()
    vscatter.opposite()
    tell(5).wait_recv()
    gather_gains(3, gsum.at[2], 5)
    tell(6).start()
    tell(7).start()
    vscatter.late()
    tell(6).wait_recv()
    tell(8).start()
    for q, item in enumerate(sums):
        item.end()
        rows = slice(size * q, size * q + size)
        _, input_part = norm_back(tok[rows, :].astype(F32), gain1, item.total())
        for i in range(4):
            cols = slice(256 * i, 256 * i + 256)
            mid_grad = accum[3, 128 * i + size * q : 128 * i + size * q + size, :]
            tokens_grad[rows, cols] = (mid_grad + input_part[:, cols]).astype(BF16)
    tell(7).wait_recv()
    tell(8).wait_recv()
    gather_gains(4, gsum.at[3], 6, 7, 8)
    place = blk.plane(0, 0)
    offset = blk.c * 64 + head.h * 8
    lane = block * 8 + head.h

    def turned(first, shift):
        return pltpu.roll(gsum[4, :, pl.ds(pl.multiple_of(first, 128), 128)], lax.rem(128 - shift, 128), 1)

    first_out[...] = turned(place * 128, offset)[:, 0:8]
    second_out[...] = turned(1024 + place * 128, offset)[:, 0:8]
    qn_out[...] = turned(2048, lane)[:, 0:1]
    kn_out[...] = turned(2176, lane)[:, 0:1]
    vscatter.end()
    vsum = vscatter.total()
    query_out[...] = vsum[:, 0:256]
    key_out[...] = vsum[:, 256:384]
    value_out[...] = vsum[:, 384:512]
    output_out[...] = vsum[:, 512:768]
    for k in range(9):
        tell(k).wait_send()


def hand_over_kernel(*refs):
    count = len(refs) // 2
    for i in range(count):
        refs[count + i][...] = refs[i][...]


def sems(*counts):
    return [pltpu.SemaphoreType.DMA((c,)) for c in counts]


def per_device(
    tokens, doc_starts, first_gain, query_weight, key_matrix, value_matrix, querynorm, keynorm,
    output_weight, second_gain, gate_weight, up_weight, down_weight, grad_out,
):
    freqs = np.tile(THETA ** (-np.arange(64, dtype=np.float64) / 64), 2).astype(np.float32)
    vm = pl.BlockSpec(memory_space=pltpu.VMEM)
    hbm = pl.BlockSpec(memory_space=pl.ANY)
    outs = [
        ((128, 1024), BF16), ((128, 1024), BF16), ((64, 256), F32), ((64, 128), F32), ((64, 128), F32),
        ((64, 256), F32), ((64, 384), F32), ((64, 384), F32), ((64, 384), F32),
        ((1, 8), F32), ((1, 8), F32), ((1, 1), F32), ((1, 1), F32), ((1024, 1024), BF16),
    ]
    scratch = [
        ((1024, 128), F32), ((1024, 128), F32),
        ((1024, 1920), BF16), ((1024, 1024), BF16), ((1024, 1024), BF16), ((1024, 1024), BF16), ((16384, 256), BF16),
        ((2, 1024, 128), BF16), ((1024, 128), BF16), ((1024, 256), F32), ((1024, 128), F32), ((4, 1024, 256), F32),
        ((1024, 256), BF16), ((512, 256), BF16), ((2, 1024, 256), BF16), ((2, 1024, 256), BF16), ((128, 1024), F32),
        ((8, 128, 1024), BF16), ((7, 128, 1024), BF16), ((8, 128, 1024), BF16), ((7, 128, 1024), BF16),
        ((1024, 1152), BF16), ((1024, 256), BF16), ((512, 256), BF16), ((2, 1024, 256), BF16),
        ((8, 2, 64, 1152), BF16), ((8, 64, 1152), BF16), ((7, 64, 1152), BF16),
        ((8, 2, 64, 768), BF16), ((8, 64, 768), BF16), ((7, 64, 768), BF16),
        ((2, 1024, 256), BF16), ((8, 1024, 256), BF16), ((7, 1024, 256), BF16), ((512, 256), BF16), ((512, 256), BF16),
        ((1, 2304), F32), ((9, 1, 2304), F32), ((5, 1, 2304), F32),
    ]
    counts = (11, 11, 8, 8, 11, 11, 8, 8, 4, 4, 8 * PARTS, 8 * PARTS, 11 * PARTS, 11 * PARTS, 11, 11)
    counts += (8, 8, 8, 8, 1, 1, 11, 11, 8, 8, 8, 8, 1, 1, 8, 8, 8, 8, 9, 9, 2)
    made = pl.pallas_call(
        layer_kernel,
        out_shape=[jax.ShapeDtypeStruct(s, d) for s, d in outs],
        in_specs=[pl.BlockSpec(memory_space=pltpu.SMEM)] + [vm] * 14,
        out_specs=[vm] * 13 + [hbm],
        scratch_shapes=[pltpu.VMEM(s, d) for s, d in scratch] + sems(*counts),
        compiler_params=pltpu.CompilerParams(vmem_limit_bytes=VMEM_LIMIT, collective_id=1, has_side_effects=True),
    )(
        doc_starts, tokens, grad_out, query_weight, key_matrix, value_matrix, output_weight.T, gate_weight, up_weight,
        down_weight.T, first_gain.reshape(8, 128), second_gain.reshape(8, 128), querynorm[None, :], keynorm[None, :], freqs[None, :],
    )
    made = pl.pallas_call(
        hand_over_kernel,
        out_shape=[jax.ShapeDtypeStruct(s, d) for s, d in outs[:13]],
        in_specs=[vm] * 13,
        out_specs=[vm] * 13,
    )(*made[:13])
    layer_out, tokens_grad, query, key, value, output, gate, up, down, first, second, qn, kn = made
    return (
        layer_out, tokens_grad, first.reshape(8), query, key, value, qn.reshape(1), kn.reshape(1),
        output.T, second.reshape(8), gate, up, down.T,
    )


def solution(mesh):
    return jax.shard_map(
        per_device,
        mesh=mesh,
        in_specs=(
            P(("blk", "head"), None),
            P(),
            P(),
            P("blk", "head"),
            P("blk", "head"),
            P("blk", "head"),
            P(),
            P(),
            P("head", "blk"),
            P(),
            P("blk", "head"),
            P("blk", "head"),
            P("head", "blk"),
            P(("blk", "head"), None),
        ),
        out_specs=(
            P(("blk", "head"), None),
            P(("blk", "head"), None),
            P(("blk", "head")),
            P("blk", "head"),
            P("blk", "head"),
            P("blk", "head"),
            P(("blk", "head")),
            P(("blk", "head")),
            P("head", "blk"),
            P(("blk", "head")),
            P("blk", "head"),
            P("blk", "head"),
            P("head", "blk"),
        ),
        check_vma=False,
    )
```
